32 devices in a mesh: section: 2 (over y), dp: 16 (over z, x, core).
Axes of the slice: x: 2, y: 2, z: 4, core: 2. Of those that a mesh axis runs over, the one named last changes fastest.
Arguments:
- tokens: bfloat16 [2, 16, 2, 128, 768], P(None, 'dp'), may hold values from -6 to 6
- cotangent: bfloat16 [2, 16, 2, 128, 768], P(None, 'dp'), may hold values from -6 to 6
- boxes: int32 [2, 16, 2, 4], P(None, 'dp'), may hold values from 0 to 16, as said below
- timesteps: int32 [2, 16], P(None, 'dp'), may hold values from 0 to 999
- w_ada: float32 [2, 768, 4608], P('section', 'dp'), may hold values from -0.4375 to 0.4375
- w_qkv: float32 [2, 768, 2304], P('section', 'dp'), may hold values from -0.21875 to 0.21875
- w_proj: float32 [2, 768, 768], P('section', 'dp'), may hold values from -0.625 to 0.625
- w_up: float32 [2, 768, 3072], P('section', 'dp'), may hold values from -0.21875 to 0.21875
- w_down: float32 [2, 3072, 768], P('section', 'dp'), may hold values from -0.109375 to 0.109375
Outputs:
- acts: float32 [2, 2, 16, 2, 128, 768], P('section', None, 'dp')
- grad_in: float32 [2, 2, 16, 2, 128, 768], P('section', None, 'dp')
- grad_ada: float32 [2, 768, 4608], P('section', 'dp')
- grad_qkv: float32 [2, 768, 2304], P('section', 'dp')
- grad_proj: float32 [2, 768, 768], P('section', 'dp')
- grad_up: float32 [2, 768, 3072], P('section', 'dp')
- grad_down: float32 [2, 3072, 768], P('section', 'dp')
The draws below stay inside these ranges and needn't reach their ends.
Inputs may be any that keep to these rules, and one draw needn't show every extreme that they name: boxes hold (top, bottom, left, right) with top < bottom <= 8 and left < right <= 16, so every box holds one patch or more.
All inputs are finite; a program needn't handle non-finite values.
Results may differ from the reference program's by a relative error of at most 0.028.
The reference program's roundings to bfloat16 on the way count: a program that leaves them out, or rounds other values in their place, can miss the bound.
Values may be sent and summed in bfloat16 or wider, within the bound.
No kernel may reach another device: no remote copies, remote signals or barrier semaphores. Data moves between devices by JAX's collectives and lax.ppermute only.
A program may use at most 256 MiB of HBM per device.

```python
import math
import jax
import jax.numpy as jnp
from jax import lax

D = 768
HEADS = 12
HEAD_DIM = 64
FF = 3072
GH = 8
GW = 16
FRAMES = 2
MICRO = 2
PATCHES = 128
CLIPS = 16


def draw_boxes(key, part):
    key = jax.random.fold_in(key, 7)
    keys = jax.random.split(key, 4)
    shape = (MICRO, CLIPS, FRAMES)
    top_edge = jax.random.randint(keys[0], shape, 0, GH)
    bottom_edge = jax.random.randint(keys[1], shape, top_edge + 1, GH + 1)
    left_edge = jax.random.randint(keys[2], shape, 0, GW)
    right_edge = jax.random.randint(keys[3], shape, left_edge + 1, GW + 1)
    return jnp.stack([top_edge, bottom_edge, left_edge, right_edge], axis=-1).astype(jnp.int32)


def with_ends(entries, own_key, least, largest):
    extent = entries.shape
    place = [jax.random.randint(jax.random.fold_in(own_key, axis), (), 0, extent[axis]) for axis in range(len(extent))]
    entries = entries.at[tuple(place)].set(least)
    longest = extent.index(max(extent))
    place[longest] = (place[longest] + 1) % extent[longest]
    return entries.at[tuple(place)].set(largest)


def raised(drawn, own_key, source, target, blocks, factor):
    def block_of(position):
        return (jnp.arange(drawn.shape[position]) // (drawn.shape[position] // blocks)).reshape((-1,) + (1,) * (drawn.ndim - 1 - position))

    near = jax.random.permutation(own_key, blocks)[block_of(target)]
    other_side = (block_of(target) + blocks // 2) % blocks
    return jnp.where((block_of(source) == near) | (block_of(source) == other_side), factor * drawn, drawn)


def shard_levels(key, extent, cuts, low, top_value):
    gain = 1.0
    for dim, blocks in cuts:
        steps = jax.random.uniform(jax.random.fold_in(jax.random.fold_in(key, 6), dim), (blocks,), jnp.float32, low / len(cuts), top_value / len(cuts))
        gain = gain * jnp.repeat(jnp.exp(steps), extent[dim] // blocks).reshape((-1,) + (1,) * (len(extent) - 1 - dim))
    return gain


def bell_draw(rng, dims, width, bound, shards=(), kind=jnp.bfloat16):
    loudness = shard_levels(rng, dims, shards, -0.22, 0.18) if shards else 1.0
    result = jax.random.normal(rng, dims, jnp.float32) * width * loudness
    return jnp.minimum(jnp.maximum(result, -bound), bound).astype(kind)


def heavy_noise(own_key, shape, scale, most, cuts, heavy, kind=jnp.bfloat16):
    entries = scale * jax.random.normal(own_key, shape, jnp.float32)
    if cuts:
        entries = entries * shard_levels(own_key, shape, cuts, -0.22, 0.18)
    return jnp.clip(raised(entries, jax.random.fold_in(own_key, 3), *heavy), -most, most).astype(kind)


def setup_inputs(seed: int = 0) -> dict:
    splits = jax.random.split(jax.random.key(seed), 10)
    return {
        "tokens": heavy_noise(splits[0], (MICRO, CLIPS, FRAMES, PATCHES, D), 1.0, 6.0, ((1, 16),), (1, 4, 16, 2.0)),
        "cotangent": bell_draw(splits[1], (MICRO, CLIPS, FRAMES, PATCHES, D), 1.0, 6.0, ((1, 16),)),
        "boxes": draw_boxes(jax.random.fold_in(splits[9], 71), 0),
        "timesteps": with_ends(jax.random.randint(splits[3], (MICRO, CLIPS), 0, 1000), jax.random.fold_in(splits[3], 1), 0, 999).astype(jnp.int32),
        "w_ada": bell_draw(splits[4], (2, D, 6 * D), (D // 4) ** -0.5, 0.4375, ((0, 2), (1, 16)), jnp.float32),
        "w_qkv": bell_draw(splits[5], (2, D, 3 * D), D ** -0.5, 0.21875, ((0, 2), (1, 16)), jnp.float32),
        "w_proj": bell_draw(splits[6], (2, D, D), (D // 8) ** -0.5, 0.625, ((0, 2), (1, 16)), jnp.float32),
        "w_up": bell_draw(splits[7], (2, D, FF), D ** -0.5, 0.21875, ((0, 2), (1, 16)), jnp.float32),
        "w_down": bell_draw(splits[8], (2, FF, D), FF ** -0.5, 0.109375, ((0, 2), (1, 16)), jnp.float32),
    }


@jax.custom_vjp
def low(v):
    return lax.optimization_barrier(v.astype(jnp.bfloat16)).astype(jnp.float32)

@jax.custom_vjp
def low_back(v):
    return v

def low_keep(v):
    return (low(v), None)

def low_pass(kept, grad):
    return (grad,)

def back_keep(v):
    return (v, None)

def back_low(kept, grad):
    return (low(grad),)
low.defvjp(low_keep, low_pass)
low_back.defvjp(back_keep, back_low)
ln_eps = 1e-06
top_precision = lax.Precision.HIGHEST

def sinusoid(step_value):
    half_width = D // 2
    frequency = jnp.exp(-math.log(10000.0) * jnp.arange(half_width, dtype=jnp.float32) / half_width)
    angles = step_value.astype(jnp.float32) * frequency
    return jnp.concatenate([jnp.cos(angles), jnp.sin(angles)])

def condition(step_value, box_rows):
    embed_pair = jnp.stack([sinusoid(jnp.zeros((), jnp.int32)), sinusoid(step_value)])
    low_embed = low(jax.nn.silu(embed_pair))
    cell_ids = jnp.arange(PATCHES, dtype=jnp.int32)
    row_ids = (cell_ids // GW)[None, :]
    col_ids = (cell_ids % GW)[None, :]
    inside = (row_ids >= box_rows[:, 0:1]) & (row_ids < box_rows[:, 1:2]) & (col_ids >= box_rows[:, 2:3]) & (col_ids < box_rows[:, 3:4])
    return (low_embed, inside.astype(jnp.float32).reshape(-1))

def layer_norm(values):
    centred = values - lax.optimization_barrier(jnp.mean(values, axis=-1, keepdims=True))
    return centred * lax.rsqrt(lax.optimization_barrier(jnp.mean(centred * centred, axis=-1, keepdims=True)) + ln_eps)

def layer(inputs, weights, low_embed, given_mask, temporal):
    w_ada, w_qkv, w_proj, w_up, w_down = [low(matrix) for matrix in weights]
    flat = inputs.reshape(-1, D)
    modulation = jnp.dot(low_embed, w_ada, precision=top_precision)
    per_token = jnp.where(given_mask[:, None] > 0.5, modulation[0], modulation[1])
    shift_a, scale_a, gate_a, shift_b, scale_b, gate_b = jnp.split(per_token, 6, axis=1)
    mixed_a = low(layer_norm(flat) * (1.0 + scale_a) + shift_a)
    packed = low_back(low(jnp.dot(mixed_a, w_qkv, precision=top_precision)))
    heads = packed.reshape(FRAMES, PATCHES, 3, HEADS, HEAD_DIM)
    queries, key_part, values = (heads[:, :, 0], heads[:, :, 1], heads[:, :, 2])
    scaling = HEAD_DIM ** (-0.5)
    if temporal:
        scores = low_back(jnp.einsum('fphe,gphe->hfgp', queries, key_part, precision=top_precision) * scaling)
        shares = low(jax.nn.softmax(scores, axis=2))
        attended = jnp.einsum('hfgp,gphe->fphe', shares, values, precision=top_precision)
    else:
        scores = low_back(jnp.einsum('fphe,fqhe->fhpq', queries, key_part, precision=top_precision) * scaling)
        shares = low(jax.nn.softmax(scores, axis=-1))
        attended = jnp.einsum('fhpq,fqhe->fphe', shares, values, precision=top_precision)
    merged = low_back(low(attended.reshape(-1, D)))
    branch = low_back(jnp.dot(merged, w_proj, precision=top_precision))
    middle = flat + gate_a * branch
    mixed_b = low(layer_norm(middle) * (1.0 + scale_b) + shift_b)
    hidden = low_back(jnp.dot(mixed_b, w_up, precision=top_precision))
    active = low(jax.nn.gelu(hidden, approximate=True))
    out_branch = low_back(jnp.dot(active, w_down, precision=top_precision))
    return (middle + gate_b * out_branch).reshape(FRAMES, PATCHES, D)

def reference(tokens, cotangent, boxes, timesteps, w_ada, w_qkv, w_proj, w_up, w_down):
    section_one = (w_ada[0], w_qkv[0], w_proj[0], w_up[0], w_down[0])
    section_two = (w_ada[1], w_qkv[1], w_proj[1], w_up[1], w_down[1])
    clip_count = MICRO * CLIPS
    token_all = tokens.astype(jnp.float32).reshape(clip_count, FRAMES, PATCHES, D)
    cot_all = cotangent.astype(jnp.float32).reshape(clip_count, FRAMES, PATCHES, D)
    box_all = boxes.reshape(clip_count, FRAMES, 4)
    step_all = timesteps.reshape(clip_count)

    def one_clip(totals, clip_item):
        token_clip, cotangent_clip, box_rows, step_value = clip_item
        low_embed, given_mask = condition(step_value, box_rows)

        def clip_pass(first_weights, second_weights, layer_in, extra_term):
            first_out = layer(layer_in, first_weights, low_embed, given_mask, False)
            second_in = low_back(low(first_out)) + extra_term
            second_out = layer(second_in, second_weights, low_embed, given_mask, True)
            return (first_out, second_out)
        outputs, pullback = jax.vjp(clip_pass, section_one, section_two, token_clip, jnp.zeros_like(token_clip))
        first_grads, second_grads, grad_token, grad_extra = pullback((jnp.zeros_like(outputs[0]), cotangent_clip))
        totals = jax.tree.map(jnp.add, totals, (first_grads, second_grads))
        return (totals, (outputs[0], outputs[1], grad_token, grad_extra))
    start = jax.tree.map(jnp.zeros_like, (section_one, section_two))
    totals, stacked = lax.scan(one_clip, start, (token_all, cot_all, box_all, step_all))
    out_shape = (2, MICRO, CLIPS, FRAMES, PATCHES, D)
    acts = jnp.stack([stacked[0], stacked[1]]).reshape(out_shape)
    grad_in = jnp.stack([stacked[2], stacked[3]]).reshape(out_shape)
    first_grads, second_grads = totals
    return (acts, grad_in, jnp.stack([first_grads[0], second_grads[0]]), jnp.stack([first_grads[1], second_grads[1]]), jnp.stack([first_grads[2], second_grads[2]]), jnp.stack([first_grads[3], second_grads[3]]), jnp.stack([first_grads[4], second_grads[4]]))
```

```python
from functools import partial
import math

import jax
import jax.numpy as jnp
from jax import lax
from jax.experimental import pallas as pl
from jax.experimental.pallas import tpu as pltpu
from jax.sharding import PartitionSpec as P

HEAD_DIM = 64
GW = 16
LANES = 128
CHUNK = 32
EPS = 1e-06
VMEM_BYTES = 56 * 1024 * 1024
f32 = jnp.float32
bf16 = jnp.bfloat16
NN = (((1,), (0,)), ((), ()))
NT = (((1,), (1,)), ((), ()))
TN = (((0,), (0,)), ((), ()))


def mm(a, b, dims=NN):
    return lax.dot_general(a, b, dims, preferred_element_type=f32)


def ln(v):
    centred = v - jnp.mean(v, axis=-1, keepdims=True)
    inv = lax.rsqrt(jnp.mean(centred * centred, axis=-1, keepdims=True) + EPS)
    return centred * inv, inv


def ln_back(normed, inv, grad):
    return inv * (
        grad
        - jnp.mean(grad, axis=-1, keepdims=True)
        - normed * jnp.mean(grad * normed, axis=-1, keepdims=True)
    )


def chunks(count, body):
    @pl.loop(0, count // CHUNK)
    def _(i):
        body(pl.ds(pl.multiple_of(i * CHUNK, CHUNK), CHUNK))


class Refs(dict):
    __getattr__ = dict.__getitem__


class Cfg:
    def __init__(self, frames, patches, width, hidden, blocks):
        self.frames, self.patches, self.width, self.hidden = frames, patches, width, hidden
        self.rows = frames * patches
        self.ratio = hidden // width
        self.blocks = blocks
        self.own = width // blocks
        self.scaling = HEAD_DIM ** (-0.5)


def weight_copies(c, w, r):
    own = c.own
    out = {}
    for j in range(3):
        out["q%d" % j] = pltpu.make_async_copy(
            w.at[:, pl.ds(j * own, own), :], r.wq.at[j], r.wsem.at[j]
        )
    out["p"] = pltpu.make_async_copy(w.at[:, pl.ds(3 * own, own), :], r.wp, r.wsem.at[3])
    for j in range(c.ratio):
        out["u%d" % j] = pltpu.make_async_copy(
            w.at[:, pl.ds((4 + j) * own, own), :], r.wu.at[j], r.wsem.at[4 + j]
        )
    step = c.blocks // c.ratio
    for j in range(c.ratio):
        out["d%d" % j] = pltpu.make_async_copy(
            w.at[pl.ds(j * step, step), pl.ds((4 + c.ratio) * own, c.ratio * own), :],
            r.wd.at[pl.ds(j * step, step)],
            r.wsem.at[4 + c.ratio + j],
        )
    return out


def weight_scratch(c):
    return dict(
        wq=pltpu.VMEM((3, c.blocks, c.own, c.width), bf16),
        wp=pltpu.VMEM((c.blocks, c.own, c.width), bf16),
        wu=pltpu.VMEM((c.ratio, c.blocks, c.own, c.width), bf16),
        wd=pltpu.VMEM((c.blocks, c.ratio * c.own, c.width), bf16),
        wsem=pltpu.SemaphoreType.DMA((4 + 2 * c.ratio,)),
    )


def square(c, ref, *index):
    return ref[index].reshape(c.width, c.width)


def down_block(c, r, j):
    step = c.blocks // c.ratio
    return r.wd[j * step : (j + 1) * step].reshape(c.width, c.width)


def fill_given(c, ctl, r):
    patch = lax.broadcasted_iota(jnp.int32, (c.patches, LANES), 0)
    row, col = patch // GW, patch % GW
    for f in range(c.frames):
        top, bottom, left, right = (ctl[1 + 4 * f + i] for i in range(4))
        inside = (row >= top) & (row < bottom) & (col >= left) & (col < right)
        r.given[f * c.patches : (f + 1) * c.patches, :] = jnp.where(inside, 1.0, 0.0)


def pick(c, r, index, given):
    where = slice(index * c.width, (index + 1) * c.width)
    return jnp.where(given, r.mod[0:1, where], r.mod[1:2, where])


def is_given(r, rows):
    return r.given[rows, 0:1] > 0.5


def forward_a(c, r):
    def body(rows):
        given = is_given(r, rows)
        normed, _ = ln(r.x[rows, :].astype(f32))
        r.mixed_a[rows, :] = (normed * (1.0 + pick(c, r, 1, given)) + pick(c, r, 0, given)).astype(
            bf16
        )

    chunks(c.rows, body)


def forward_qkv(c, r, wait):
    for j in range(3):
        wait("q%d" % j)
        r.packed[:, j * c.width : (j + 1) * c.width] = mm(
            r.mixed_a[...], square(c, r.wq, j)
        ).astype(bf16)


def halves(pair):
    first = lax.broadcasted_iota(jnp.int32, pair.shape, 1) < HEAD_DIM
    zero = jnp.zeros_like(pair)
    return jnp.concatenate([jnp.where(first, pair, zero), jnp.where(first, zero, pair)], axis=0)


def softmax_rows(scores):
    top = jnp.max(scores, axis=-1, keepdims=True)
    exponent = jnp.exp(scores - top)
    return exponent * (1.0 / jnp.sum(exponent, axis=-1, keepdims=True))


def spatial_tiles(c):
    for f in range(c.frames):
        for pair in range(c.width // LANES):
            yield slice(f * c.patches, (f + 1) * c.patches), pair


def spatial_merge(c, r):
    for rows, pair in spatial_tiles(c):
        q, k, v = (
            r.packed[rows, i * c.width + pair * LANES : i * c.width + (pair + 1) * LANES]
            for i in range(3)
        )
        shares = softmax_rows(mm(halves(q), k, NT) * c.scaling).astype(bf16)
        side = jnp.concatenate([shares[: c.patches], shares[c.patches :]], axis=1)
        r.merged[rows, pair * LANES : (pair + 1) * LANES] = mm(side, halves(v)).astype(bf16)


def spatial_back(c, r):
    for rows, pair in spatial_tiles(c):
        cols = [
            slice(i * c.width + pair * LANES, i * c.width + (pair + 1) * LANES) for i in range(3)
        ]
        q, k, v = (r.packed[rows, cols[i]] for i in range(3))
        q2, k2 = halves(q), halves(k)
        d2 = halves(r.grad_merged[rows, cols[0]])
        soft = softmax_rows(mm(q2, k, NT) * c.scaling)
        grad_shares = mm(d2, v, NT)
        inner = jnp.sum(soft * grad_shares, axis=-1, keepdims=True)
        grad_scores = (soft * (grad_shares - inner)).astype(bf16)
        side = jnp.concatenate([grad_scores[: c.patches], grad_scores[c.patches :]], axis=1)
        r.grad_packed[rows, cols[0]] = (mm(side, k2) * c.scaling).astype(bf16)
        r.grad_packed[rows, cols[1]] = (mm(grad_scores, q2, TN) * c.scaling).astype(bf16)
        r.grad_packed[rows, cols[2]] = mm(soft.astype(bf16), d2, TN).astype(bf16)


def fill_heads(c, r):
    lane = lax.broadcasted_iota(jnp.int32, (c.width, LANES), 0) // HEAD_DIM
    col = lax.broadcasted_iota(jnp.int32, (c.width, LANES), 1)
    r.heads_in[...] = jnp.where(lane == col, 1.0, 0.0).astype(bf16)
    col = lax.broadcasted_iota(jnp.int32, (LANES, c.width), 0)
    lane = lax.broadcasted_iota(jnp.int32, (LANES, c.width), 1) // HEAD_DIM
    r.heads_out[...] = jnp.where(lane == col, 1.0, 0.0).astype(bf16)


def head_sums(r, product):
    high = product.astype(bf16)
    low = (product - high.astype(f32)).astype(bf16)
    return mm(high, r.heads_in[...]) + mm(low, r.heads_in[...])


def frame_pairs(c):
    return [(f, g) for f in range(c.frames) for g in range(c.frames)]


def temporal_parts(c, r, ref, rows, part):
    return [
        ref[
            pl.ds(pl.multiple_of(f * c.patches + rows.start, CHUNK), CHUNK),
            part * c.width : (part + 1) * c.width,
        ].astype(f32)
        for f in range(c.frames)
    ]


def temporal_soft(c, r, queries, keys):
    product = jnp.concatenate([queries[f] * keys[g] for f, g in frame_pairs(c)], axis=0)
    scores = head_sums(r, product) * c.scaling
    soft = []
    for f in range(c.frames):
        row = [scores[(f * c.frames + g) * CHUNK : (f * c.frames + g + 1) * CHUNK] for g in range(c.frames)]
        top = row[0]
        for entry in row[1:]:
            top = jnp.maximum(top, entry)
        exponent = [jnp.exp(entry - top) for entry in row]
        total = exponent[0]
        for entry in exponent[1:]:
            total = total + entry
        soft += [entry * (1.0 / total) for entry in exponent]
    return soft


def spread(r, columns):
    wide = mm(jnp.concatenate([v.astype(bf16) for v in columns], axis=0), r.heads_out[...])
    return [wide[i * CHUNK : (i + 1) * CHUNK] for i in range(len(columns))]


def temporal_merge(c, r):
    def body(rows):
        queries, keys, values = (temporal_parts(c, r, r.packed, rows, i) for i in range(3))
        shares = spread(r, temporal_soft(c, r, queries, keys))
        for f in range(c.frames):
            total = shares[f * c.frames] * values[0]
            for g in range(1, c.frames):
                total = total + shares[f * c.frames + g] * values[g]
            at = pl.ds(pl.multiple_of(f * c.patches + rows.start, CHUNK), CHUNK)
            r.merged[at, :] = total.astype(bf16)

    chunks(c.patches, body)


def temporal_back(c, r):
    n = c.frames

    def body(rows):
        queries, keys, values = (temporal_parts(c, r, r.packed, rows, i) for i in range(3))
        grads = temporal_parts(c, r, r.grad_merged, rows, 0)
        soft = temporal_soft(c, r, queries, keys)
        product = jnp.concatenate([grads[f] * values[g] for f, g in frame_pairs(c)], axis=0)
        wide = head_sums(r, product)
        grad_shares = [wide[i * CHUNK : (i + 1) * CHUNK] for i in range(n * n)]
        grad_scores = []
        for f in range(n):
            inner = soft[f * n] * grad_shares[f * n]
            for g in range(1, n):
                inner = inner + soft[f * n + g] * grad_shares[f * n + g]
            grad_scores += [
                soft[f * n + g] * (grad_shares[f * n + g] - inner) for g in range(n)
            ]
        shares = spread(r, soft)
        scores = spread(r, grad_scores)

        def put(frame, part, value):
            at = pl.ds(pl.multiple_of(frame * c.patches + rows.start, CHUNK), CHUNK)
            r.grad_packed[at, part * c.width : (part + 1) * c.width] = value.astype(bf16)

        for f in range(n):
            put(f, 0, sum(scores[f * n + g] * keys[g] for g in range(n)) * c.scaling)
            put(f, 1, sum(scores[g * n + f] * queries[g] for g in range(n)) * c.scaling)
            put(f, 2, sum(shares[g * n + f] * grads[g] for g in range(n)))

    chunks(c.patches, body)


def forward_b(c, r, wait):
    wait("p")
    r.branch[...] = mm(r.merged[...], r.wp[...].reshape(c.width, c.width))

    def body(rows):
        given = is_given(r, rows)
        middle = r.x[rows, :].astype(f32) + pick(c, r, 2, given) * r.branch[rows, :]
        r.middle[rows, :] = middle
        normed, _ = ln(middle)
        r.mixed_b[rows, :] = (normed * (1.0 + pick(c, r, 4, given)) + pick(c, r, 3, given)).astype(
            bf16
        )

    chunks(c.rows, body)


GELU_A = math.sqrt(2.0 / math.pi)
GELU_B = 0.044715


def forward_mlp(c, r, wait):
    for j in range(c.ratio):
        wait("u%d" % j)
        cols = slice(j * c.width, (j + 1) * c.width)
        r.hidden[:, cols] = mm(r.mixed_b[...], square(c, r.wu, j))

        def body(rows):
            h = r.hidden[rows, cols]
            bent = jnp.tanh(GELU_A * (h + GELU_B * (h * h * h)))
            r.active[rows, cols] = (0.5 * h * (1.0 + bent)).astype(bf16)

        chunks(c.rows, body)
    for j in range(c.ratio):
        wait("d%d" % j)
    r.out_branch[...] = mm(r.active[...], r.wd[...].reshape(c.hidden, c.width))


def forward_end(c, r):
    def body(rows):
        given = is_given(r, rows)
        result = r.middle[rows, :] + pick(c, r, 5, given) * r.out_branch[rows, :]
        r.acts[rows, :] = result
        if "send" in r:
            r.send[rows, :] = result.astype(bf16)

    chunks(c.rows, body)


def add_sums(c, r, index, given, value):
    cols = slice(index * c.width, (index + 1) * c.width)
    mine = jnp.where(given, value, 0.0)
    rest = jnp.where(given, 0.0, value)
    shape = (CHUNK // 8, 8, c.width)
    r.sums[0, :, cols] += jnp.sum(mine.reshape(shape), axis=0)
    r.sums[1, :, cols] += jnp.sum(rest.reshape(shape), axis=0)


def backward_mlp(c, r, wait, gelu_again):
    def start(rows):
        given = is_given(r, rows)
        grad = r.grad[rows, :].astype(f32)
        r.grad_out_b[rows, :] = (pick(c, r, 5, given) * grad).astype(bf16)
        add_sums(c, r, 5, given, grad * r.out_branch[rows, :])

    chunks(c.rows, start)
    for j in range(c.ratio):
        wait("d%d" % j)
        cols = slice(j * c.width, (j + 1) * c.width)
        r.temp[...] = mm(r.grad_out_b[...], down_block(c, r, j), NT)

        def body(rows):
            h = r.hidden[rows, cols]
            square_h = h * h
            bent = jnp.tanh(GELU_A * (h + GELU_B * (square_h * h)))
            slope = 0.5 * (1.0 + bent) + 0.5 * h * (1.0 - bent * bent) * (
                GELU_A * (1.0 + 3.0 * GELU_B * square_h)
            )
            r.grad_hidden[rows, cols] = (r.temp[rows, :] * slope).astype(bf16)
            if gelu_again:
                r.active[rows, cols] = (0.5 * h * (1.0 + bent)).astype(bf16)

        chunks(c.rows, body)
    for j in range(c.ratio):
        wait("u%d" % j)
        part = mm(r.grad_hidden[:, j * c.width : (j + 1) * c.width], square(c, r.wu, j), NT)
        if j == 0:
            r.temp[...] = part
        else:
            r.temp[...] += part


def backward_mid(c, r, wait):
    def body(rows):
        given = is_given(r, rows)
        normed, inv = ln(r.middle[rows, :])
        scale = 1.0 + pick(c, r, 4, given)
        r.mixed_b[rows, :] = (normed * scale + pick(c, r, 3, given)).astype(bf16)
        grad_mixed = r.temp[rows, :]
        middle = r.grad[rows, :].astype(f32) + ln_back(normed, inv, grad_mixed * scale)
        r.grad_middle[rows, :] = middle
        r.grad_branch[rows, :] = (pick(c, r, 2, given) * middle).astype(bf16)
        add_sums(c, r, 3, given, grad_mixed)
        add_sums(c, r, 4, given, grad_mixed * normed)
        add_sums(c, r, 2, given, middle * r.branch[rows, :])

    chunks(c.rows, body)
    wait("p")
    r.grad_merged[...] = mm(
        r.grad_branch[...], r.wp[...].reshape(c.width, c.width), NT
    ).astype(bf16)


def backward_end(c, r, wait):
    for j in range(3):
        wait("q%d" % j)
        part = mm(r.grad_packed[:, j * c.width : (j + 1) * c.width], square(c, r.wq, j), NT)
        if j == 0:
            r.temp[...] = part
        else:
            r.temp[...] += part

    def body(rows):
        given = is_given(r, rows)
        normed, inv = ln(r.x[rows, :].astype(f32))
        scale = 1.0 + pick(c, r, 1, given)
        r.mixed_a[rows, :] = (normed * scale + pick(c, r, 0, given)).astype(bf16)
        grad_mixed = r.temp[rows, :]
        result = r.grad_middle[rows, :] + ln_back(normed, inv, grad_mixed * scale)
        r.grad_in[rows, :] = result
        if "send" in r:
            r.send[rows, :] = result.astype(bf16)
        add_sums(c, r, 0, given, grad_mixed)
        add_sums(c, r, 1, given, grad_mixed * normed)

    chunks(c.rows, body)
    r.grad_mod[...] = jnp.sum(r.sums[...], axis=1)


def sizes(c):
    wide, rows = c.width, c.rows
    return dict(
        x=((rows, wide), bf16),
        mod=((2, 6 * wide), f32),
        given=((rows, LANES), f32),
        mixed_a=((rows, wide), bf16),
        packed=((rows, 3 * wide), bf16),
        merged=((rows, wide), bf16),
        branch=((rows, wide), f32),
        middle=((rows, wide), f32),
        mixed_b=((rows, wide), bf16),
        hidden=((rows, c.hidden), f32),
        active=((rows, c.hidden), bf16),
        out_branch=((rows, wide), f32),
        acts=((rows, wide), f32),
        send=((rows, wide), bf16),
        grad=((rows, wide), bf16),
        grad_out_b=((rows, wide), bf16),
        grad_hidden=((rows, c.hidden), bf16),
        temp=((rows, wide), f32),
        grad_middle=((rows, wide), f32),
        grad_branch=((rows, wide), bf16),
        grad_merged=((rows, wide), bf16),
        grad_packed=((rows, 3 * wide), bf16),
        grad_in=((rows, wide), f32),
        sums=((2, 8, 6 * wide), f32),
        grad_mod=((2, 6 * wide), f32),
        heads_in=((wide, LANES), bf16),
        heads_out=((LANES, wide), bf16),
    )


KEPT = ("packed", "merged", "branch", "middle", "hidden", "out_branch")
TERMS = (
    "mixed_a",
    "grad_packed",
    "merged",
    "grad_branch",
    "mixed_b",
    "grad_hidden",
    "active",
    "grad_out_b",
)


class Traffic:
    def __init__(self, sems):
        self.sems, self.used, self.pending = sems, 0, {}

    def start(self, name, src, dst):
        copy = pltpu.make_async_copy(src, dst, self.sems.at[self.used])
        self.used += 1
        copy.start()
        self.pending[name] = copy

    def wait(self, name):
        if name in self.pending:
            self.pending.pop(name).wait()

    def drain(self):
        for name in list(self.pending):
            self.wait(name)


def start_weights(copies, order, traffic):
    for name in order:
        copies[name].start()
        traffic.pending[name] = copies[name]


def order_forward(c):
    return (
        ["q0", "q1", "q2", "p"]
        + ["u%d" % j for j in range(c.ratio)]
        + ["d%d" % j for j in range(c.ratio)]
    )


def order_backward(c):
    return (
        ["d%d" % j for j in range(c.ratio)]
        + ["u%d" % j for j in range(c.ratio)]
        + ["p", "q0", "q1", "q2"]
    )


def run_forward(c, r, t, temporal):
    t.wait("mod")
    t.wait("x")
    forward_a(c, r)
    forward_qkv(c, r, t.wait)
    if temporal:
        fill_heads(c, r)
        temporal_merge(c, r)
    else:
        spatial_merge(c, r)
    forward_b(c, r, t.wait)
    forward_mlp(c, r, t.wait)
    forward_end(c, r)


def spatial_forward_kernel(c, micro, names, refs):
    h = Refs(names_hbm(names, refs))
    r = h.vmem

    @pl.when(h.ctl[0] == 0)
    def _():
        t = Traffic(r.sems)
        t.start("x", h.x.at[micro], r.x)
        t.start("mod", h.mod.at[micro], r.mod)
        start_weights(weight_copies(c, h.w, r), order_forward(c), t)
        fill_given(c, h.ctl, r)
        run_forward(c, r, t, False)
        t.start("acts", r.acts, h.acts.at[micro])
        t.start("send", r.send, h.send)
        for name in KEPT:
            t.start(name, r[name], h[name])
        t.drain()


def temporal_kernel(c, micro, names, refs):
    h = Refs(names_hbm(names, refs))
    r = h.vmem

    @pl.when(h.ctl[0] == 1)
    def _():
        t = Traffic(r.sems)
        t.start("x", h.x, r.x)
        t.start("mod", h.mod.at[micro], r.mod)
        start_weights(weight_copies(c, h.w, r), order_forward(c), t)
        t.start("grad", h.cot.at[micro], r.grad)
        fill_given(c, h.ctl, r)
        forward = Refs({k: v for k, v in r.items() if k != "send"})
        run_forward(c, forward, t, True)
        t.start("acts", r.acts, h.acts.at[micro])
        r.sums[...] = jnp.zeros_like(r.sums)
        t.wait("grad")
        backward_mlp(c, r, t.wait, False)
        backward_mid(c, r, t.wait)
        temporal_back(c, r)
        backward_end(c, r, t.wait)
        put_backward(c, micro, h, r, t)
        t.drain()


def put_backward(c, micro, h, r, t):
    if "send" in h:
        t.start("send", r.send, h.send)
    t.start("grad_in", r.grad_in, h.grad_in.at[micro])
    t.start("grad_mod", r.grad_mod, h.grad_mod.at[micro])
    for name in TERMS:
        t.start(name, r[name], h[name].at[pl.ds(micro * c.rows, c.rows), :])


def spatial_backward_kernel(c, micro, names, refs):
    h = Refs(names_hbm(names, refs))
    r = h.vmem

    @pl.when(h.ctl[0] == 0)
    def _():
        t = Traffic(r.sems)
        t.start("grad", h.grad, r.grad)
        t.start("mod", h.mod.at[micro], r.mod)
        t.start("out_branch", h.out_branch, r.out_branch)
        t.start("hidden", h.hidden, r.hidden)
        copies = weight_copies(c, h.w, r)
        order = order_backward(c)
        start_weights(copies, order[: 2 * c.ratio], t)
        for name in ("middle", "branch", "packed", "merged"):
            t.start(name, h[name + "_kept"] if name in TERMS else h[name], r[name])
        t.start("x", h.x.at[micro], r.x)
        start_weights(copies, order[2 * c.ratio :], t)
        fill_given(c, h.ctl, r)
        r.sums[...] = jnp.zeros_like(r.sums)
        for name in ("grad", "mod", "out_branch", "hidden"):
            t.wait(name)
        backward_mlp(c, r, t.wait, True)
        t.wait("middle")
        t.wait("branch")
        backward_mid(c, r, t.wait)
        t.wait("packed")
        t.wait("merged")
        spatial_back(c, r)
        t.wait("x")
        backward_end(c, r, t.wait)
        put_backward(c, micro, h, r, t)
        t.drain()


def names_hbm(names, refs):
    outer, inner = names
    found = dict(zip(outer, refs[: len(outer)], strict=True))
    found["vmem"] = Refs(zip(inner, refs[len(outer) :], strict=True))
    return found


def call(c, kernel, micro, operands, news, alias, scratch, flops):
    ins = list(operands)
    outs = list(alias) + list(news)
    shapes = [jax.ShapeDtypeStruct(operands[n].shape, operands[n].dtype) for n in alias]
    shapes += [jax.ShapeDtypeStruct(*news[n]) for n in news]
    table = sizes(c)
    inner = {n: pltpu.VMEM(*table[n]) for n in scratch}
    inner.update(weight_scratch(c))
    inner["sems"] = pltpu.SemaphoreType.DMA((32,))
    in_names = [n if n not in alias else "_" + n for n in ins]
    names = (in_names + outs, list(inner))
    got = pl.pallas_call(
        lambda *refs: kernel(c, micro, names, refs),
        out_shape=shapes,
        in_specs=[
            pl.BlockSpec(memory_space=pltpu.SMEM if n == "ctl" else pl.ANY) for n in ins
        ],
        out_specs=[pl.BlockSpec(memory_space=pl.ANY)] * len(outs),
        scratch_shapes=list(inner.values()),
        input_output_aliases={ins.index(n): i for i, n in enumerate(alias)},
        compiler_params=pltpu.CompilerParams(vmem_limit_bytes=VMEM_BYTES),
        cost_estimate=pl.CostEstimate(flops=flops, bytes_accessed=20_000_000, transcendentals=0),
    )(*operands.values())
    return dict(zip(outs, got, strict=True))


def gradients_kernel(c, count, *refs):
    terms = Refs(zip(TERMS, refs[: len(TERMS)], strict=True))
    out = refs[len(TERMS)]
    held = Refs(zip(TERMS, refs[len(TERMS) + 1 : 2 * len(TERMS) + 1], strict=True))
    slots, in_sems, out_sems = refs[2 * len(TERMS) + 1 :]
    order = ("active", "grad_out_b", "mixed_b", "grad_hidden", "merged", "grad_branch", "mixed_a", "grad_packed")
    copies = {
        n: pltpu.make_async_copy(terms[n], held[n], in_sems.at[i]) for i, n in enumerate(order)
    }
    for n in order:
        copies[n].start()
    wide, own, step = c.width, c.own, c.blocks // c.ratio
    waited = set()
    flying = {}

    def need(name):
        if name not in waited:
            copies[name].wait()
            waited.add(name)

    jobs = [("active", j, "grad_out_b", 0, 4 + c.ratio + j) for j in range(c.ratio)]
    jobs += [("mixed_b", 0, "grad_hidden", j, 4 + j) for j in range(c.ratio)]
    jobs += [("merged", 0, "grad_branch", 0, 3)]
    jobs += [("mixed_a", 0, "grad_packed", j, j) for j in range(3)]
    for number, (left, lj, right, rj, block) in enumerate(jobs):
        need(left)
        need(right)
        slot = number % 2
        if slot in flying:
            flying.pop(slot).wait()
        value = mm(
            held[left][:, lj * wide : (lj + 1) * wide],
            held[right][:, rj * wide : (rj + 1) * wide],
            TN,
        ).astype(bf16)
        if block >= 4 + c.ratio:
            slots[slot] = value.reshape(slots.shape[1:])
            j = block - 4 - c.ratio
            src = slots.at[slot].reshape(step, c.ratio * own, wide)
            dst = out.at[pl.ds(j * step, step), pl.ds((4 + c.ratio) * own, c.ratio * own), :]
        else:
            slots[slot] = value.reshape(slots.shape[1:])
            src = slots.at[slot]
            dst = out.at[:, pl.ds(block * own, own), :]
        flying[slot] = pltpu.make_async_copy(src, dst, out_sems.at[slot])
        flying[slot].start()
    for copy in flying.values():
        copy.wait()


def weight_gradients(c, terms):
    per_block = (4 + 2 * c.ratio) * c.own
    shapes = [terms[n].shape for n in TERMS]
    count = shapes[0][0]
    return pl.pallas_call(
        partial(gradients_kernel, c, count),
        out_shape=jax.ShapeDtypeStruct((c.blocks, per_block, c.width), bf16),
        in_specs=[pl.BlockSpec(memory_space=pl.ANY)] * len(TERMS),
        out_specs=pl.BlockSpec(memory_space=pl.ANY),
        scratch_shapes=[pltpu.VMEM(s, bf16) for s in shapes]
        + [
            pltpu.VMEM((2, c.blocks, c.own, c.width), bf16),
            pltpu.SemaphoreType.DMA((len(TERMS),)),
            pltpu.SemaphoreType.DMA((2,)),
        ],
        compiler_params=pltpu.CompilerParams(vmem_limit_bytes=VMEM_BYTES),
        cost_estimate=pl.CostEstimate(
            flops=2 * count * c.width * c.width * (4 + 2 * c.ratio),
            bytes_accessed=24_000_000,
            transcendentals=0,
        ),
    )(*[terms[n] for n in TERMS])


def swap(block, distance):
    count = lax.axis_size("dp")
    return lax.ppermute(block, "dp", [(i, i ^ distance) for i in range(count)])


def gather_small(block):
    count = lax.axis_size("dp")
    if count & (count - 1):
        return lax.all_gather(block, "dp", axis=0, tiled=False)
    mine = lax.axis_index("dp")
    held, distance = block[None], 1
    while distance < count:
        other = swap(held, distance)
        lower = (mine & distance) == 0
        held = jnp.where(
            lower, jnp.concatenate([held, other]), jnp.concatenate([other, held])
        )
        distance *= 2
    return held


def scatter_small(blocks):
    count = lax.axis_size("dp")
    if count & (count - 1):
        return lax.psum_scatter(blocks, "dp", scatter_dimension=0, tiled=False)
    mine = lax.axis_index("dp")
    distance = count // 2
    while distance:
        low, high = blocks[:distance], blocks[distance:]
        upper = (mine & distance) != 0
        other = swap(jnp.where(upper, low, high), distance)
        blocks = jnp.where(upper, high, low) + other
        distance //= 2
    return blocks[0]


def embed_columns(steps, index, width):
    half = width // 2
    place = (index % half).astype(f32)
    frequency = jnp.exp(-math.log(10000.0) * place / half)
    angles = steps.astype(f32)[:, None] * frequency[None, :]
    wave = jnp.where((index < half)[None, :], jnp.cos(angles), jnp.sin(angles))
    return jax.nn.silu(wave).astype(bf16)


def by_blocks(w, own, width):
    parts = w.shape[1] // width
    return w.reshape(own, parts, width).transpose(1, 0, 2).reshape(parts * own, width)


def from_blocks(blocks, own, width):
    parts = blocks.shape[0] // own
    return blocks.reshape(parts, own, width).transpose(1, 0, 2).reshape(own, parts * width)


def local(tokens, cotangent, boxes, timesteps, w_ada, w_qkv, w_proj, w_up, w_down):
    section = lax.axis_index("section")
    group = lax.axis_size("dp")
    micro_count, _, frames, patches, width = tokens.shape
    hidden = w_up.shape[2]
    rows = frames * patches
    own = width // group
    ratio = hidden // width
    direct = own % 16 == 0 and group % ratio == 0
    c = Cfg(frames, patches, width, hidden, group if direct else ratio)

    shard = jnp.concatenate(
        [
            by_blocks(w_qkv[0].astype(bf16), own, width),
            w_proj[0].astype(bf16),
            by_blocks(w_up[0].astype(bf16), own, width),
            w_down[0].astype(bf16),
        ],
        axis=0,
    )
    weights = lax.all_gather(shard, "dp", axis=0, tiled=False)
    squares = 4 + ratio
    if not direct:
        weights = jnp.concatenate(
            [
                weights[:, i * own : (i + 1) * own].reshape(c.blocks, c.own, width)
                for i in range(squares)
            ]
            + [weights[:, squares * own :].reshape(c.blocks, ratio * c.own, width)],
            axis=1,
        )

    start = lax.axis_index("dp") * own
    index = start + jnp.arange(own, dtype=jnp.int32)
    steps = gather_small(timesteps.reshape(micro_count))
    steps = jnp.concatenate([jnp.zeros((group, 1), steps.dtype), steps], axis=1)
    embed = embed_columns(steps.reshape(-1), index, width)
    modulation = jnp.dot(embed, w_ada[0].astype(bf16), preferred_element_type=f32)
    modulation = scatter_small(modulation.reshape(group, 1 + micro_count, 6 * width))
    modulation = jnp.stack(
        [jnp.stack([modulation[0], modulation[1 + m]]) for m in range(micro_count)]
    )
    ctl = [
        jnp.concatenate([section.astype(jnp.int32)[None], boxes[m].reshape(-1)])
        for m in range(micro_count)
    ]

    tokens = tokens.reshape(micro_count, rows, width)
    cotangent = cotangent.reshape(micro_count, rows, width)
    whole = ((micro_count, rows, width), f32)
    one = ((rows, width), bf16)
    flops = 2 * rows * width * width * (4 + 2 * ratio)
    table = sizes(c)

    forward_names = [
        "x", "mod", "given", "mixed_a", "packed", "merged", "branch", "middle", "mixed_b",
        "hidden", "active", "out_branch", "acts", "send",
    ]
    back_names = [
        "grad", "grad_out_b", "grad_hidden", "temp", "grad_middle", "grad_branch", "grad_merged",
        "grad_packed", "grad_in", "sums", "grad_mod",
    ]
    kept, received = [], []
    acts = None
    for m in range(micro_count):
        operands = dict(ctl=ctl[m], x=tokens, mod=modulation, w=weights)
        news = dict(send=one, **{n: table[n] for n in KEPT})
        if acts is None:
            news["acts"] = whole
        else:
            operands["acts"] = acts
        alias = ["acts"] if acts is not None else []
        got = call(c, spatial_forward_kernel, m, operands, news, alias, forward_names, flops)
        acts = got["acts"]
        kept.append(got)
        received.append(lax.ppermute(got["send"], "section", [(0, 1)]))

    shared = None
    grads = []
    for m in range(micro_count):
        operands = dict(
            ctl=ctl[m], x=received[m], mod=modulation, w=weights, cot=cotangent, acts=acts
        )
        news = dict(send=one)
        alias = ["acts"]
        if shared is None:
            news["grad_in"] = whole
            news["grad_mod"] = ((micro_count, 2, 6 * width), f32)
            for n in TERMS:
                news[n] = ((micro_count * rows, table[n][0][1]), bf16)
        else:
            operands.update(shared)
            alias += list(shared)
        names = forward_names + back_names + ["heads_in", "heads_out"]
        got = call(c, temporal_kernel, m, operands, news, alias, names, 3 * flops)
        acts = got["acts"]
        shared = {n: got[n] for n in ("grad_in", "grad_mod") + TERMS}
        grads.append(lax.ppermute(got["send"], "section", [(1, 0)]))

    for m in range(micro_count):
        operands = dict(ctl=ctl[m], x=tokens, mod=modulation, w=weights, grad=grads[m])
        for n in KEPT:
            operands[n + "_kept" if n in TERMS else n] = kept[m][n]
        operands.update(shared)
        names = [n for n in forward_names if n not in ("acts", "send")] + back_names
        shared = call(
            c, spatial_backward_kernel, m, operands, {}, list(shared), names, 2 * flops
        )

    terms = weight_gradients(c, shared)
    if not direct:
        terms = jnp.concatenate(
            [
                terms[:, i * c.own : (i + 1) * c.own].reshape(group, own, width)
                for i in range(squares)
            ]
            + [terms[:, squares * c.own :].reshape(group, ratio * own, width)],
            axis=1,
        )
    total = lax.psum_scatter(terms, "dp", scatter_dimension=0, tiled=False).astype(f32)
    grad_qkv = from_blocks(total[: 3 * own], own, width)
    grad_proj = total[3 * own : 4 * own]
    grad_up = from_blocks(total[4 * own : squares * own], own, width)
    grad_down = total[squares * own :]

    sums = shared["grad_mod"]
    sums = jnp.concatenate([jnp.sum(sums[:, 0], axis=0, keepdims=True), sums[:, 1]])
    sums = gather_small(sums.astype(bf16)).reshape(group * (1 + micro_count), 6 * width)
    grad_ada = lax.dot_general(embed, sums, TN, preferred_element_type=f32)

    out_shape = (1, micro_count, 1, frames, patches, width)
    return (
        acts.reshape(out_shape),
        shared["grad_in"].reshape(out_shape),
        grad_ada[None],
        grad_qkv[None],
        grad_proj[None],
        grad_up[None],
        grad_down[None],
    )


def solution(mesh):
    placed = (
        P(None, "dp", None, None, None),
        P(None, "dp", None, None, None),
        P(None, "dp", None, None),
        P(None, "dp"),
        P("section", "dp", None),
        P("section", "dp", None),
        P("section", "dp", None),
        P("section", "dp", None),
        P("section", "dp", None),
    )
    return jax.shard_map(
        local,
        mesh=mesh,
        in_specs=placed,
        out_specs=(
            P("section", None, "dp", None, None, None),
            P("section", None, "dp", None, None, None),
            P("section", "dp", None),
            P("section", "dp", None),
            P("section", "dp", None),
            P("section", "dp", None),
            P("section", "dp", None),
        ),
        check_vma=False,
    )
```

```python
from functools import partial
import math

import jax
import jax.numpy as jnp
from jax import lax
from jax.experimental import pallas as pl
from jax.experimental.pallas import tpu as pltpu
from jax.sharding import PartitionSpec as P

HEAD_DIM = 64
GW = 16
LANES = 128
TILE = 64
EPS = 1e-06
VMEM_BYTES = 56 * 1024 * 1024
f32 = jnp.float32
bf16 = jnp.bfloat16
NN = (((1,), (0,)), ((), ()))
NT = (((1,), (1,)), ((), ()))
TN = (((0,), (0,)), ((), ()))


def mm(a, b, dims=NN):
    return lax.dot_general(a, b, dims, preferred_element_type=f32)


def ln(v):
    centred = v - jnp.mean(v, axis=-1, keepdims=True)
    inv = lax.rsqrt(jnp.mean(centred * centred, axis=-1, keepdims=True) + EPS)
    return centred * inv, inv


def ln_back(normed, inv, grad):
    return inv * (
        grad
        - jnp.mean(grad, axis=-1, keepdims=True)
        - normed * jnp.mean(grad * normed, axis=-1, keepdims=True)
    )


def whole(count, body):
    body(slice(0, count))


def tiles(count, body):
    for start in range(0, count, TILE):
        body(start)


class Refs(dict):
    __getattr__ = dict.__getitem__


class Cfg:
    def __init__(self, frames, patches, width, hidden, blocks):
        self.frames, self.patches, self.width, self.hidden = frames, patches, width, hidden
        self.rows = frames * patches
        self.ratio = hidden // width
        self.blocks = blocks
        self.own = width // blocks
        self.scaling = HEAD_DIM ** (-0.5)


def weight_copies(c, w, r):
    own = c.own
    out = {}
    for j in range(3):
        out["q%d" % j] = pltpu.make_async_copy(
            w.at[:, pl.ds(j * own, own), :], r.wq.at[j], r.wsem.at[j]
        )
    out["p"] = pltpu.make_async_copy(w.at[:, pl.ds(3 * own, own), :], r.wp, r.wsem.at[3])
    for j in range(c.ratio):
        out["u%d" % j] = pltpu.make_async_copy(
            w.at[:, pl.ds((4 + j) * own, own), :], r.wu.at[j], r.wsem.at[4 + j]
        )
    step = c.blocks // c.ratio
    for j in range(c.ratio):
        out["d%d" % j] = pltpu.make_async_copy(
            w.at[pl.ds(j * step, step), pl.ds((4 + c.ratio) * own, c.ratio * own), :],
            r.wd.at[pl.ds(j * step, step)],
            r.wsem.at[4 + c.ratio + j],
        )
    return out


def weight_scratch(c):
    return dict(
        wq=pltpu.VMEM((3, c.blocks, c.own, c.width), bf16),
        wp=pltpu.VMEM((c.blocks, c.own, c.width), bf16),
        wu=pltpu.VMEM((c.ratio, c.blocks, c.own, c.width), bf16),
        wd=pltpu.VMEM((c.blocks, c.ratio * c.own, c.width), bf16),
        wsem=pltpu.SemaphoreType.DMA((4 + 2 * c.ratio,)),
    )


def square(c, ref, *index):
    return ref[index].reshape(c.width, c.width)


def down_block(c, r, j):
    step = c.blocks // c.ratio
    return r.wd[j * step : (j + 1) * step].reshape(c.width, c.width)


def fill_given(c, ctl, r):
    patch = lax.broadcasted_iota(jnp.int32, (c.patches, LANES), 0)
    row, col = patch // GW, patch % GW
    for f in range(c.frames):
        top, bottom, left, right = (ctl[1 + 4 * f + i] for i in range(4))
        inside = (row >= top) & (row < bottom) & (col >= left) & (col < right)
        r.given[f * c.patches : (f + 1) * c.patches, :] = jnp.where(inside, 1.0, 0.0)


def pick(c, r, index, given):
    where = slice(index * c.width, (index + 1) * c.width)
    return jnp.where(given, r.mod[0:1, where], r.mod[1:2, where])


def is_given(r, rows):
    return r.given[rows, 0:1] > 0.5


def forward_a(c, r):
    def body(rows):
        given = is_given(r, rows)
        normed, _ = ln(r.x[rows, :].astype(f32))
        r.mixed_a[rows, :] = (normed * (1.0 + pick(c, r, 1, given)) + pick(c, r, 0, given)).astype(
            bf16
        )

    whole(c.rows, body)


def forward_qkv(c, r, wait):
    for j in range(3):
        wait("q%d" % j)
        r.packed[:, j * c.width : (j + 1) * c.width] = mm(
            r.mixed_a[...], square(c, r.wq, j)
        ).astype(bf16)


def halves(pair):
    first = lax.broadcasted_iota(jnp.int32, pair.shape, 1) < HEAD_DIM
    zero = jnp.zeros_like(pair)
    return jnp.concatenate([jnp.where(first, pair, zero), jnp.where(first, zero, pair)], axis=0)


def softmax_rows(scores):
    top = jnp.max(scores, axis=-1, keepdims=True)
    exponent = jnp.exp(scores - top)
    return exponent * (1.0 / jnp.sum(exponent, axis=-1, keepdims=True))


def spatial_tiles(c):
    for f in range(c.frames):
        for pair in range(c.width // LANES):
            yield slice(f * c.patches, (f + 1) * c.patches), pair


def spatial_merge(c, r):
    for rows, pair in spatial_tiles(c):
        q, k, v = (
            r.packed[rows, i * c.width + pair * LANES : i * c.width + (pair + 1) * LANES]
            for i in range(3)
        )
        shares = softmax_rows(mm(halves(q), k, NT) * c.scaling).astype(bf16)
        side = jnp.concatenate([shares[: c.patches], shares[c.patches :]], axis=1)
        r.merged[rows, pair * LANES : (pair + 1) * LANES] = mm(side, halves(v)).astype(bf16)


def spatial_back(c, r):
    for rows, pair in spatial_tiles(c):
        cols = [
            slice(i * c.width + pair * LANES, i * c.width + (pair + 1) * LANES) for i in range(3)
        ]
        q, k, v = (r.packed[rows, cols[i]] for i in range(3))
        q2, k2 = halves(q), halves(k)
        d2 = halves(r.grad_merged[rows, cols[0]])
        soft = softmax_rows(mm(q2, k, NT) * c.scaling)
        grad_shares = mm(d2, v, NT)
        inner = jnp.sum(soft * grad_shares, axis=-1, keepdims=True)
        grad_scores = (soft * (grad_shares - inner)).astype(bf16)
        side = jnp.concatenate([grad_scores[: c.patches], grad_scores[c.patches :]], axis=1)
        r.grad_packed[rows, cols[0]] = (mm(side, k2) * c.scaling).astype(bf16)
        r.grad_packed[rows, cols[1]] = (mm(grad_scores, q2, TN) * c.scaling).astype(bf16)
        r.grad_packed[rows, cols[2]] = mm(soft.astype(bf16), d2, TN).astype(bf16)


def fill_heads(c, r):
    lane = lax.broadcasted_iota(jnp.int32, (c.width, LANES), 0) // HEAD_DIM
    col = lax.broadcasted_iota(jnp.int32, (c.width, LANES), 1)
    r.heads_in[...] = jnp.where(lane == col, 1.0, 0.0).astype(bf16)
    col = lax.broadcasted_iota(jnp.int32, (LANES, c.width), 0)
    lane = lax.broadcasted_iota(jnp.int32, (LANES, c.width), 1) // HEAD_DIM
    r.heads_out[...] = jnp.where(lane == col, 1.0, 0.0).astype(bf16)


def head_sums(r, product):
    high = product.astype(bf16)
    low = (product - high.astype(f32)).astype(bf16)
    return mm(high, r.heads_in[...]) + mm(low, r.heads_in[...])


def frame_pairs(c):
    return [(f, g) for f in range(c.frames) for g in range(c.frames)]


def temporal_parts(c, r, ref, rows, part):
    return [
        ref[
            f * c.patches + rows : f * c.patches + rows + TILE,
            part * c.width : (part + 1) * c.width,
        ].astype(f32)
        for f in range(c.frames)
    ]


def temporal_soft(c, r, queries, keys):
    product = jnp.concatenate([queries[f] * keys[g] for f, g in frame_pairs(c)], axis=0)
    scores = head_sums(r, product) * c.scaling
    soft = []
    for f in range(c.frames):
        row = [scores[(f * c.frames + g) * TILE : (f * c.frames + g + 1) * TILE] for g in range(c.frames)]
        top = row[0]
        for entry in row[1:]:
            top = jnp.maximum(top, entry)
        exponent = [jnp.exp(entry - top) for entry in row]
        total = exponent[0]
        for entry in exponent[1:]:
            total = total + entry
        soft += [entry * (1.0 / total) for entry in exponent]
    return soft


def spread(r, columns):
    wide = mm(jnp.concatenate([v.astype(bf16) for v in columns], axis=0), r.heads_out[...])
    return [wide[i * TILE : (i + 1) * TILE] for i in range(len(columns))]


def temporal_merge(c, r):
    def body(rows):
        queries, keys, values = (temporal_parts(c, r, r.packed, rows, i) for i in range(3))
        shares = spread(r, temporal_soft(c, r, queries, keys))
        for f in range(c.frames):
            total = shares[f * c.frames] * values[0]
            for g in range(1, c.frames):
                total = total + shares[f * c.frames + g] * values[g]
            at = f * c.patches + rows
            r.merged[at : at + TILE, :] = total.astype(bf16)

    tiles(c.patches, body)


def temporal_back(c, r):
    n = c.frames

    def body(rows):
        queries, keys, values = (temporal_parts(c, r, r.packed, rows, i) for i in range(3))
        grads = temporal_parts(c, r, r.grad_merged, rows, 0)
        soft = temporal_soft(c, r, queries, keys)
        product = jnp.concatenate([grads[f] * values[g] for f, g in frame_pairs(c)], axis=0)
        wide = head_sums(r, product)
        grad_shares = [wide[i * TILE : (i + 1) * TILE] for i in range(n * n)]
        grad_scores = []
        for f in range(n):
            inner = soft[f * n] * grad_shares[f * n]
            for g in range(1, n):
                inner = inner + soft[f * n + g] * grad_shares[f * n + g]
            grad_scores += [
                soft[f * n + g] * (grad_shares[f * n + g] - inner) for g in range(n)
            ]
        shares = spread(r, soft)
        scores = spread(r, grad_scores)

        def put(frame, part, value):
            at = frame * c.patches + rows
            r.grad_packed[at : at + TILE, part * c.width : (part + 1) * c.width] = value.astype(bf16)

        for f in range(n):
            put(f, 0, sum(scores[f * n + g] * keys[g] for g in range(n)) * c.scaling)
            put(f, 1, sum(scores[g * n + f] * queries[g] for g in range(n)) * c.scaling)
            put(f, 2, sum(shares[g * n + f] * grads[g] for g in range(n)))

    tiles(c.patches, body)


def forward_b(c, r, wait):
    wait("p")
    r.branch[...] = mm(r.merged[...], r.wp[...].reshape(c.width, c.width))

    def body(rows):
        given = is_given(r, rows)
        middle = r.x[rows, :].astype(f32) + pick(c, r, 2, given) * r.branch[rows, :]
        r.middle[rows, :] = middle
        normed, _ = ln(middle)
        r.mixed_b[rows, :] = (normed * (1.0 + pick(c, r, 4, given)) + pick(c, r, 3, given)).astype(
            bf16
        )

    whole(c.rows, body)


GELU_A = math.sqrt(2.0 / math.pi)
GELU_B = 0.044715


def forward_mlp(c, r, wait):
    for j in range(c.ratio):
        wait("u%d" % j)
        cols = slice(j * c.width, (j + 1) * c.width)
        r.hidden[:, cols] = mm(r.mixed_b[...], square(c, r.wu, j))

        def body(rows):
            h = r.hidden[rows, cols]
            bent = jnp.tanh(GELU_A * (h + GELU_B * (h * h * h)))
            r.active[rows, cols] = (0.5 * h * (1.0 + bent)).astype(bf16)

        whole(c.rows, body)
    for j in range(c.ratio):
        wait("d%d" % j)
    r.out_branch[...] = mm(r.active[...], r.wd[...].reshape(c.hidden, c.width))


def forward_end(c, r):
    def body(rows):
        given = is_given(r, rows)
        result = r.middle[rows, :] + pick(c, r, 5, given) * r.out_branch[rows, :]
        r.acts[rows, :] = result
        if "send" in r:
            r.send[rows, :] = result.astype(bf16)

    whole(c.rows, body)


def add_sums(c, r, index, given, value):
    cols = slice(index * c.width, (index + 1) * c.width)
    mine = jnp.where(given, value, 0.0)
    rest = jnp.where(given, 0.0, value)
    shape = (value.shape[0] // 8, 8, c.width)
    r.sums[0, :, cols] = jnp.sum(mine.reshape(shape), axis=0)
    r.sums[1, :, cols] = jnp.sum(rest.reshape(shape), axis=0)


def backward_mlp(c, r, wait, gelu_again, put):
    def start(rows):
        given = is_given(r, rows)
        grad = r.grad[rows, :].astype(f32)
        r.grad_out_b[rows, :] = (pick(c, r, 5, given) * grad).astype(bf16)
        add_sums(c, r, 5, given, grad * r.out_branch[rows, :])

    whole(c.rows, start)
    put("grad_out_b")
    for j in range(c.ratio):
        wait("d%d" % j)
        cols = slice(j * c.width, (j + 1) * c.width)
        r.temp[...] = mm(r.grad_out_b[...], down_block(c, r, j), NT)

        def body(rows):
            h = r.hidden[rows, cols]
            square_h = h * h
            bent = jnp.tanh(GELU_A * (h + GELU_B * (square_h * h)))
            slope = 0.5 * (1.0 + bent) + 0.5 * h * (1.0 - bent * bent) * (
                GELU_A * (1.0 + 3.0 * GELU_B * square_h)
            )
            r.grad_hidden[rows, cols] = (r.temp[rows, :] * slope).astype(bf16)
            if gelu_again:
                r.active[rows, cols] = (0.5 * h * (1.0 + bent)).astype(bf16)

        whole(c.rows, body)
    for j in range(c.ratio):
        wait("u%d" % j)
        part = mm(r.grad_hidden[:, j * c.width : (j + 1) * c.width], square(c, r.wu, j), NT)
        if j == 0:
            r.temp[...] = part
        else:
            r.temp[...] += part


def backward_mid(c, r, wait, mix_again):
    def body(rows):
        given = is_given(r, rows)
        normed, inv = ln(r.middle[rows, :])
        scale = 1.0 + pick(c, r, 4, given)
        if mix_again:
            r.mixed_b[rows, :] = (normed * scale + pick(c, r, 3, given)).astype(bf16)
        grad_mixed = r.temp[rows, :]
        middle = r.grad[rows, :].astype(f32) + ln_back(normed, inv, grad_mixed * scale)
        r.grad_middle[rows, :] = middle
        r.grad_branch[rows, :] = (pick(c, r, 2, given) * middle).astype(bf16)
        add_sums(c, r, 3, given, grad_mixed)
        add_sums(c, r, 4, given, grad_mixed * normed)
        add_sums(c, r, 2, given, middle * r.branch[rows, :])

    whole(c.rows, body)
    wait("p")
    r.grad_merged[...] = mm(
        r.grad_branch[...], r.wp[...].reshape(c.width, c.width), NT
    ).astype(bf16)


def backward_end(c, r, wait, mix_again):
    for j in range(3):
        wait("q%d" % j)
        part = mm(r.grad_packed[:, j * c.width : (j + 1) * c.width], square(c, r.wq, j), NT)
        if j == 0:
            r.temp[...] = part
        else:
            r.temp[...] += part

    def body(rows):
        given = is_given(r, rows)
        normed, inv = ln(r.x[rows, :].astype(f32))
        scale = 1.0 + pick(c, r, 1, given)
        if mix_again:
            r.mixed_a[rows, :] = (normed * scale + pick(c, r, 0, given)).astype(bf16)
        grad_mixed = r.temp[rows, :]
        result = r.grad_middle[rows, :] + ln_back(normed, inv, grad_mixed * scale)
        r.grad_in[rows, :] = result
        if "send" in r:
            r.send[rows, :] = result.astype(bf16)
        add_sums(c, r, 0, given, grad_mixed)
        add_sums(c, r, 1, given, grad_mixed * normed)

    whole(c.rows, body)
    r.grad_mod[...] = jnp.sum(r.sums[...], axis=1)


def sizes(c):
    wide, rows = c.width, c.rows
    return dict(
        x=((rows, wide), bf16),
        mod=((2, 6 * wide), f32),
        given=((rows, LANES), f32),
        mixed_a=((rows, wide), bf16),
        packed=((rows, 3 * wide), bf16),
        merged=((rows, wide), bf16),
        branch=((rows, wide), f32),
        middle=((rows, wide), f32),
        mixed_b=((rows, wide), bf16),
        hidden=((rows, c.hidden), f32),
        active=((rows, c.hidden), bf16),
        out_branch=((rows, wide), f32),
        acts=((rows, wide), f32),
        send=((rows, wide), bf16),
        grad=((rows, wide), bf16),
        grad_out_b=((rows, wide), bf16),
        grad_hidden=((rows, c.hidden), bf16),
        temp=((rows, wide), f32),
        grad_middle=((rows, wide), f32),
        grad_branch=((rows, wide), bf16),
        grad_merged=((rows, wide), bf16),
        grad_packed=((rows, 3 * wide), bf16),
        grad_in=((rows, wide), f32),
        sums=((2, 8, 6 * wide), f32),
        grad_mod=((2, 6 * wide), f32),
        heads_in=((wide, LANES), bf16),
        heads_out=((LANES, wide), bf16),
    )


KEPT = ("packed", "merged", "branch", "middle", "hidden", "out_branch")
TERMS = (
    "mixed_a",
    "grad_packed",
    "merged",
    "grad_branch",
    "mixed_b",
    "grad_hidden",
    "active",
    "grad_out_b",
)


class Traffic:
    def __init__(self, sems):
        self.sems, self.used, self.pending = sems, 0, {}

    def start(self, name, src, dst):
        copy = pltpu.make_async_copy(src, dst, self.sems.at[self.used])
        self.used += 1
        copy.start()
        self.pending[name] = copy

    def wait(self, name):
        if name in self.pending:
            self.pending.pop(name).wait()

    def drain(self):
        for name in list(self.pending):
            self.wait(name)


def start_weights(copies, order, traffic):
    for name in order:
        copies[name].start()
        traffic.pending[name] = copies[name]


def order_forward(c):
    return (
        ["q0", "q1", "q2", "p"]
        + ["u%d" % j for j in range(c.ratio)]
        + ["d%d" % j for j in range(c.ratio)]
    )


def order_backward(c):
    return (
        ["d%d" % j for j in range(c.ratio)]
        + ["u%d" % j for j in range(c.ratio)]
        + ["p", "q0", "q1", "q2"]
    )


def run_forward(c, r, t, temporal, put):
    t.wait("mod")
    t.wait("x")
    forward_a(c, r)
    put("mixed_a")
    forward_qkv(c, r, t.wait)
    put("packed")
    if temporal:
        fill_heads(c, r)
        temporal_merge(c, r)
    else:
        spatial_merge(c, r)
    put("merged")
    forward_b(c, r, t.wait)
    put("branch")
    put("middle")
    put("mixed_b")
    forward_mlp(c, r, t.wait)
    put("hidden")
    put("active")
    put("out_branch")
    forward_end(c, r)
    put("acts")
    put("send")


def spatial_forward_kernel(c, micro, names, refs):
    h = Refs(names_hbm(names, refs))
    r = h.vmem

    @pl.when(h.ctl[0] == 0)
    def _():
        t = Traffic(r.sems)
        t.start("x", h.x.at[micro], r.x)
        t.start("mod", h.mod.at[micro], r.mod)
        start_weights(weight_copies(c, h.w, r), order_forward(c), t)
        fill_given(c, h.ctl, r)

        def put(name):
            if name in KEPT or name == "send":
                t.start(name, r[name], h[name])
            elif name == "acts":
                t.start(name, r.acts, h.acts.at[micro])

        run_forward(c, r, t, False, put)
        t.drain()


def temporal_kernel(c, micro, names, refs):
    h = Refs(names_hbm(names, refs))
    r = h.vmem

    @pl.when(h.ctl[0] == 1)
    def _():
        t = Traffic(r.sems)
        t.start("x", h.x, r.x)
        t.start("mod", h.mod.at[micro], r.mod)
        start_weights(weight_copies(c, h.w, r), order_forward(c), t)
        t.start("grad", h.cot.at[micro], r.grad)
        fill_given(c, h.ctl, r)
        forward = Refs({k: v for k, v in r.items() if k != "send"})
        put = partial(put_backward, c, micro, h, r, t)
        run_forward(c, forward, t, True, lambda name: name == "send" or put(name))
        t.wait("grad")
        run_backward(c, r, t, True, put)
        t.drain()


def put_backward(c, micro, h, r, t, name):
    if name == "send":
        if "send" in h:
            t.start("send", r.send, h.send)
    elif name in ("acts", "grad_in", "grad_mod"):
        t.start(name, r[name], h[name].at[micro])
    elif name in TERMS:
        t.start(name, r[name], h[name].at[pl.ds(micro * c.rows, c.rows), :])


def run_backward(c, r, t, temporal, put):
    backward_mlp(c, r, t.wait, not temporal, put)
    put("grad_hidden")
    t.wait("middle")
    t.wait("branch")
    backward_mid(c, r, t.wait, not temporal)
    put("grad_branch")
    t.wait("packed")
    t.wait("merged")
    if temporal:
        temporal_back(c, r)
    else:
        put("active")
        put("mixed_b")
        put("merged")
        spatial_back(c, r)
    put("grad_packed")
    t.wait("x")
    backward_end(c, r, t.wait, not temporal)
    if not temporal:
        put("mixed_a")
    put("send")
    put("grad_in")
    put("grad_mod")


def spatial_backward_kernel(c, micro, names, refs):
    h = Refs(names_hbm(names, refs))
    r = h.vmem

    @pl.when(h.ctl[0] == 0)
    def _():
        t = Traffic(r.sems)
        t.start("grad", h.grad, r.grad)
        t.start("mod", h.mod.at[micro], r.mod)
        t.start("out_branch", h.out_branch, r.out_branch)
        t.start("hidden", h.hidden, r.hidden)
        copies = weight_copies(c, h.w, r)
        order = order_backward(c)
        start_weights(copies, order[: 2 * c.ratio], t)
        for name in ("middle", "branch", "packed", "merged"):
            t.start(name, h[name + "_kept"] if name in TERMS else h[name], r[name])
        t.start("x", h.x.at[micro], r.x)
        start_weights(copies, order[2 * c.ratio :], t)
        fill_given(c, h.ctl, r)
        for name in ("grad", "mod", "out_branch", "hidden"):
            t.wait(name)
        run_backward(c, r, t, False, partial(put_backward, c, micro, h, r, t))
        t.drain()


def names_hbm(names, refs):
    outer, inner = names
    found = dict(zip(outer, refs[: len(outer)], strict=True))
    found["vmem"] = Refs(zip(inner, refs[len(outer) :], strict=True))
    return found


def call(c, kernel, micro, operands, news, alias, scratch, flops):
    ins = list(operands)
    outs = list(alias) + list(news)
    shapes = [jax.ShapeDtypeStruct(operands[n].shape, operands[n].dtype) for n in alias]
    shapes += [jax.ShapeDtypeStruct(*news[n]) for n in news]
    table = sizes(c)
    inner = {n: pltpu.VMEM(*table[n]) for n in scratch}
    inner.update(weight_scratch(c))
    inner["sems"] = pltpu.SemaphoreType.DMA((32,))
    in_names = [n if n not in alias else "_" + n for n in ins]
    names = (in_names + outs, list(inner))
    got = pl.pallas_call(
        lambda *refs: kernel(c, micro, names, refs),
        out_shape=shapes,
        in_specs=[
            pl.BlockSpec(memory_space=pltpu.SMEM if n == "ctl" else pl.ANY) for n in ins
        ],
        out_specs=[pl.BlockSpec(memory_space=pl.ANY)] * len(outs),
        scratch_shapes=list(inner.values()),
        input_output_aliases={ins.index(n): i for i, n in enumerate(alias)},
        compiler_params=pltpu.CompilerParams(vmem_limit_bytes=VMEM_BYTES),
        cost_estimate=pl.CostEstimate(flops=flops, bytes_accessed=20_000_000, transcendentals=0),
    )(*operands.values())
    return dict(zip(outs, got, strict=True))


def gradients_kernel(c, count, *refs):
    terms = Refs(zip(TERMS, refs[: len(TERMS)], strict=True))
    out = refs[len(TERMS)]
    held = Refs(zip(TERMS, refs[len(TERMS) + 1 : 2 * len(TERMS) + 1], strict=True))
    slots, in_sems, out_sems = refs[2 * len(TERMS) + 1 :]
    order = ("active", "grad_out_b", "mixed_b", "grad_hidden", "merged", "grad_branch", "mixed_a", "grad_packed")
    copies = {
        n: pltpu.make_async_copy(terms[n], held[n], in_sems.at[i]) for i, n in enumerate(order)
    }
    for n in order:
        copies[n].start()
    wide, own, step = c.width, c.own, c.blocks // c.ratio
    waited = set()
    flying = {}

    def need(name):
        if name not in waited:
            copies[name].wait()
            waited.add(name)

    jobs = [("active", j, "grad_out_b", 0, 4 + c.ratio + j) for j in range(c.ratio)]
    jobs += [("mixed_b", 0, "grad_hidden", j, 4 + j) for j in range(c.ratio)]
    jobs += [("merged", 0, "grad_branch", 0, 3)]
    jobs += [("mixed_a", 0, "grad_packed", j, j) for j in range(3)]
    for number, (left, lj, right, rj, block) in enumerate(jobs):
        need(left)
        need(right)
        slot = number % 2
        if slot in flying:
            flying.pop(slot).wait()
        value = mm(
            held[left][:, lj * wide : (lj + 1) * wide],
            held[right][:, rj * wide : (rj + 1) * wide],
            TN,
        ).astype(bf16)
        if block >= 4 + c.ratio:
            slots[slot] = value.reshape(slots.shape[1:])
            j = block - 4 - c.ratio
            src = slots.at[slot].reshape(step, c.ratio * own, wide)
            dst = out.at[pl.ds(j * step, step), pl.ds((4 + c.ratio) * own, c.ratio * own), :]
        else:
            slots[slot] = value.reshape(slots.shape[1:])
            src = slots.at[slot]
            dst = out.at[:, pl.ds(block * own, own), :]
        flying[slot] = pltpu.make_async_copy(src, dst, out_sems.at[slot])
        flying[slot].start()
    for copy in flying.values():
        copy.wait()


def weight_gradients(c, terms):
    per_block = (4 + 2 * c.ratio) * c.own
    shapes = [terms[n].shape for n in TERMS]
    count = shapes[0][0]
    return pl.pallas_call(
        partial(gradients_kernel, c, count),
        out_shape=jax.ShapeDtypeStruct((c.blocks, per_block, c.width), bf16),
        in_specs=[pl.BlockSpec(memory_space=pl.ANY)] * len(TERMS),
        out_specs=pl.BlockSpec(memory_space=pl.ANY),
        scratch_shapes=[pltpu.VMEM(s, bf16) for s in shapes]
        + [
            pltpu.VMEM((2, c.blocks, c.own, c.width), bf16),
            pltpu.SemaphoreType.DMA((len(TERMS),)),
            pltpu.SemaphoreType.DMA((2,)),
        ],
        compiler_params=pltpu.CompilerParams(vmem_limit_bytes=VMEM_BYTES),
        cost_estimate=pl.CostEstimate(
            flops=2 * count * c.width * c.width * (4 + 2 * c.ratio),
            bytes_accessed=24_000_000,
            transcendentals=0,
        ),
    )(*[terms[n] for n in TERMS])


def swap(block, distance):
    count = lax.axis_size("dp")
    return lax.ppermute(block, "dp", [(i, i ^ distance) for i in range(count)])


def gather_small(block):
    count = lax.axis_size("dp")
    if count & (count - 1):
        return lax.all_gather(block, "dp", axis=0, tiled=False)
    mine = lax.axis_index("dp")
    held, distance = block[None], count // 2
    while distance:
        other = swap(held, distance)
        lower = (mine & distance) == 0
        pair = [jnp.where(lower, held, other), jnp.where(lower, other, held)]
        held = jnp.stack(pair, axis=1).reshape((-1,) + block.shape)
        distance //= 2
    return held


def scatter_small(blocks):
    count = lax.axis_size("dp")
    if count & (count - 1):
        return lax.psum_scatter(blocks, "dp", scatter_dimension=0, tiled=False)
    mine = lax.axis_index("dp")
    distance = 1
    while distance < count:
        low, high = blocks[0::2], blocks[1::2]
        upper = (mine & distance) != 0
        other = swap(jnp.where(upper, low, high), distance)
        blocks = jnp.where(upper, high, low) + other
        distance *= 2
    return blocks[0]


def embed_columns(steps, index, width):
    half = width // 2
    place = (index % half).astype(f32)
    frequency = jnp.exp(-math.log(10000.0) * place / half)
    angles = steps.astype(f32)[:, None] * frequency[None, :]
    wave = jnp.where((index < half)[None, :], jnp.cos(angles), jnp.sin(angles))
    return jax.nn.silu(wave).astype(bf16)


def by_blocks(w, own, width):
    parts = w.shape[1] // width
    return w.reshape(own, parts, width).transpose(1, 0, 2).reshape(parts * own, width)


def from_blocks(blocks, own, width):
    parts = blocks.shape[0] // own
    return blocks.reshape(parts, own, width).transpose(1, 0, 2).reshape(own, parts * width)


def local(tokens, cotangent, boxes, timesteps, w_ada, w_qkv, w_proj, w_up, w_down):
    section = lax.axis_index("section")
    group = lax.axis_size("dp")
    micro_count, _, frames, patches, width = tokens.shape
    hidden = w_up.shape[2]
    rows = frames * patches
    own = width // group
    ratio = hidden // width
    direct = own % 16 == 0 and group % ratio == 0
    c = Cfg(frames, patches, width, hidden, group if direct else ratio)

    shard = jnp.concatenate(
        [
            by_blocks(w_qkv[0].astype(bf16), own, width),
            w_proj[0].astype(bf16),
            by_blocks(w_up[0].astype(bf16), own, width),
            w_down[0].astype(bf16),
        ],
        axis=0,
    )
    weights = lax.all_gather(shard, "dp", axis=0, tiled=False)
    squares = 4 + ratio
    if not direct:
        weights = jnp.concatenate(
            [
                weights[:, i * own : (i + 1) * own].reshape(c.blocks, c.own, width)
                for i in range(squares)
            ]
            + [weights[:, squares * own :].reshape(c.blocks, ratio * c.own, width)],
            axis=1,
        )

    start = lax.axis_index("dp") * own
    index = start + jnp.arange(own, dtype=jnp.int32)
    steps = gather_small(timesteps.reshape(micro_count))
    steps = jnp.concatenate([jnp.zeros((group, 1), steps.dtype), steps], axis=1)
    embed = embed_columns(steps.reshape(-1), index, width)
    modulation = jnp.dot(embed, w_ada[0].astype(bf16), preferred_element_type=f32)
    modulation = scatter_small(modulation.reshape(group, 1 + micro_count, 6 * width))
    modulation = jnp.stack(
        [jnp.stack([modulation[0], modulation[1 + m]]) for m in range(micro_count)]
    )
    ctl = [
        jnp.concatenate([section.astype(jnp.int32)[None], boxes[m].reshape(-1)])
        for m in range(micro_count)
    ]

    tokens = tokens.reshape(micro_count, rows, width)
    cotangent = cotangent.reshape(micro_count, rows, width)
    whole = ((micro_count, rows, width), f32)
    one = ((rows, width), bf16)
    flops = 2 * rows * width * width * (4 + 2 * ratio)
    table = sizes(c)

    forward_names = [
        "x", "mod", "given", "mixed_a", "packed", "merged", "branch", "middle", "mixed_b",
        "hidden", "active", "out_branch", "acts", "send",
    ]
    back_names = [
        "grad", "grad_out_b", "grad_hidden", "temp", "grad_middle", "grad_branch", "grad_merged",
        "grad_packed", "grad_in", "sums", "grad_mod",
    ]
    kept, received = [], []
    acts = None
    for m in range(micro_count):
        operands = dict(ctl=ctl[m], x=tokens, mod=modulation, w=weights)
        news = dict(send=one, **{n: table[n] for n in KEPT})
        if acts is None:
            news["acts"] = whole
        else:
            operands["acts"] = acts
        alias = ["acts"] if acts is not None else []
        got = call(c, spatial_forward_kernel, m, operands, news, alias, forward_names, flops)
        acts = got["acts"]
        kept.append(got)
        received.append(lax.ppermute(got["send"], "section", [(0, 1)]))

    shared = None
    grads = []
    for m in range(micro_count):
        operands = dict(
            ctl=ctl[m], x=received[m], mod=modulation, w=weights, cot=cotangent, acts=acts
        )
        news = dict(send=one)
        alias = ["acts"]
        if shared is None:
            news["grad_in"] = whole
            news["grad_mod"] = ((micro_count, 2, 6 * width), f32)
            for n in TERMS:
                news[n] = ((micro_count * rows, table[n][0][1]), bf16)
        else:
            operands.update(shared)
            alias += list(shared)
        names = forward_names + back_names + ["heads_in", "heads_out"]
        got = call(c, temporal_kernel, m, operands, news, alias, names, 3 * flops)
        acts = got["acts"]
        shared = {n: got[n] for n in ("grad_in", "grad_mod") + TERMS}
        grads.append(lax.ppermute(got["send"], "section", [(1, 0)]))

    for m in range(micro_count):
        operands = dict(ctl=ctl[m], x=tokens, mod=modulation, w=weights, grad=grads[m])
        for n in KEPT:
            operands[n + "_kept" if n in TERMS else n] = kept[m][n]
        operands.update(shared)
        names = [n for n in forward_names if n not in ("acts", "send")] + back_names
        shared = call(
            c, spatial_backward_kernel, m, operands, {}, list(shared), names, 2 * flops
        )

    terms = weight_gradients(c, shared)
    if not direct:
        terms = jnp.concatenate(
            [
                terms[:, i * c.own : (i + 1) * c.own].reshape(group, own, width)
                for i in range(squares)
            ]
            + [terms[:, squares * c.own :].reshape(group, ratio * own, width)],
            axis=1,
        )
    total = lax.psum_scatter(terms, "dp", scatter_dimension=0, tiled=False).astype(f32)
    grad_qkv = from_blocks(total[: 3 * own], own, width)
    grad_proj = total[3 * own : 4 * own]
    grad_up = from_blocks(total[4 * own : squares * own], own, width)
    grad_down = total[squares * own :]

    sums = shared["grad_mod"]
    sums = jnp.concatenate([jnp.sum(sums[:, 0], axis=0, keepdims=True), sums[:, 1]])
    sums = gather_small(sums.astype(bf16)).reshape(group * (1 + micro_count), 6 * width)
    grad_ada = lax.dot_general(embed, sums, TN, preferred_element_type=f32)

    out_shape = (1, micro_count, 1, frames, patches, width)
    return (
        acts.reshape(out_shape),
        shared["grad_in"].reshape(out_shape),
        grad_ada[None],
        grad_qkv[None],
        grad_proj[None],
        grad_up[None],
        grad_down[None],
    )


def solution(mesh):
    placed = (
        P(None, "dp", None, None, None),
        P(None, "dp", None, None, None),
        P(None, "dp", None, None),
        P(None, "dp"),
        P("section", "dp", None),
        P("section", "dp", None),
        P("section", "dp", None),
        P("section", "dp", None),
        P("section", "dp", None),
    )
    return jax.shard_map(
        local,
        mesh=mesh,
        in_specs=placed,
        out_specs=(
            P("section", None, "dp", None, None, None),
            P("section", None, "dp", None, None, None),
            P("section", "dp", None),
            P("section", "dp", None),
            P("section", "dp", None),
            P("section", "dp", None),
            P("section", "dp", None),
        ),
        check_vma=False,
    )
```

```python
from functools import partial
import math

import jax
import jax.numpy as jnp
from jax import lax
from jax.experimental import pallas as pl
from jax.experimental.pallas import tpu as pltpu
from jax.sharding import PartitionSpec as P

HEAD_DIM = 64
GW = 16
LANES = 128
TILE = 64
STEP = 256
EPS = 1e-06
VMEM_BYTES = 56 * 1024 * 1024
f32 = jnp.float32
bf16 = jnp.bfloat16
NN = (((1,), (0,)), ((), ()))
NT = (((1,), (1,)), ((), ()))
TN = (((0,), (0,)), ((), ()))


def mm(a, b, dims=NN):
    return lax.dot_general(a, b, dims, preferred_element_type=f32)


def ln(v):
    centred = v - jnp.mean(v, axis=-1, keepdims=True)
    inv = lax.rsqrt(jnp.mean(centred * centred, axis=-1, keepdims=True) + EPS)
    return centred * inv, inv


def ln_back(normed, inv, grad):
    return inv * (
        grad
        - jnp.mean(grad, axis=-1, keepdims=True)
        - normed * jnp.mean(grad * normed, axis=-1, keepdims=True)
    )


def by_rows(count, body):
    @pl.loop(0, count // STEP)
    def _(i):
        body(pl.ds(pl.multiple_of(i * STEP, STEP), STEP))


def tiles(count, body):
    @pl.loop(0, count // TILE)
    def _(i):
        body(pl.multiple_of(i * TILE, TILE))


def columns(c, j):
    return pl.ds(pl.multiple_of(j * c.width, c.width), c.width)


class Refs(dict):
    __getattr__ = dict.__getitem__


class Names:
    def __getattr__(self, name):
        return name


N = Names()
DP, SECTION = "dp", "section"


class Cfg:
    def __init__(self, frames, patches, width, hidden, blocks):
        self.frames, self.patches, self.width, self.hidden = frames, patches, width, hidden
        self.rows = frames * patches
        self.ratio = hidden // width
        self.blocks = blocks
        self.own = width // blocks
        self.scaling = HEAD_DIM ** (-0.5)


def weight_copy(c, w, r, part, j):
    if part == 0:
        return pltpu.make_async_copy(w.at[:, pl.ds(j * c.own, c.own), :], r.wq.at[j], r.wsem.at[j])
    if part == 1:
        return pltpu.make_async_copy(w.at[:, pl.ds(3 * c.own, c.own), :], r.wp, r.wsem.at[3])
    if part == 2:
        rows = pl.ds((4 + j) * c.own, c.own)
        return pltpu.make_async_copy(w.at[:, rows, :], r.wu.at[j], r.wsem.at[4 + j])
    step = c.blocks // c.ratio
    rows = pl.ds((4 + c.ratio) * c.own, c.ratio * c.own)
    return pltpu.make_async_copy(
        w.at[pl.ds(j * step, step), rows, :],
        r.wd.at[pl.ds(j * step, step)],
        r.wsem.at[4 + c.ratio + j],
    )


def start_weights(c, w, r, order):
    for part in order:
        for j in range((3, 1, c.ratio, c.ratio)[part]):
            weight_copy(c, w, r, part, j).start()


def weight_scratch(c):
    return dict(
        wq=pltpu.VMEM((3, c.blocks, c.own, c.width), bf16),
        wp=pltpu.VMEM((c.blocks, c.own, c.width), bf16),
        wu=pltpu.VMEM((c.ratio, c.blocks, c.own, c.width), bf16),
        wd=pltpu.VMEM((c.blocks, c.ratio * c.own, c.width), bf16),
        wsem=pltpu.SemaphoreType.DMA((4 + 2 * c.ratio,)),
    )


def square(c, ref, j):
    return ref[j].reshape(c.width, c.width)


def down_block(c, r, j):
    step = c.blocks // c.ratio
    return r.wd[pl.ds(j * step, step)].reshape(c.width, c.width)


def fill_given(c, ctl, r):
    patch = lax.broadcasted_iota(jnp.int32, (c.patches, LANES), 0)
    row, col = patch // GW, patch % GW
    for f in range(c.frames):
        top, bottom, left, right = (ctl[1 + 4 * f + i] for i in range(4))
        inside = (row >= top) & (row < bottom) & (col >= left) & (col < right)
        r.given[f * c.patches : (f + 1) * c.patches, :] = jnp.where(inside, 1.0, 0.0)


def pick(c, r, index, given):
    where = slice(index * c.width, (index + 1) * c.width)
    return jnp.where(given, r.mod[0:1, where], r.mod[1:2, where])


def is_given(r, rows):
    return r.given[rows, 0:1] > 0.5


def forward_a(c, r):
    def body(rows):
        given = is_given(r, rows)
        normed, _ = ln(r.x[rows, :].astype(f32))
        r.mixed_a[rows, :] = (normed * (1.0 + pick(c, r, 1, given)) + pick(c, r, 0, given)).astype(
            bf16
        )

    by_rows(c.rows, body)


def forward_qkv(c, r, wait):
    @pl.loop(0, 3)
    def _(j):
        wait(0, j)
        r.packed[:, columns(c, j)] = mm(r.mixed_a[...], square(c, r.wq, j)).astype(bf16)


def halves(pair):
    first = lax.broadcasted_iota(jnp.int32, pair.shape, 1) < HEAD_DIM
    zero = jnp.zeros_like(pair)
    return jnp.concatenate([jnp.where(first, pair, zero), jnp.where(first, zero, pair)], axis=0)


def softmax_rows(scores):
    top = jnp.max(scores, axis=-1, keepdims=True)
    exponent = jnp.exp(scores - top)
    return exponent * (1.0 / jnp.sum(exponent, axis=-1, keepdims=True))


def spatial_tiles(c, body):
    @pl.loop(0, c.width // LANES, unroll=2)
    def _(pair):
        cols = [pl.ds(pl.multiple_of(i * c.width + pair * LANES, LANES), LANES) for i in range(3)]
        for f in range(c.frames):
            body(slice(f * c.patches, (f + 1) * c.patches), cols)


def spatial_merge(c, r):
    def body(rows, cols):
        q, k, v = (r.packed[rows, cols[i]] for i in range(3))
        shares = softmax_rows(mm(halves(q), k, NT) * c.scaling).astype(bf16)
        side = jnp.concatenate([shares[: c.patches], shares[c.patches :]], axis=1)
        r.merged[rows, cols[0]] = mm(side, halves(v)).astype(bf16)

    spatial_tiles(c, body)


def spatial_back(c, r):
    def body(rows, cols):
        q, k, v = (r.packed[rows, cols[i]] for i in range(3))
        q2, k2 = halves(q), halves(k)
        d2 = halves(r.grad_merged[rows, cols[0]])
        soft = softmax_rows(mm(q2, k, NT) * c.scaling)
        grad_shares = mm(d2, v, NT)
        inner = jnp.sum(soft * grad_shares, axis=-1, keepdims=True)
        grad_scores = (soft * (grad_shares - inner)).astype(bf16)
        side = jnp.concatenate([grad_scores[: c.patches], grad_scores[c.patches :]], axis=1)
        r.grad_packed[rows, cols[0]] = (mm(side, k2) * c.scaling).astype(bf16)
        r.grad_packed[rows, cols[1]] = (mm(grad_scores, q2, TN) * c.scaling).astype(bf16)
        r.grad_packed[rows, cols[2]] = mm(soft.astype(bf16), d2, TN).astype(bf16)

    spatial_tiles(c, body)


def fill_heads(c, r):
    lane = lax.broadcasted_iota(jnp.int32, (c.width, LANES), 0) // HEAD_DIM
    col = lax.broadcasted_iota(jnp.int32, (c.width, LANES), 1)
    r.heads_in[...] = jnp.where(lane == col, 1.0, 0.0).astype(bf16)
    col = lax.broadcasted_iota(jnp.int32, (LANES, c.width), 0)
    lane = lax.broadcasted_iota(jnp.int32, (LANES, c.width), 1) // HEAD_DIM
    r.heads_out[...] = jnp.where(lane == col, 1.0, 0.0).astype(bf16)


def head_sums(r, product):
    high = product.astype(bf16)
    low = (product - high.astype(f32)).astype(bf16)
    return mm(high, r.heads_in[...]) + mm(low, r.heads_in[...])


def frame_pairs(c):
    return [(f, g) for f in range(c.frames) for g in range(c.frames)]


def temporal_parts(c, r, ref, rows, part):
    return [
        ref[pl.ds(f * c.patches + rows, TILE), part * c.width : (part + 1) * c.width].astype(f32)
        for f in range(c.frames)
    ]


def temporal_soft(c, r, queries, keys):
    product = jnp.concatenate([queries[f] * keys[g] for f, g in frame_pairs(c)], axis=0)
    scores = head_sums(r, product) * c.scaling
    soft = []
    for f in range(c.frames):
        row = [scores[(f * c.frames + g) * TILE : (f * c.frames + g + 1) * TILE] for g in range(c.frames)]
        top = row[0]
        for entry in row[1:]:
            top = jnp.maximum(top, entry)
        exponent = [jnp.exp(entry - top) for entry in row]
        total = exponent[0]
        for entry in exponent[1:]:
            total = total + entry
        soft += [entry * (1.0 / total) for entry in exponent]
    return soft


def spread(r, columns):
    wide = mm(jnp.concatenate([v.astype(bf16) for v in columns], axis=0), r.heads_out[...])
    return [wide[i * TILE : (i + 1) * TILE] for i in range(len(columns))]


def temporal_merge(c, r):
    def body(rows):
        queries, keys, values = (temporal_parts(c, r, r.packed, rows, i) for i in range(3))
        shares = spread(r, temporal_soft(c, r, queries, keys))
        for f in range(c.frames):
            total = shares[f * c.frames] * values[0]
            for g in range(1, c.frames):
                total = total + shares[f * c.frames + g] * values[g]
            at = f * c.patches + rows
            r.merged[pl.ds(at, TILE), :] = total.astype(bf16)

    tiles(c.patches, body)


def temporal_back(c, r):
    n = c.frames

    def body(rows):
        queries, keys, values = (temporal_parts(c, r, r.packed, rows, i) for i in range(3))
        grads = temporal_parts(c, r, r.grad_merged, rows, 0)
        soft = temporal_soft(c, r, queries, keys)
        product = jnp.concatenate([grads[f] * values[g] for f, g in frame_pairs(c)], axis=0)
        wide = head_sums(r, product)
        grad_shares = [wide[i * TILE : (i + 1) * TILE] for i in range(n * n)]
        grad_scores = []
        for f in range(n):
            inner = soft[f * n] * grad_shares[f * n]
            for g in range(1, n):
                inner = inner + soft[f * n + g] * grad_shares[f * n + g]
            grad_scores += [
                soft[f * n + g] * (grad_shares[f * n + g] - inner) for g in range(n)
            ]
        shares = spread(r, soft)
        scores = spread(r, grad_scores)

        def put(frame, part, value):
            at = frame * c.patches + rows
            r.grad_packed[pl.ds(at, TILE), part * c.width : (part + 1) * c.width] = value.astype(bf16)

        for f in range(n):
            put(f, 0, sum(scores[f * n + g] * keys[g] for g in range(n)) * c.scaling)
            put(f, 1, sum(scores[g * n + f] * queries[g] for g in range(n)) * c.scaling)
            put(f, 2, sum(shares[g * n + f] * grads[g] for g in range(n)))

    tiles(c.patches, body)


def forward_b(c, r, wait):
    wait(1, 0)
    r.branch[...] = mm(r.merged[...], r.wp[...].reshape(c.width, c.width))

    def body(rows):
        given = is_given(r, rows)
        middle = r.x[rows, :].astype(f32) + pick(c, r, 2, given) * r.branch[rows, :]
        r.middle[rows, :] = middle
        normed, _ = ln(middle)
        r.mixed_b[rows, :] = (normed * (1.0 + pick(c, r, 4, given)) + pick(c, r, 3, given)).astype(
            bf16
        )

    by_rows(c.rows, body)


GELU_A = math.sqrt(2.0 / math.pi)
GELU_B = 0.044715


def forward_mlp(c, r, wait):
    @pl.loop(0, c.ratio)
    def _(j):
        wait(2, j)
        cols = columns(c, j)
        r.hidden[:, cols] = mm(r.mixed_b[...], square(c, r.wu, j))

        def body(rows):
            h = r.hidden[rows, cols]
            bent = jnp.tanh(GELU_A * (h + GELU_B * (h * h * h)))
            r.active[rows, cols] = (0.5 * h * (1.0 + bent)).astype(bf16)

        by_rows(c.rows, body)

    for j in range(c.ratio):
        wait(3, j)
    r.out_branch[...] = mm(r.active[...], r.wd[...].reshape(c.hidden, c.width))


def forward_end(c, r):
    def body(rows):
        given = is_given(r, rows)
        result = r.middle[rows, :] + pick(c, r, 5, given) * r.out_branch[rows, :]
        r.acts[rows, :] = result
        if N.send in r:
            r.send[rows, :] = result.astype(bf16)

    by_rows(c.rows, body)


def add_sums(c, r, index, given, value):
    cols = slice(index * c.width, (index + 1) * c.width)
    mine = jnp.where(given, value, 0.0)
    rest = jnp.where(given, 0.0, value)
    shape = (value.shape[0] // 8, 8, c.width)
    r.sums[0, :, cols] += jnp.sum(mine.reshape(shape), axis=0)
    r.sums[1, :, cols] += jnp.sum(rest.reshape(shape), axis=0)


def backward_mlp(c, r, wait, gelu_again, put):
    def start(rows):
        given = is_given(r, rows)
        grad = r.grad[rows, :].astype(f32)
        r.grad_out_b[rows, :] = (pick(c, r, 5, given) * grad).astype(bf16)
        add_sums(c, r, 5, given, grad * r.out_branch[rows, :])

    by_rows(c.rows, start)
    put(N.grad_out_b)

    @pl.loop(0, c.ratio)
    def _(j):
        wait(3, j)
        cols = columns(c, j)
        r.temp[...] = mm(r.grad_out_b[...], down_block(c, r, j), NT)

        def body(rows):
            h = r.hidden[rows, cols]
            square_h = h * h
            bent = jnp.tanh(GELU_A * (h + GELU_B * (square_h * h)))
            slope = 0.5 * (1.0 + bent) + 0.5 * h * (1.0 - bent * bent) * (
                GELU_A * (1.0 + 3.0 * GELU_B * square_h)
            )
            r.grad_hidden[rows, cols] = (r.temp[rows, :] * slope).astype(bf16)
            if gelu_again:
                r.active[rows, cols] = (0.5 * h * (1.0 + bent)).astype(bf16)

        by_rows(c.rows, body)

    r.temp[...] = jnp.zeros_like(r.temp)

    @pl.loop(0, c.ratio)
    def _(j):
        wait(2, j)
        r.temp[...] += mm(r.grad_hidden[:, columns(c, j)], square(c, r.wu, j), NT)


def backward_mid(c, r, wait, mix_again):
    def body(rows):
        given = is_given(r, rows)
        normed, inv = ln(r.middle[rows, :])
        scale = 1.0 + pick(c, r, 4, given)
        if mix_again:
            r.mixed_b[rows, :] = (normed * scale + pick(c, r, 3, given)).astype(bf16)
        grad_mixed = r.temp[rows, :]
        middle = r.grad[rows, :].astype(f32) + ln_back(normed, inv, grad_mixed * scale)
        r.grad_middle[rows, :] = middle
        r.grad_branch[rows, :] = (pick(c, r, 2, given) * middle).astype(bf16)
        add_sums(c, r, 3, given, grad_mixed)
        add_sums(c, r, 4, given, grad_mixed * normed)
        add_sums(c, r, 2, given, middle * r.branch[rows, :])

    by_rows(c.rows, body)
    wait(1, 0)
    r.grad_merged[...] = mm(
        r.grad_branch[...], r.wp[...].reshape(c.width, c.width), NT
    ).astype(bf16)


def backward_end(c, r, wait, mix_again):
    r.temp[...] = jnp.zeros_like(r.temp)

    @pl.loop(0, 3)
    def _(j):
        wait(0, j)
        r.temp[...] += mm(r.grad_packed[:, columns(c, j)], square(c, r.wq, j), NT)

    def body(rows):
        given = is_given(r, rows)
        normed, inv = ln(r.x[rows, :].astype(f32))
        scale = 1.0 + pick(c, r, 1, given)
        if mix_again:
            r.mixed_a[rows, :] = (normed * scale + pick(c, r, 0, given)).astype(bf16)
        grad_mixed = r.temp[rows, :]
        result = r.grad_middle[rows, :] + ln_back(normed, inv, grad_mixed * scale)
        r.grad_in[rows, :] = result
        if N.send in r:
            r.send[rows, :] = result.astype(bf16)
        add_sums(c, r, 0, given, grad_mixed)
        add_sums(c, r, 1, given, grad_mixed * normed)

    by_rows(c.rows, body)
    r.grad_mod[...] = jnp.sum(r.sums[...], axis=1)


def sizes(c):
    wide, rows = c.width, c.rows
    return dict(
        x=((rows, wide), bf16),
        mod=((2, 6 * wide), f32),
        given=((rows, LANES), f32),
        mixed_a=((rows, wide), bf16),
        packed=((rows, 3 * wide), bf16),
        merged=((rows, wide), bf16),
        branch=((rows, wide), f32),
        middle=((rows, wide), f32),
        mixed_b=((rows, wide), bf16),
        hidden=((rows, c.hidden), f32),
        active=((rows, c.hidden), bf16),
        out_branch=((rows, wide), f32),
        acts=((rows, wide), f32),
        send=((rows, wide), bf16),
        grad=((rows, wide), bf16),
        grad_out_b=((rows, wide), bf16),
        grad_hidden=((rows, c.hidden), bf16),
        temp=((rows, wide), f32),
        grad_middle=((rows, wide), f32),
        grad_branch=((rows, wide), bf16),
        grad_merged=((rows, wide), bf16),
        grad_packed=((rows, 3 * wide), bf16),
        grad_in=((rows, wide), f32),
        sums=((2, 8, 6 * wide), f32),
        grad_mod=((2, 6 * wide), f32),
        heads_in=((wide, LANES), bf16),
        heads_out=((LANES, wide), bf16),
    )


KEPT = (N.packed, N.merged, N.branch, N.middle, N.hidden, N.out_branch)
TERMS = (
    N.mixed_a,
    N.grad_packed,
    N.merged,
    N.grad_branch,
    N.mixed_b,
    N.grad_hidden,
    N.active,
    N.grad_out_b,
)


class Traffic:
    def __init__(self, sems):
        self.sems, self.used, self.pending = sems, 0, {}

    def start(self, name, src, dst):
        copy = pltpu.make_async_copy(src, dst, self.sems.at[self.used])
        self.used += 1
        copy.start()
        self.pending[name] = copy

    def wait(self, name):
        if name in self.pending:
            self.pending.pop(name).wait()

    def drain(self):
        for name in list(self.pending):
            self.wait(name)


def wait_weight(c, w, r, part, j):
    weight_copy(c, w, r, part, j).wait()


def run_forward(c, r, t, temporal, put, weight_wait):
    t.wait(N.mod)
    t.wait(N.x)
    forward_a(c, r)
    put(N.mixed_a)
    forward_qkv(c, r, weight_wait)
    put(N.packed)
    if temporal:
        fill_heads(c, r)
        temporal_merge(c, r)
    else:
        spatial_merge(c, r)
    put(N.merged)
    forward_b(c, r, weight_wait)
    put(N.branch)
    put(N.middle)
    put(N.mixed_b)
    forward_mlp(c, r, weight_wait)
    put(N.hidden)
    put(N.active)
    put(N.out_branch)
    forward_end(c, r)
    put(N.acts)
    put(N.send)


def spatial_forward_kernel(c, micro, names, refs):
    h = Refs(names_hbm(names, refs))
    r = h.vmem

    @pl.when(h.ctl[0] == 0)
    def _():
        t = Traffic(r.sems)
        t.start(N.x, h.x.at[micro], r.x)
        t.start(N.mod, h.mod.at[micro], r.mod)
        start_weights(c, h.w, r, (0, 1, 2, 3))
        fill_given(c, h.ctl, r)

        def put(name):
            if name in KEPT or name == N.send:
                t.start(name, r[name], h[name])
            elif name == N.acts:
                t.start(name, r.acts, h.acts.at[micro])

        run_forward(c, r, t, False, put, partial(wait_weight, c, h.w, r))
        t.drain()


def temporal_kernel(c, micro, names, refs):
    h = Refs(names_hbm(names, refs))
    r = h.vmem

    @pl.when(h.ctl[0] == 1)
    def _():
        t = Traffic(r.sems)
        t.start(N.x, h.x, r.x)
        t.start(N.mod, h.mod.at[micro], r.mod)
        start_weights(c, h.w, r, (0, 1, 2, 3))
        t.start(N.grad, h.cot.at[micro], r.grad)
        fill_given(c, h.ctl, r)
        forward = Refs({k: v for k, v in r.items() if k != N.send})
        put = partial(put_backward, c, micro, h, r, t)
        run_forward(
            c,
            forward,
            t,
            True,
            lambda name: name == N.send or put(name),
            partial(wait_weight, c, h.w, r),
        )
        t.wait(N.grad)
        run_backward(c, r, t, True, put, lambda part, j: None)
        t.drain()


def put_backward(c, micro, h, r, t, name):
    if name == N.send:
        if N.send in h:
            t.start(N.send, r.send, h.send)
    elif name in (N.acts, N.grad_in, N.grad_mod):
        t.start(name, r[name], h[name].at[micro])
    elif name in TERMS:
        t.start(name, r[name], h[name].at[pl.ds(micro * c.rows, c.rows), :])


def run_backward(c, r, t, temporal, put, weight_wait):
    r.sums[...] = jnp.zeros_like(r.sums)
    backward_mlp(c, r, weight_wait, not temporal, put)
    put(N.grad_hidden)
    t.wait(N.middle)
    t.wait(N.branch)
    backward_mid(c, r, weight_wait, not temporal)
    put(N.grad_branch)
    t.wait(N.packed)
    t.wait(N.merged)
    if temporal:
        temporal_back(c, r)
    else:
        put(N.active)
        put(N.mixed_b)
        put(N.merged)
        spatial_back(c, r)
    put(N.grad_packed)
    t.wait(N.x)
    backward_end(c, r, weight_wait, not temporal)
    if not temporal:
        put(N.mixed_a)
    put(N.send)
    put(N.grad_in)
    put(N.grad_mod)


def spatial_backward_kernel(c, micro, names, refs):
    h = Refs(names_hbm(names, refs))
    r = h.vmem

    @pl.when(h.ctl[0] == 0)
    def _():
        t = Traffic(r.sems)
        t.start(N.grad, h.grad, r.grad)
        t.start(N.mod, h.mod.at[micro], r.mod)
        t.start(N.out_branch, h.out_branch, r.out_branch)
        t.start(N.hidden, h.hidden, r.hidden)
        start_weights(c, h.w, r, (3, 2))
        for name in (N.middle, N.branch, N.packed, N.merged):
            t.start(name, h[name + "_kept"] if name in TERMS else h[name], r[name])
        t.start(N.x, h.x.at[micro], r.x)
        start_weights(c, h.w, r, (1, 0))
        fill_given(c, h.ctl, r)
        for name in (N.grad, N.mod, N.out_branch, N.hidden):
            t.wait(name)
        run_backward(
            c, r, t, False, partial(put_backward, c, micro, h, r, t), partial(wait_weight, c, h.w, r)
        )
        t.drain()


def names_hbm(names, refs):
    outer, inner = names
    found = dict(zip(outer, refs[: len(outer)], strict=True))
    found[N.vmem] = Refs(zip(inner, refs[len(outer) :], strict=True))
    return found


def call(c, kernel, micro, operands, news, alias, scratch, flops):
    ins = list(operands)
    outs = list(alias) + list(news)
    shapes = [jax.ShapeDtypeStruct(operands[n].shape, operands[n].dtype) for n in alias]
    shapes += [jax.ShapeDtypeStruct(*news[n]) for n in news]
    table = sizes(c)
    inner = {n: pltpu.VMEM(*table[n]) for n in scratch}
    inner.update(weight_scratch(c))
    inner[N.sems] = pltpu.SemaphoreType.DMA((32,))
    in_names = [n if n not in alias else "_" + n for n in ins]
    names = (in_names + outs, list(inner))
    got = pl.pallas_call(
        lambda *refs: kernel(c, micro, names, refs),
        out_shape=shapes,
        in_specs=[
            pl.BlockSpec(memory_space=pltpu.SMEM if n == N.ctl else pl.ANY) for n in ins
        ],
        out_specs=[pl.BlockSpec(memory_space=pl.ANY)] * len(outs),
        scratch_shapes=list(inner.values()),
        input_output_aliases={ins.index(n): i for i, n in enumerate(alias)},
        compiler_params=pltpu.CompilerParams(vmem_limit_bytes=VMEM_BYTES),
        cost_estimate=pl.CostEstimate(flops=flops, bytes_accessed=20_000_000, transcendentals=0),
    )(*operands.values())
    return dict(zip(outs, got, strict=True))


def gradients_kernel(c, *refs):
    count = len(TERMS)
    held = Refs(zip(TERMS, refs[count + 1 : 2 * count + 1], strict=True))
    out, slots, in_sems, out_sems = refs[count], *refs[2 * count + 1 :]
    copies = {
        n: pltpu.make_async_copy(refs[i], held[n], in_sems.at[i]) for i, n in enumerate(TERMS)
    }
    for n in reversed(TERMS):
        copies[n].start()
    wide, own, step = c.width, c.own, c.blocks // c.ratio
    down = 4 + c.ratio

    def put(block, j=None):
        if j is None:
            src, dst = slots.at[block], out.at[:, pl.ds(block * own, own), :]
        else:
            src = slots.at[block].reshape(step, c.ratio * own, wide)
            dst = out.at[pl.ds(j * step, step), pl.ds(down * own, c.ratio * own), :]
        return pltpu.make_async_copy(src, dst, out_sems.at[block])

    def product(block, left, right):
        slots[block] = mm(left, right, TN).astype(bf16).reshape(slots.shape[1:])

    copies[N.grad_out_b].wait()
    copies[N.active].wait()

    @pl.loop(0, c.ratio)
    def _(j):
        product(down + j, held.active[:, columns(c, j)], held.grad_out_b[...])
        put(down + j, j).start()

    copies[N.grad_hidden].wait()
    copies[N.mixed_b].wait()

    @pl.loop(0, c.ratio)
    def _(j):
        product(4 + j, held.mixed_b[...], held.grad_hidden[:, columns(c, j)])
        put(4 + j).start()

    copies[N.grad_branch].wait()
    copies[N.merged].wait()
    product(3, held.merged[...], held.grad_branch[...])
    put(3).start()
    copies[N.grad_packed].wait()
    copies[N.mixed_a].wait()

    @pl.loop(0, 3)
    def _(j):
        product(j, held.mixed_a[...], held.grad_packed[:, columns(c, j)])
        put(j).start()

    for block in range(down):
        put(block).wait()
    for j in range(c.ratio):
        put(down + j, j).wait()


def weight_gradients(c, terms):
    per_block = (4 + 2 * c.ratio) * c.own
    shapes = [terms[n].shape for n in TERMS]
    count = shapes[0][0]
    return pl.pallas_call(
        partial(gradients_kernel, c),
        out_shape=jax.ShapeDtypeStruct((c.blocks, per_block, c.width), bf16),
        in_specs=[pl.BlockSpec(memory_space=pl.ANY)] * len(TERMS),
        out_specs=pl.BlockSpec(memory_space=pl.ANY),
        scratch_shapes=[pltpu.VMEM(s, bf16) for s in shapes]
        + [
            pltpu.VMEM((4 + 2 * c.ratio, c.blocks, c.own, c.width), bf16),
            pltpu.SemaphoreType.DMA((len(TERMS),)),
            pltpu.SemaphoreType.DMA((4 + 2 * c.ratio,)),
        ],
        compiler_params=pltpu.CompilerParams(vmem_limit_bytes=VMEM_BYTES),
        cost_estimate=pl.CostEstimate(
            flops=2 * count * c.width * c.width * (4 + 2 * c.ratio),
            bytes_accessed=24_000_000,
            transcendentals=0,
        ),
    )(*[terms[n] for n in TERMS])


def swap(block, distance):
    count = lax.axis_size(DP)
    return lax.ppermute(block, DP, [(i, i ^ distance) for i in range(count)])


def gather_small(block):
    count = lax.axis_size(DP)
    if count & (count - 1):
        return lax.all_gather(block, DP, axis=0, tiled=False)
    mine = lax.axis_index(DP)
    held, distance = block[None], count // 2
    while distance:
        other = swap(held, distance)
        lower = (mine & distance) == 0
        pair = [jnp.where(lower, held, other), jnp.where(lower, other, held)]
        held = jnp.stack(pair, axis=1).reshape((-1,) + block.shape)
        distance //= 2
    return held


def scatter_small(blocks):
    count = lax.axis_size(DP)
    if count & (count - 1):
        return lax.psum_scatter(blocks, DP, scatter_dimension=0, tiled=False)
    mine = lax.axis_index(DP)
    distance = 1
    while distance < count:
        low, high = blocks[0::2], blocks[1::2]
        upper = (mine & distance) != 0
        other = swap(jnp.where(upper, low, high), distance)
        blocks = jnp.where(upper, high, low) + other
        distance *= 2
    return blocks[0]


def embed_columns(steps, index, width):
    half = width // 2
    place = (index % half).astype(f32)
    frequency = jnp.exp(-math.log(10000.0) * place / half)
    angles = steps.astype(f32)[:, None] * frequency[None, :]
    wave = jnp.where((index < half)[None, :], jnp.cos(angles), jnp.sin(angles))
    return jax.nn.silu(wave).astype(bf16)


def by_blocks(w, own, width):
    parts = w.shape[1] // width
    return w.reshape(own, parts, width).transpose(1, 0, 2).reshape(parts * own, width)


def from_blocks(blocks, own, width):
    parts = blocks.shape[0] // own
    return blocks.reshape(parts, own, width).transpose(1, 0, 2).reshape(own, parts * width)


def local(tokens, cotangent, boxes, timesteps, w_ada, w_qkv, w_proj, w_up, w_down):
    section = lax.axis_index(SECTION)
    group = lax.axis_size(DP)
    micro_count, _, frames, patches, width = tokens.shape
    hidden = w_up.shape[2]
    rows = frames * patches
    own = width // group
    ratio = hidden // width
    direct = own % 16 == 0 and group % ratio == 0
    c = Cfg(frames, patches, width, hidden, group if direct else ratio)

    shard = jnp.concatenate(
        [
            by_blocks(w_qkv[0].astype(bf16), own, width),
            w_proj[0].astype(bf16),
            by_blocks(w_up[0].astype(bf16), own, width),
            w_down[0].astype(bf16),
        ],
        axis=0,
    )
    weights = lax.all_gather(shard, DP, axis=0, tiled=False)
    squares = 4 + ratio
    if not direct:
        weights = jnp.concatenate(
            [
                weights[:, i * own : (i + 1) * own].reshape(c.blocks, c.own, width)
                for i in range(squares)
            ]
            + [weights[:, squares * own :].reshape(c.blocks, ratio * c.own, width)],
            axis=1,
        )

    start = lax.axis_index(DP) * own
    index = start + jnp.arange(own, dtype=jnp.int32)
    steps = gather_small(timesteps.reshape(micro_count))
    steps = jnp.concatenate([jnp.zeros((group, 1), steps.dtype), steps], axis=1)
    embed = embed_columns(steps.reshape(-1), index, width)
    modulation = jnp.dot(embed, w_ada[0].astype(bf16), preferred_element_type=f32)
    modulation = scatter_small(modulation.reshape(group, 1 + micro_count, 6 * width))
    modulation = jnp.stack(
        [jnp.stack([modulation[0], modulation[1 + m]]) for m in range(micro_count)]
    )
    ctl = [
        jnp.concatenate([section.astype(jnp.int32)[None], boxes[m].reshape(-1)])
        for m in range(micro_count)
    ]

    tokens = tokens.reshape(micro_count, rows, width)
    cotangent = cotangent.reshape(micro_count, rows, width)
    whole = ((micro_count, rows, width), f32)
    one = ((rows, width), bf16)
    flops = 2 * rows * width * width * (4 + 2 * ratio)
    table = sizes(c)

    forward_names = [
        N.x, N.mod, N.given, N.mixed_a, N.packed, N.merged, N.branch, N.middle, N.mixed_b,
        N.hidden, N.active, N.out_branch, N.acts, N.send,
    ]
    back_names = [
        N.grad, N.grad_out_b, N.grad_hidden, N.temp, N.grad_middle, N.grad_branch, N.grad_merged,
        N.grad_packed, N.grad_in, N.sums, N.grad_mod,
    ]
    kept, received = [], []
    acts = None
    for m in range(micro_count):
        operands = dict(ctl=ctl[m], x=tokens, mod=modulation, w=weights)
        news = dict(send=one, **{n: table[n] for n in KEPT})
        if acts is None:
            news[N.acts] = whole
        else:
            operands[N.acts] = acts
        alias = [N.acts] if acts is not None else []
        got = call(c, spatial_forward_kernel, m, operands, news, alias, forward_names, flops)
        acts = got[N.acts]
        kept.append(got)
        received.append(lax.ppermute(got[N.send], SECTION, [(0, 1)]))

    shared = None
    grads = []
    for m in range(micro_count):
        operands = dict(
            ctl=ctl[m], x=received[m], mod=modulation, w=weights, cot=cotangent, acts=acts
        )
        news = dict(send=one)
        alias = [N.acts]
        if shared is None:
            news[N.grad_in] = whole
            news[N.grad_mod] = ((micro_count, 2, 6 * width), f32)
            for n in TERMS:
                news[n] = ((micro_count * rows, table[n][0][1]), bf16)
        else:
            operands.update(shared)
            alias += list(shared)
        names = forward_names + back_names + [N.heads_in, N.heads_out]
        got = call(c, temporal_kernel, m, operands, news, alias, names, 3 * flops)
        acts = got[N.acts]
        shared = {n: got[n] for n in (N.grad_in, N.grad_mod) + TERMS}
        grads.append(lax.ppermute(got[N.send], SECTION, [(1, 0)]))

    for m in range(micro_count):
        operands = dict(ctl=ctl[m], x=tokens, mod=modulation, w=weights, grad=grads[m])
        for n in KEPT:
            operands[n + "_kept" if n in TERMS else n] = kept[m][n]
        operands.update(shared)
        names = [n for n in forward_names if n not in (N.acts, N.send)] + back_names
        shared = call(
            c, spatial_backward_kernel, m, operands, {}, list(shared), names, 2 * flops
        )

    terms = weight_gradients(c, shared)
    if not direct:
        terms = jnp.concatenate(
            [
                terms[:, i * c.own : (i + 1) * c.own].reshape(group, own, width)
                for i in range(squares)
            ]
            + [terms[:, squares * c.own :].reshape(group, ratio * own, width)],
            axis=1,
        )
    total = lax.psum_scatter(terms, DP, scatter_dimension=0, tiled=False).astype(f32)
    grad_qkv = from_blocks(total[: 3 * own], own, width)
    grad_proj = total[3 * own : 4 * own]
    grad_up = from_blocks(total[4 * own : squares * own], own, width)
    grad_down = total[squares * own :]

    sums = shared[N.grad_mod]
    sums = jnp.concatenate([jnp.sum(sums[:, 0], axis=0, keepdims=True), sums[:, 1]])
    sums = gather_small(sums.astype(bf16)).reshape(group * (1 + micro_count), 6 * width)
    grad_ada = lax.dot_general(embed, sums, TN, preferred_element_type=f32)

    out_shape = (1, micro_count, 1, frames, patches, width)
    return (
        acts.reshape(out_shape),
        shared[N.grad_in].reshape(out_shape),
        grad_ada[None],
        grad_qkv[None],
        grad_proj[None],
        grad_up[None],
        grad_down[None],
    )


def solution(mesh):
    placed = (
        P(None, DP, None, None, None),
        P(None, DP, None, None, None),
        P(None, DP, None, None),
        P(None, DP),
        P(SECTION, DP, None),
        P(SECTION, DP, None),
        P(SECTION, DP, None),
        P(SECTION, DP, None),
        P(SECTION, DP, None),
    )
    return jax.shard_map(
        local,
        mesh=mesh,
        in_specs=placed,
        out_specs=(
            P(SECTION, None, DP, None, None, None),
            P(SECTION, None, DP, None, None, None),
            P(SECTION, DP, None),
            P(SECTION, DP, None),
            P(SECTION, DP, None),
            P(SECTION, DP, None),
            P(SECTION, DP, None),
        ),
        check_vma=False,
    )
```

```python
from functools import partial
import math

import jax
import jax.numpy as jnp
from jax import lax
from jax.experimental import pallas as pl
from jax.experimental.pallas import tpu as pltpu
from jax.sharding import PartitionSpec as P

HEAD_DIM = 64
GW = 16
LANES = 128
TILE = 64
STEP = 256
EPS = 1e-06
VMEM_BYTES = 56 * 1024 * 1024
f32 = jnp.float32
bf16 = jnp.bfloat16
NN = (((1,), (0,)), ((), ()))
NT = (((1,), (1,)), ((), ()))
TN = (((0,), (0,)), ((), ()))


def mm(a, b, dims=NN):
    return lax.dot_general(a, b, dims, preferred_element_type=f32)


def ln(v):
    centred = v - jnp.mean(v, axis=-1, keepdims=True)
    inv = lax.rsqrt(jnp.mean(centred * centred, axis=-1, keepdims=True) + EPS)
    return centred * inv, inv


def ln_back(normed, inv, grad):
    return inv * (
        grad
        - jnp.mean(grad, axis=-1, keepdims=True)
        - normed * jnp.mean(grad * normed, axis=-1, keepdims=True)
    )


def by_rows(count, body):
    @pl.loop(0, count // STEP)
    def _(i):
        body(pl.ds(pl.multiple_of(i * STEP, STEP), STEP))


def tiles(count, body):
    @pl.loop(0, count // TILE)
    def _(i):
        body(pl.multiple_of(i * TILE, TILE))


def columns(c, j):
    return pl.ds(pl.multiple_of(j * c.width, c.width), c.width)


class Refs(dict):
    __getattr__ = dict.__getitem__


class Names:
    def __getattr__(self, name):
        return name


N = Names()
DP, SECTION = "dp", "section"


class Cfg:
    def __init__(self, frames, patches, width, hidden, blocks):
        self.frames, self.patches, self.width, self.hidden = frames, patches, width, hidden
        self.rows = frames * patches
        self.ratio = hidden // width
        self.blocks = blocks
        self.own = width // blocks
        self.scaling = HEAD_DIM ** (-0.5)


def weight_copy(c, w, r, part, j):
    if part == 0:
        return pltpu.make_async_copy(w.at[:, pl.ds(j * c.own, c.own), :], r.wq.at[j], r.wsem.at[j])
    if part == 1:
        return pltpu.make_async_copy(w.at[:, pl.ds(3 * c.own, c.own), :], r.wp, r.wsem.at[3])
    if part == 2:
        rows = pl.ds((4 + j) * c.own, c.own)
        return pltpu.make_async_copy(w.at[:, rows, :], r.wu.at[j], r.wsem.at[4 + j])
    step = c.blocks // c.ratio
    rows = pl.ds((4 + c.ratio) * c.own, c.ratio * c.own)
    return pltpu.make_async_copy(
        w.at[pl.ds(j * step, step), rows, :],
        r.wd.at[pl.ds(j * step, step)],
        r.wsem.at[4 + c.ratio + j],
    )


def start_weights(c, w, r, order):
    for part in order:
        for j in range((3, 1, c.ratio, c.ratio)[part]):
            weight_copy(c, w, r, part, j).start()


def weight_scratch(c):
    return dict(
        wq=pltpu.VMEM((3, c.blocks, c.own, c.width), bf16),
        wp=pltpu.VMEM((c.blocks, c.own, c.width), bf16),
        wu=pltpu.VMEM((c.ratio, c.blocks, c.own, c.width), bf16),
        wd=pltpu.VMEM((c.blocks, c.ratio * c.own, c.width), bf16),
        wsem=pltpu.SemaphoreType.DMA((4 + 2 * c.ratio,)),
    )


def square(c, ref, j):
    return ref[j].reshape(c.width, c.width)


def down_block(c, r, j):
    step = c.blocks // c.ratio
    return r.wd[pl.ds(j * step, step)].reshape(c.width, c.width)


def fill_given(c, ctl, r):
    patch = lax.broadcasted_iota(jnp.int32, (c.patches, LANES), 0)
    row, col = patch // GW, patch % GW
    for f in range(c.frames):
        top, bottom, left, right = (ctl[1 + 4 * f + i] for i in range(4))
        inside = (row >= top) & (row < bottom) & (col >= left) & (col < right)
        r.given[f * c.patches : (f + 1) * c.patches, :] = jnp.where(inside, 1.0, 0.0)


def pick(c, r, index, given):
    where = slice(index * c.width, (index + 1) * c.width)
    return jnp.where(given, r.mod[0:1, where], r.mod[1:2, where])


def is_given(r, rows):
    return r.given[rows, 0:1] > 0.5


def forward_a(c, r):
    def body(rows):
        given = is_given(r, rows)
        normed, _ = ln(r.x[rows, :].astype(f32))
        r.mixed_a[rows, :] = (normed * (1.0 + pick(c, r, 1, given)) + pick(c, r, 0, given)).astype(
            bf16
        )

    by_rows(c.rows, body)


def forward_qkv(c, r, wait):
    @pl.loop(0, 3)
    def _(j):
        wait(0, j)
        r.packed[:, columns(c, j)] = mm(r.mixed_a[...], square(c, r.wq, j)).astype(bf16)


def halves(pair):
    first = lax.broadcasted_iota(jnp.int32, pair.shape, 1) < HEAD_DIM
    zero = jnp.zeros_like(pair)
    return jnp.concatenate([jnp.where(first, pair, zero), jnp.where(first, zero, pair)], axis=0)


def softmax_rows(scores):
    top = jnp.max(scores, axis=-1, keepdims=True)
    exponent = jnp.exp(scores - top)
    return exponent * (1.0 / jnp.sum(exponent, axis=-1, keepdims=True))


def spatial_tiles(c, body):
    @pl.loop(0, c.width // LANES, unroll=2)
    def _(pair):
        cols = [pl.ds(pl.multiple_of(i * c.width + pair * LANES, LANES), LANES) for i in range(3)]
        for f in range(c.frames):
            body(slice(f * c.patches, (f + 1) * c.patches), cols)


def spatial_merge(c, r):
    def body(rows, cols):
        q, k, v = (r.packed[rows, cols[i]] for i in range(3))
        shares = softmax_rows(mm(halves(q), k, NT) * c.scaling).astype(bf16)
        side = jnp.concatenate([shares[: c.patches], shares[c.patches :]], axis=1)
        r.merged[rows, cols[0]] = mm(side, halves(v)).astype(bf16)

    spatial_tiles(c, body)


def spatial_back(c, r):
    def body(rows, cols):
        q, k, v = (r.packed[rows, cols[i]] for i in range(3))
        q2, k2 = halves(q), halves(k)
        d2 = halves(r.grad_merged[rows, cols[0]])
        soft = softmax_rows(mm(q2, k, NT) * c.scaling)
        grad_shares = mm(d2, v, NT)
        inner = jnp.sum(soft * grad_shares, axis=-1, keepdims=True)
        grad_scores = (soft * (grad_shares - inner)).astype(bf16)
        side = jnp.concatenate([grad_scores[: c.patches], grad_scores[c.patches :]], axis=1)
        r.grad_packed[rows, cols[0]] = (mm(side, k2) * c.scaling).astype(bf16)
        r.grad_packed[rows, cols[1]] = (mm(grad_scores, q2, TN) * c.scaling).astype(bf16)
        r.grad_packed[rows, cols[2]] = mm(soft.astype(bf16), d2, TN).astype(bf16)

    spatial_tiles(c, body)


def fill_heads(c, r):
    lane = lax.broadcasted_iota(jnp.int32, (c.width, LANES), 0) // HEAD_DIM
    col = lax.broadcasted_iota(jnp.int32, (c.width, LANES), 1)
    r.heads_in[...] = jnp.where(lane == col, 1.0, 0.0).astype(bf16)
    col = lax.broadcasted_iota(jnp.int32, (LANES, c.width), 0)
    lane = lax.broadcasted_iota(jnp.int32, (LANES, c.width), 1) // HEAD_DIM
    r.heads_out[...] = jnp.where(lane == col, 1.0, 0.0).astype(bf16)


def head_sums(r, product):
    high = product.astype(bf16)
    low = (product - high.astype(f32)).astype(bf16)
    return mm(high, r.heads_in[...]) + mm(low, r.heads_in[...])


def frame_pairs(c):
    return [(f, g) for f in range(c.frames) for g in range(c.frames)]


def temporal_parts(c, r, ref, rows, part):
    return [
        ref[pl.ds(f * c.patches + rows, TILE), part * c.width : (part + 1) * c.width].astype(f32)
        for f in range(c.frames)
    ]


def temporal_soft(c, r, queries, keys):
    product = jnp.concatenate([queries[f] * keys[g] for f, g in frame_pairs(c)], axis=0)
    scores = head_sums(r, product) * c.scaling
    soft = []
    for f in range(c.frames):
        row = [scores[(f * c.frames + g) * TILE : (f * c.frames + g + 1) * TILE] for g in range(c.frames)]
        top = row[0]
        for entry in row[1:]:
            top = jnp.maximum(top, entry)
        exponent = [jnp.exp(entry - top) for entry in row]
        total = exponent[0]
        for entry in exponent[1:]:
            total = total + entry
        soft += [entry * (1.0 / total) for entry in exponent]
    return soft


def spread(r, columns):
    wide = mm(jnp.concatenate([v.astype(bf16) for v in columns], axis=0), r.heads_out[...])
    return [wide[i * TILE : (i + 1) * TILE] for i in range(len(columns))]


def temporal_merge(c, r):
    def body(rows):
        queries, keys, values = (temporal_parts(c, r, r.packed, rows, i) for i in range(3))
        shares = spread(r, temporal_soft(c, r, queries, keys))
        for f in range(c.frames):
            total = shares[f * c.frames] * values[0]
            for g in range(1, c.frames):
                total = total + shares[f * c.frames + g] * values[g]
            at = f * c.patches + rows
            r.merged[pl.ds(at, TILE), :] = total.astype(bf16)

    tiles(c.patches, body)


def temporal_back(c, r):
    n = c.frames

    def body(rows):
        queries, keys, values = (temporal_parts(c, r, r.packed, rows, i) for i in range(3))
        grads = temporal_parts(c, r, r.grad_merged, rows, 0)
        soft = temporal_soft(c, r, queries, keys)
        product = jnp.concatenate([grads[f] * values[g] for f, g in frame_pairs(c)], axis=0)
        wide = head_sums(r, product)
        grad_shares = [wide[i * TILE : (i + 1) * TILE] for i in range(n * n)]
        grad_scores = []
        for f in range(n):
            inner = soft[f * n] * grad_shares[f * n]
            for g in range(1, n):
                inner = inner + soft[f * n + g] * grad_shares[f * n + g]
            grad_scores += [
                soft[f * n + g] * (grad_shares[f * n + g] - inner) for g in range(n)
            ]
        shares = spread(r, soft)
        scores = spread(r, grad_scores)

        def put(frame, part, value):
            at = frame * c.patches + rows
            r.grad_packed[pl.ds(at, TILE), part * c.width : (part + 1) * c.width] = value.astype(bf16)

        for f in range(n):
            put(f, 0, sum(scores[f * n + g] * keys[g] for g in range(n)) * c.scaling)
            put(f, 1, sum(scores[g * n + f] * queries[g] for g in range(n)) * c.scaling)
            put(f, 2, sum(shares[g * n + f] * grads[g] for g in range(n)))

    tiles(c.patches, body)


def forward_b(c, r, wait):
    wait(1, 0)
    r.branch[...] = mm(r.merged[...], r.wp[...].reshape(c.width, c.width))

    def body(rows):
        given = is_given(r, rows)
        middle = r.x[rows, :].astype(f32) + pick(c, r, 2, given) * r.branch[rows, :]
        r.middle[rows, :] = middle
        normed, _ = ln(middle)
        r.mixed_b[rows, :] = (normed * (1.0 + pick(c, r, 4, given)) + pick(c, r, 3, given)).astype(
            bf16
        )

    by_rows(c.rows, body)


GELU_A = math.sqrt(2.0 / math.pi)
GELU_B = 0.044715


def forward_mlp(c, r, wait):
    @pl.loop(0, c.ratio)
    def _(j):
        wait(2, j)
        cols = columns(c, j)
        r.hidden[:, cols] = mm(r.mixed_b[...], square(c, r.wu, j))

        def body(rows):
            h = r.hidden[rows, cols]
            bent = jnp.tanh(GELU_A * (h + GELU_B * (h * h * h)))
            r.active[rows, cols] = (0.5 * h * (1.0 + bent)).astype(bf16)

        by_rows(c.rows, body)

    for j in range(c.ratio):
        wait(3, j)
    r.out_branch[...] = mm(r.active[...], r.wd[...].reshape(c.hidden, c.width))


def forward_end(c, r):
    def body(rows):
        given = is_given(r, rows)
        result = r.middle[rows, :] + pick(c, r, 5, given) * r.out_branch[rows, :]
        r.acts[rows, :] = result
        if N.send in r:
            r.send[rows, :] = result.astype(bf16)

    by_rows(c.rows, body)


def add_sums(c, r, index, given, value):
    cols = slice(index * c.width, (index + 1) * c.width)
    mine = jnp.where(given, value, 0.0)
    rest = jnp.where(given, 0.0, value)
    shape = (value.shape[0] // 8, 8, c.width)
    r.sums[0, :, cols] += jnp.sum(mine.reshape(shape), axis=0)
    r.sums[1, :, cols] += jnp.sum(rest.reshape(shape), axis=0)


def backward_mlp(c, r, wait, gelu_again, put):
    def start(rows):
        given = is_given(r, rows)
        grad = r.grad[rows, :].astype(f32)
        r.grad_out_b[rows, :] = (pick(c, r, 5, given) * grad).astype(bf16)
        add_sums(c, r, 5, given, grad * r.out_branch[rows, :])

    by_rows(c.rows, start)
    put(N.grad_out_b)

    @pl.loop(0, c.ratio)
    def _(j):
        wait(3, j)
        cols = columns(c, j)
        r.temp[...] = mm(r.grad_out_b[...], down_block(c, r, j), NT)

        def body(rows):
            h = r.hidden[rows, cols]
            square_h = h * h
            bent = jnp.tanh(GELU_A * (h + GELU_B * (square_h * h)))
            slope = 0.5 * (1.0 + bent) + 0.5 * h * (1.0 - bent * bent) * (
                GELU_A * (1.0 + 3.0 * GELU_B * square_h)
            )
            r.grad_hidden[rows, cols] = (r.temp[rows, :] * slope).astype(bf16)
            if gelu_again:
                r.active[rows, cols] = (0.5 * h * (1.0 + bent)).astype(bf16)

        by_rows(c.rows, body)

    r.temp[...] = jnp.zeros_like(r.temp)

    @pl.loop(0, c.ratio)
    def _(j):
        wait(2, j)
        r.temp[...] += mm(r.grad_hidden[:, columns(c, j)], square(c, r.wu, j), NT)


def backward_mid(c, r, wait, mix_again):
    def body(rows):
        given = is_given(r, rows)
        normed, inv = ln(r.middle[rows, :])
        scale = 1.0 + pick(c, r, 4, given)
        if mix_again:
            r.mixed_b[rows, :] = (normed * scale + pick(c, r, 3, given)).astype(bf16)
        grad_mixed = r.temp[rows, :]
        middle = r.grad[rows, :].astype(f32) + ln_back(normed, inv, grad_mixed * scale)
        r.grad_middle[rows, :] = middle
        r.grad_branch[rows, :] = (pick(c, r, 2, given) * middle).astype(bf16)
        add_sums(c, r, 3, given, grad_mixed)
        add_sums(c, r, 4, given, grad_mixed * normed)
        add_sums(c, r, 2, given, middle * r.branch[rows, :])

    by_rows(c.rows, body)
    wait(1, 0)
    r.grad_merged[...] = mm(
        r.grad_branch[...], r.wp[...].reshape(c.width, c.width), NT
    ).astype(bf16)


def backward_end(c, r, wait, mix_again):
    r.temp[...] = jnp.zeros_like(r.temp)

    @pl.loop(0, 3)
    def _(j):
        wait(0, j)
        r.temp[...] += mm(r.grad_packed[:, columns(c, j)], square(c, r.wq, j), NT)

    def body(rows):
        given = is_given(r, rows)
        normed, inv = ln(r.x[rows, :].astype(f32))
        scale = 1.0 + pick(c, r, 1, given)
        if mix_again:
            r.mixed_a[rows, :] = (normed * scale + pick(c, r, 0, given)).astype(bf16)
        grad_mixed = r.temp[rows, :]
        result = r.grad_middle[rows, :] + ln_back(normed, inv, grad_mixed * scale)
        r.grad_in[rows, :] = result
        if N.send in r:
            r.send[rows, :] = result.astype(bf16)
        add_sums(c, r, 0, given, grad_mixed)
        add_sums(c, r, 1, given, grad_mixed * normed)

    by_rows(c.rows, body)
    r.grad_mod[...] = jnp.sum(r.sums[...], axis=1)


def sizes(c):
    wide, rows = c.width, c.rows
    return dict(
        x=((rows, wide), bf16),
        mod=((2, 6 * wide), f32),
        given=((rows, LANES), f32),
        mixed_a=((rows, wide), bf16),
        packed=((rows, 3 * wide), bf16),
        merged=((rows, wide), bf16),
        branch=((rows, wide), f32),
        middle=((rows, wide), f32),
        mixed_b=((rows, wide), bf16),
        hidden=((rows, c.hidden), f32),
        active=((rows, c.hidden), bf16),
        out_branch=((rows, wide), f32),
        acts=((rows, wide), f32),
        send=((rows, wide), bf16),
        grad=((rows, wide), bf16),
        grad_out_b=((rows, wide), bf16),
        grad_hidden=((rows, c.hidden), bf16),
        temp=((rows, wide), f32),
        grad_middle=((rows, wide), f32),
        grad_branch=((rows, wide), bf16),
        grad_merged=((rows, wide), bf16),
        grad_packed=((rows, 3 * wide), bf16),
        grad_in=((rows, wide), f32),
        sums=((2, 8, 6 * wide), f32),
        grad_mod=((2, 6 * wide), f32),
        heads_in=((wide, LANES), bf16),
        heads_out=((LANES, wide), bf16),
    )


KEPT = (N.packed, N.merged, N.branch, N.middle, N.hidden, N.out_branch)
TERMS = (
    N.mixed_a,
    N.grad_packed,
    N.merged,
    N.grad_branch,
    N.mixed_b,
    N.grad_hidden,
    N.active,
    N.grad_out_b,
)


class Traffic:
    def __init__(self, sems):
        self.sems, self.used, self.pending = sems, 0, {}

    def start(self, name, src, dst):
        copy = pltpu.make_async_copy(src, dst, self.sems.at[self.used])
        self.used += 1
        copy.start()
        self.pending[name] = copy

    def wait(self, name):
        if name in self.pending:
            self.pending.pop(name).wait()

    def drain(self):
        for name in list(self.pending):
            self.wait(name)


def wait_weight(c, w, r, part, j):
    weight_copy(c, w, r, part, j).wait()


def run_forward(c, r, t, temporal, put, weight_wait):
    t.wait(N.mod)
    t.wait(N.x)
    forward_a(c, r)
    put(N.mixed_a)
    forward_qkv(c, r, weight_wait)
    put(N.packed)
    if temporal:
        fill_heads(c, r)
        temporal_merge(c, r)
    else:
        spatial_merge(c, r)
    put(N.merged)
    forward_b(c, r, weight_wait)
    put(N.branch)
    put(N.middle)
    put(N.mixed_b)
    forward_mlp(c, r, weight_wait)
    put(N.hidden)
    put(N.active)
    put(N.out_branch)
    forward_end(c, r)
    put(N.acts)
    put(N.send)


def spatial_forward_kernel(c, micro, names, refs):
    h = Refs(names_hbm(names, refs))
    r = h.vmem

    @pl.when(h.ctl[0] == 0)
    def _():
        t = Traffic(r.sems)
        t.start(N.x, h.x.at[micro], r.x)
        t.start(N.mod, h.mod.at[micro], r.mod)
        start_weights(c, h.w, r, (0, 1, 2, 3))
        fill_given(c, h.ctl, r)

        def put(name):
            if name in KEPT or name == N.send:
                t.start(name, r[name], h[name])
            elif name == N.acts:
                t.start(name, r.acts, h.acts.at[micro])

        run_forward(c, r, t, False, put, partial(wait_weight, c, h.w, r))
        t.drain()


def temporal_kernel(c, micro, names, refs):
    h = Refs(names_hbm(names, refs))
    r = h.vmem

    @pl.when(h.ctl[0] == 1)
    def _():
        t = Traffic(r.sems)
        t.start(N.x, h.x, r.x)
        t.start(N.mod, h.mod.at[micro], r.mod)
        start_weights(c, h.w, r, (0, 1, 2, 3))
        t.start(N.grad, h.cot.at[micro], r.grad)
        fill_given(c, h.ctl, r)
        forward = Refs({k: v for k, v in r.items() if k != N.send})
        put = partial(put_backward, c, micro, h, r, t)
        run_forward(
            c,
            forward,
            t,
            True,
            lambda name: name == N.send or put(name),
            partial(wait_weight, c, h.w, r),
        )
        t.wait(N.grad)
        run_backward(c, r, t, True, put, lambda part, j: None)
        t.drain()


def put_backward(c, micro, h, r, t, name):
    if name == N.send:
        if N.send in h:
            t.start(N.send, r.send, h.send)
    elif name in (N.acts, N.grad_in, N.grad_mod):
        t.start(name, r[name], h[name].at[micro])
    elif name in TERMS:
        t.start(name, r[name], h[name].at[pl.ds(micro * c.rows, c.rows), :])


def run_backward(c, r, t, temporal, put, weight_wait):
    r.sums[...] = jnp.zeros_like(r.sums)
    backward_mlp(c, r, weight_wait, not temporal, put)
    put(N.grad_hidden)
    t.wait(N.middle)
    t.wait(N.branch)
    backward_mid(c, r, weight_wait, not temporal)
    put(N.grad_branch)
    t.wait(N.packed)
    t.wait(N.merged)
    if temporal:
        temporal_back(c, r)
    else:
        put(N.active)
        put(N.mixed_b)
        put(N.merged)
        spatial_back(c, r)
    put(N.grad_packed)
    t.wait(N.x)
    backward_end(c, r, weight_wait, not temporal)
    if not temporal:
        put(N.mixed_a)
    put(N.send)
    put(N.grad_in)
    put(N.grad_mod)


def spatial_backward_kernel(c, micro, names, refs):
    h = Refs(names_hbm(names, refs))
    r = h.vmem

    @pl.when(h.ctl[0] == 0)
    def _():
        t = Traffic(r.sems)
        t.start(N.grad, h.grad, r.grad)
        t.start(N.mod, h.mod.at[micro], r.mod)
        t.start(N.out_branch, h.out_branch, r.out_branch)
        t.start(N.hidden, h.hidden, r.hidden)
        start_weights(c, h.w, r, (3, 2))
        for name in (N.middle, N.branch, N.packed, N.merged):
            t.start(name, h[name + "_kept"] if name in TERMS else h[name], r[name])
        t.start(N.x, h.x.at[micro], r.x)
        start_weights(c, h.w, r, (1, 0))
        fill_given(c, h.ctl, r)
        for name in (N.grad, N.mod, N.out_branch, N.hidden):
            t.wait(name)
        run_backward(
            c, r, t, False, partial(put_backward, c, micro, h, r, t), partial(wait_weight, c, h.w, r)
        )
        t.drain()


def names_hbm(names, refs):
    outer, inner = names
    found = dict(zip(outer, refs[: len(outer)], strict=True))
    found[N.vmem] = Refs(zip(inner, refs[len(outer) :], strict=True))
    return found


def call(c, kernel, micro, operands, news, alias, scratch, flops):
    ins = list(operands)
    outs = list(alias) + list(news)
    shapes = [jax.ShapeDtypeStruct(operands[n].shape, operands[n].dtype) for n in alias]
    shapes += [jax.ShapeDtypeStruct(*news[n]) for n in news]
    table = sizes(c)
    inner = {n: pltpu.VMEM(*table[n]) for n in scratch}
    inner.update(weight_scratch(c))
    inner[N.sems] = pltpu.SemaphoreType.DMA((32,))
    in_names = [n if n not in alias else "_" + n for n in ins]
    names = (in_names + outs, list(inner))
    got = pl.pallas_call(
        lambda *refs: kernel(c, micro, names, refs),
        out_shape=shapes,
        in_specs=[
            pl.BlockSpec(memory_space=pltpu.SMEM if n == N.ctl else pl.ANY) for n in ins
        ],
        out_specs=[pl.BlockSpec(memory_space=pl.ANY)] * len(outs),
        scratch_shapes=list(inner.values()),
        input_output_aliases={ins.index(n): i for i, n in enumerate(alias)},
        compiler_params=pltpu.CompilerParams(vmem_limit_bytes=VMEM_BYTES),
        cost_estimate=pl.CostEstimate(flops=flops, bytes_accessed=20_000_000, transcendentals=0),
    )(*operands.values())
    return dict(zip(outs, got, strict=True))


FIRST = (N.active, N.grad_out_b, N.mixed_a, N.grad_packed)
SECOND = (N.mixed_b, N.grad_hidden, N.merged, N.grad_branch)


def group_rows(c):
    return ((c.ratio + 1) * c.own, (c.ratio + 1) * c.own, 2 * c.own)


def gradients_kernel(c, ring, order, place, *refs):
    made = (0, 2) if order == FIRST else (1,)
    count, outs = len(order), len(made) * (4 if ring else 1)
    held = Refs(zip(order, refs[count + outs : 2 * count + outs], strict=True))
    turned, slots, in_sems, out_sems = refs[2 * count + outs :]
    copies = {
        n: pltpu.make_async_copy(refs[i], held[n], in_sems.at[i]) for i, n in enumerate(order)
    }
    for copy in copies.values():
        copy.start()
    own, step, line = c.own, c.blocks // c.ratio, c.blocks // 4
    each = outs // len(made)
    out = {g: refs[count + i * each : count + (i + 1) * each] for i, g in enumerate(made)}

    def puts(slot, group, j, tall=False):
        ref = slots.at[slot]
        if tall:
            ref = ref.reshape(step, c.ratio * own, c.width)
        if not ring:
            rows = pl.ds(j * step, step) if tall else pl.ds(0, c.blocks)
            part = pl.ds(0, c.ratio * own) if tall else pl.ds(j * own, own)
            yield pltpu.make_async_copy(ref, out[group][0].at[rows, part, :], out_sems.at[slot, 0])
            return
        if tall:
            ref = ref.reshape(2, 2, c.ratio * own, c.width)
        else:
            ref = ref.reshape(line, 2, 2, own, c.width)
        for i, (x, core) in enumerate(((0, 0), (1, 0), (0, 1), (1, 1))):
            x, core = (place[0] + x) % 2, (place[1] + core) % 2
            if tall:
                src, dst = ref.at[x, core], out[group][i].at[j, pl.ds(0, c.ratio * own), :]
            else:
                src, dst = ref.at[:, x, core], out[group][i].at[:, pl.ds(j * own, own), :]
            yield pltpu.make_async_copy(src, dst, out_sems.at[slot, i])

    def product(left, right, dims, *target):
        slots[target[0]] = mm(left, right, dims).astype(bf16).reshape(slots.shape[1:])
        for copy in puts(*target):
            copy.start()

    v = c.ratio
    if order == FIRST:
        copies[N.active].wait()
        copies[N.grad_out_b].wait()

        @pl.loop(0, c.ratio)
        def _(j):
            product(held.active[:, columns(c, j)], held.grad_out_b[...], TN, j, 0, j, True)

        copies[N.mixed_a].wait()
        turned[...] = held.mixed_a[...].T
        copies[N.grad_packed].wait()
        product(turned[...], held.grad_packed[:, 2 * c.width :], NN, v, 0, c.ratio)

        @pl.loop(0, 2)
        def _(j):
            product(turned[...], held.grad_packed[:, columns(c, j)], NN, v + 1 + j, 2, j)

        targets = [(j, 0, j, True) for j in range(c.ratio)] + [(v, 0, c.ratio)]
        targets += [(v + 1 + j, 2, j) for j in range(2)]
    else:
        copies[N.mixed_b].wait()
        turned[...] = held.mixed_b[...].T
        copies[N.grad_hidden].wait()

        @pl.loop(0, c.ratio)
        def _(j):
            product(turned[...], held.grad_hidden[:, columns(c, j)], NN, j, 1, j)

        copies[N.merged].wait()
        copies[N.grad_branch].wait()
        product(held.merged[...], held.grad_branch[...], TN, v, 1, c.ratio)
        targets = [(j, 1, j) for j in range(c.ratio + 1)]
    for target in targets:
        for copy in puts(*target):
            copy.wait()


def weight_gradients(c, ring, order, place, terms):
    made = (0, 2) if order == FIRST else (1,)
    jobs = c.ratio + (3 if order == FIRST else 1)
    shapes = [terms[n].shape for n in order]
    line, each = (c.blocks // 4, 4) if ring else (c.blocks, 1)
    out = []
    for group in made:
        out += [jax.ShapeDtypeStruct((line, group_rows(c)[group], c.width), bf16)] * each
    got = pl.pallas_call(
        partial(gradients_kernel, c, ring, order),
        out_shape=out,
        in_specs=[pl.BlockSpec(memory_space=pltpu.SMEM)]
        + [pl.BlockSpec(memory_space=pl.ANY)] * len(order),
        out_specs=[pl.BlockSpec(memory_space=pl.ANY)] * len(out),
        scratch_shapes=[pltpu.VMEM(s, bf16) for s in shapes]
        + [
            pltpu.VMEM((c.width, shapes[0][0]), bf16),
            pltpu.VMEM((jobs, c.blocks, c.own, c.width), bf16),
            pltpu.SemaphoreType.DMA((len(order),)),
            pltpu.SemaphoreType.DMA((jobs, 4)),
        ],
        compiler_params=pltpu.CompilerParams(vmem_limit_bytes=VMEM_BYTES),
        cost_estimate=pl.CostEstimate(
            flops=2 * shapes[0][0] * c.width * c.width * jobs,
            bytes_accessed=12_000_000,
            transcendentals=0,
        ),
    )(place, *[terms[n] for n in order])
    return [got[i * each : (i + 1) * each] for i in range(len(made))]


def add(*parts):
    total = parts[0].astype(f32)
    for part in parts[1:]:
        total = total + part.astype(f32)
    return total


LINE = (3, 2, 1)


def line_terms(terms, z):
    return [lax.dynamic_index_in_dim(terms, z ^ k, 0, keepdims=False) for k in (0,) + LINE]


def line_swap(terms):
    return terms[:1] + [swap(term, 4 * k) for term, k in zip(terms[1:], LINE)]


def ring_sums(first, second, z, small):
    meet = lax.optimization_barrier
    (near0, far0, *core0), (near2, far2, *core2) = first
    far0 = add(far0, swap(core0[1], 1)).astype(bf16)
    pair = [add(near2, swap(core2[0], 1)).astype(bf16), add(far2, swap(core2[1], 1)).astype(bf16)]
    terms2 = line_terms(jnp.stack(pair, axis=1), z)

    far0, terms2, small = meet((far0, terms2, small))
    near1, far1, *core1 = second(far0)
    far0, terms2 = swap(far0, 2), line_swap(terms2)
    near0 = add(near0, swap(core0[0], 1)).astype(bf16)
    far1 = add(far1, swap(core1[1], 1)).astype(bf16)
    near1 = add(near1, swap(core1[0], 1)).astype(bf16)
    small = gather_step(gather_step(small, 8), 4)

    far0, terms2, near0, far1, near1, small = meet((far0, terms2, near0, far1, near1, small))
    terms0 = line_swap(line_terms(add(near0, far0).astype(bf16), z))
    far1 = swap(far1, 2)
    sum2 = add(*terms2)
    other2 = sum2[1].astype(bf16)
    small = gather_step(gather_step(small, 2), 1)

    terms0, far1, other2, small = meet((terms0, far1, other2, small))
    terms1 = line_swap(line_terms(add(near1, far1).astype(bf16), z))
    sum2 = sum2[0] + swap(other2, 2).astype(f32)
    return add(*terms0), add(*terms1), sum2, small


def swap(block, distance):
    count = lax.axis_size(DP)
    return lax.ppermute(block, DP, [(i, i ^ distance) for i in range(count)])


def gather_small(block):
    count = lax.axis_size(DP)
    if count & (count - 1):
        return lax.all_gather(block, DP, axis=0, tiled=False)
    held, distance = block[None], count // 2
    while distance:
        held = gather_step(held, distance)
        distance //= 2
    return held


def gather_step(held, distance):
    other = swap(held, distance)
    lower = (lax.axis_index(DP) & distance) == 0
    pair = [jnp.where(lower, held, other), jnp.where(lower, other, held)]
    return jnp.stack(pair, axis=1).reshape((-1,) + held.shape[1:])


def scatter_small(blocks):
    count = lax.axis_size(DP)
    if count & (count - 1):
        return lax.psum_scatter(blocks, DP, scatter_dimension=0, tiled=False)
    mine = lax.axis_index(DP)
    distance = 1
    while distance < count:
        low, high = blocks[0::2], blocks[1::2]
        upper = (mine & distance) != 0
        other = swap(jnp.where(upper, low, high), distance)
        blocks = jnp.where(upper, high, low) + other
        distance *= 2
    return blocks[0]


def embed_columns(steps, index, width):
    half = width // 2
    place = (index % half).astype(f32)
    frequency = jnp.exp(-math.log(10000.0) * place / half)
    angles = steps.astype(f32)[:, None] * frequency[None, :]
    wave = jnp.where((index < half)[None, :], jnp.cos(angles), jnp.sin(angles))
    return jax.nn.silu(wave).astype(bf16)


def by_blocks(w, own, width):
    parts = w.shape[1] // width
    return w.reshape(own, parts, width).transpose(1, 0, 2).reshape(parts * own, width)


def from_blocks(blocks, own, width):
    parts = blocks.shape[0] // own
    return blocks.reshape(parts, own, width).transpose(1, 0, 2).reshape(own, parts * width)


def local(tokens, cotangent, boxes, timesteps, w_ada, w_qkv, w_proj, w_up, w_down):
    section = lax.axis_index(SECTION)
    group = lax.axis_size(DP)
    micro_count, _, frames, patches, width = tokens.shape
    hidden = w_up.shape[2]
    rows = frames * patches
    own = width // group
    ratio = hidden // width
    direct = own % 16 == 0 and group % ratio == 0
    ring = direct and group == 16 and ratio == 4
    c = Cfg(frames, patches, width, hidden, group if direct else ratio)

    shard = jnp.concatenate(
        [
            by_blocks(w_qkv[0].astype(bf16), own, width),
            w_proj[0].astype(bf16),
            by_blocks(w_up[0].astype(bf16), own, width),
            w_down[0].astype(bf16),
        ],
        axis=0,
    )
    weights = lax.all_gather(shard, DP, axis=0, tiled=False)
    squares = 4 + ratio
    if not direct:
        weights = jnp.concatenate(
            [
                weights[:, i * own : (i + 1) * own].reshape(c.blocks, c.own, width)
                for i in range(squares)
            ]
            + [weights[:, squares * own :].reshape(c.blocks, ratio * c.own, width)],
            axis=1,
        )

    start = lax.axis_index(DP) * own
    index = start + jnp.arange(own, dtype=jnp.int32)
    steps = gather_small(timesteps.reshape(micro_count))
    steps = jnp.concatenate([jnp.zeros((group, 1), steps.dtype), steps], axis=1)
    embed = embed_columns(steps.reshape(-1), index, width)
    modulation = jnp.dot(embed, w_ada[0].astype(bf16), preferred_element_type=f32)
    modulation = scatter_small(modulation.reshape(group, 1 + micro_count, 6 * width))
    modulation = jnp.stack(
        [jnp.stack([modulation[0], modulation[1 + m]]) for m in range(micro_count)]
    )
    ctl = [
        jnp.concatenate([section.astype(jnp.int32)[None], boxes[m].reshape(-1)])
        for m in range(micro_count)
    ]

    tokens = tokens.reshape(micro_count, rows, width)
    cotangent = cotangent.reshape(micro_count, rows, width)
    whole = ((micro_count, rows, width), f32)
    one = ((rows, width), bf16)
    flops = 2 * rows * width * width * (4 + 2 * ratio)
    table = sizes(c)

    forward_names = [
        N.x, N.mod, N.given, N.mixed_a, N.packed, N.merged, N.branch, N.middle, N.mixed_b,
        N.hidden, N.active, N.out_branch, N.acts, N.send,
    ]
    back_names = [
        N.grad, N.grad_out_b, N.grad_hidden, N.temp, N.grad_middle, N.grad_branch, N.grad_merged,
        N.grad_packed, N.grad_in, N.sums, N.grad_mod,
    ]
    kept, received = [], []
    acts = None
    for m in range(micro_count):
        operands = dict(ctl=ctl[m], x=tokens, mod=modulation, w=weights)
        news = dict(send=one, **{n: table[n] for n in KEPT})
        if acts is None:
            news[N.acts] = whole
        else:
            operands[N.acts] = acts
        alias = [N.acts] if acts is not None else []
        got = call(c, spatial_forward_kernel, m, operands, news, alias, forward_names, flops)
        acts = got[N.acts]
        kept.append(got)
        received.append(lax.ppermute(got[N.send], SECTION, [(0, 1)]))

    shared = None
    grads = []
    for m in range(micro_count):
        operands = dict(
            ctl=ctl[m], x=received[m], mod=modulation, w=weights, cot=cotangent, acts=acts
        )
        news = dict(send=one)
        alias = [N.acts]
        if shared is None:
            news[N.grad_in] = whole
            news[N.grad_mod] = ((micro_count, 2, 6 * width), f32)
            for n in TERMS:
                news[n] = ((micro_count * rows, table[n][0][1]), bf16)
        else:
            operands.update(shared)
            alias += list(shared)
        names = forward_names + back_names + [N.heads_in, N.heads_out]
        got = call(c, temporal_kernel, m, operands, news, alias, names, 3 * flops)
        acts = got[N.acts]
        shared = {n: got[n] for n in (N.grad_in, N.grad_mod) + TERMS}
        grads.append(lax.ppermute(got[N.send], SECTION, [(1, 0)]))

    for m in range(micro_count):
        operands = dict(ctl=ctl[m], x=tokens, mod=modulation, w=weights, grad=grads[m])
        for n in KEPT:
            operands[n + "_kept" if n in TERMS else n] = kept[m][n]
        operands.update(shared)
        names = [n for n in forward_names if n not in (N.acts, N.send)] + back_names
        shared = call(
            c, spatial_backward_kernel, m, operands, {}, list(shared), names, 2 * flops
        )

    dp_index = lax.axis_index(DP)
    place = jnp.stack([dp_index // 2 % 2, dp_index % 2]).astype(jnp.int32)
    first = weight_gradients(c, ring, FIRST, place, shared)

    def second(after):
        place_now, _ = lax.optimization_barrier((place, after))
        return weight_gradients(c, ring, SECOND, place_now, shared)[0]

    sums = shared[N.grad_mod]
    sums = jnp.concatenate([jnp.sum(sums[:, 0], axis=0, keepdims=True), sums[:, 1]]).astype(bf16)
    if ring:
        *totals, sums = ring_sums(first, second, dp_index // 4, sums[None])
    else:
        sums = gather_small(sums)
        groups = first[0], second(place), first[1]
        joined = [parts[0] for parts in groups]
        if not direct:
            tall = ratio * c.own
            joined = [
                jnp.concatenate(
                    [
                        part[:, i * c.own : (i + 1) * c.own].reshape(group, own, width)
                        for i in range(part.shape[1] // c.own)
                    ],
                    axis=1,
                )
                for part in (joined[0][:, tall:], joined[1], joined[2])
            ]
            tall = groups[0][0][:, :tall].reshape(group, ratio * own, width)
            joined[0] = jnp.concatenate([tall, joined[0]], axis=1)
        total = lax.psum_scatter(
            jnp.concatenate(joined, axis=1), DP, scatter_dimension=0, tiled=False
        ).astype(f32)
        first = (ratio + 1) * own
        totals = total[:first], total[first : 2 * first], total[2 * first :]
    tall = ratio * own
    down, up, proj = totals[0][:tall], totals[1][:tall], totals[1][tall:]
    qkv = jnp.concatenate([totals[2], totals[0][tall:]])
    grad_qkv = from_blocks(qkv, own, width)
    grad_proj = proj
    grad_up = from_blocks(up, own, width)
    grad_down = down

    sums = sums.reshape(group * (1 + micro_count), 6 * width)
    grad_ada = lax.dot_general(embed, sums, TN, preferred_element_type=f32)

    out_shape = (1, micro_count, 1, frames, patches, width)
    return (
        acts.reshape(out_shape),
        shared[N.grad_in].reshape(out_shape),
        grad_ada[None],
        grad_qkv[None],
        grad_proj[None],
        grad_up[None],
        grad_down[None],
    )


def solution(mesh):
    placed = (
        P(None, DP, None, None, None),
        P(None, DP, None, None, None),
        P(None, DP, None, None),
        P(None, DP),
        P(SECTION, DP, None),
        P(SECTION, DP, None),
        P(SECTION, DP, None),
        P(SECTION, DP, None),
        P(SECTION, DP, None),
    )
    return jax.shard_map(
        local,
        mesh=mesh,
        in_specs=placed,
        out_specs=(
            P(SECTION, None, DP, None, None, None),
            P(SECTION, None, DP, None, None, None),
            P(SECTION, DP, None),
            P(SECTION, DP, None),
            P(SECTION, DP, None),
            P(SECTION, DP, None),
            P(SECTION, DP, None),
        ),
        check_vma=False,
    )
```

```python
from functools import partial
import math

import jax
import jax.numpy as jnp
from jax import lax
from jax.experimental import pallas as pl
from jax.experimental.pallas import tpu as pltpu
from jax.sharding import PartitionSpec as P

HEAD_DIM = 64
GW = 16
LANES = 128
TILE = 64
STEP = 256
EPS = 1e-06
SPARE_BYTES = 10 * 1024 * 1024
f32 = jnp.float32
bf16 = jnp.bfloat16
NN = (((1,), (0,)), ((), ()))
NT = (((1,), (1,)), ((), ()))
TN = (((0,), (0,)), ((), ()))


def mm(a, b, dims=NN):
    return lax.dot_general(a, b, dims, preferred_element_type=f32)


def ln(v):
    centred = v - jnp.mean(v, axis=-1, keepdims=True)
    inv = lax.rsqrt(jnp.mean(centred * centred, axis=-1, keepdims=True) + EPS)
    return centred * inv, inv


def ln_back(normed, inv, grad):
    return inv * (
        grad
        - jnp.mean(grad, axis=-1, keepdims=True)
        - normed * jnp.mean(grad * normed, axis=-1, keepdims=True)
    )


def by_rows(count, body):
    @pl.loop(0, count // STEP)
    def _(i):
        body(pl.ds(pl.multiple_of(i * STEP, STEP), STEP))


def tiles(count, body):
    @pl.loop(0, count // TILE)
    def _(i):
        body(pl.multiple_of(i * TILE, TILE))


def columns(c, j):
    return pl.ds(pl.multiple_of(j * c.width, c.width), c.width)


class Refs(dict):
    __getattr__ = dict.__getitem__


class Names:
    def __getattr__(self, name):
        return name


N = Names()
DP, SECTION = "dp", "section"


class Cfg:
    def __init__(self, frames, patches, width, hidden, blocks):
        self.frames, self.patches, self.width, self.hidden = frames, patches, width, hidden
        self.rows = frames * patches
        self.ratio = hidden // width
        self.blocks = blocks
        self.own = width // blocks
        self.scaling = HEAD_DIM ** (-0.5)


def weight_copies(c, src, dst, sems):
    cuts = (0, 4 * c.own, (4 + c.ratio) * c.own, (4 + 2 * c.ratio) * c.own)
    parts = [pl.ds(a, b - a) for a, b in zip(cuts, cuts[1:])]
    return [
        pltpu.make_async_copy(src.at[:, part, :], dst.at[:, part, :], sems.at[i])
        for i, part in enumerate(parts)
    ]


def square(c, r, j):
    rows = pl.ds(pl.multiple_of(j * c.own, c.own), c.own)
    return r.w[:, rows, :].reshape(c.width, c.width)


def down_block(c, r, j):
    step = c.blocks // c.ratio
    block = r.w[pl.ds(j * step, step), (4 + c.ratio) * c.own :, :]
    return block.reshape(c.width, c.width)


def down_whole(c, r):
    return r.w[:, (4 + c.ratio) * c.own :, :].reshape(c.hidden, c.width)


def fill_given(c, ctl, r):
    patch = lax.broadcasted_iota(jnp.int32, (c.patches, LANES), 0)
    row, col = patch // GW, patch % GW
    for f in range(c.frames):
        top, bottom, left, right = (ctl[1 + 4 * f + i] for i in range(4))
        inside = (row >= top) & (row < bottom) & (col >= left) & (col < right)
        r.given[f * c.patches : (f + 1) * c.patches, :] = jnp.where(inside, 1.0, 0.0)


def pick(c, r, index, given):
    where = slice(index * c.width, (index + 1) * c.width)
    return jnp.where(given, r.mod[0:1, where], r.mod[1:2, where])


def is_given(r, rows):
    return r.given[rows, 0:1] > 0.5


def forward_a(c, r):
    def body(rows):
        given = is_given(r, rows)
        normed, _ = ln(r.x[rows, :].astype(f32))
        r.mixed_a[rows, :] = (normed * (1.0 + pick(c, r, 1, given)) + pick(c, r, 0, given)).astype(
            bf16
        )

    by_rows(c.rows, body)


def forward_qkv(c, r):
    @pl.loop(0, 3)
    def _(j):
        r.packed[:, columns(c, j)] = mm(r.mixed_a[...], square(c, r, j)).astype(bf16)


def halves(pair):
    first = lax.broadcasted_iota(jnp.int32, pair.shape, 1) < HEAD_DIM
    zero = jnp.zeros_like(pair)
    return jnp.concatenate([jnp.where(first, pair, zero), jnp.where(first, zero, pair)], axis=0)


def softmax_rows(scores):
    top = jnp.max(scores, axis=-1, keepdims=True)
    exponent = jnp.exp(scores - top)
    return exponent * (1.0 / jnp.sum(exponent, axis=-1, keepdims=True))


def spatial_tiles(c, body):
    @pl.loop(0, c.width // LANES, unroll=2)
    def _(pair):
        cols = [pl.ds(pl.multiple_of(i * c.width + pair * LANES, LANES), LANES) for i in range(3)]
        for f in range(c.frames):
            body(slice(f * c.patches, (f + 1) * c.patches), cols)


def spatial_merge(c, r):
    def body(rows, cols):
        q, k, v = (r.packed[rows, cols[i]] for i in range(3))
        shares = softmax_rows(mm(halves(q), k, NT) * c.scaling).astype(bf16)
        side = jnp.concatenate([shares[: c.patches], shares[c.patches :]], axis=1)
        r.merged[rows, cols[0]] = mm(side, halves(v)).astype(bf16)

    spatial_tiles(c, body)


def spatial_back(c, r):
    def body(rows, cols):
        q, k, v = (r.packed[rows, cols[i]] for i in range(3))
        q2, k2 = halves(q), halves(k)
        d2 = halves(r.grad_merged[rows, cols[0]])
        soft = softmax_rows(mm(q2, k, NT) * c.scaling)
        grad_shares = mm(d2, v, NT)
        inner = jnp.sum(soft * grad_shares, axis=-1, keepdims=True)
        grad_scores = (soft * (grad_shares - inner)).astype(bf16)
        side = jnp.concatenate([grad_scores[: c.patches], grad_scores[c.patches :]], axis=1)
        r.grad_packed[rows, cols[0]] = (mm(side, k2) * c.scaling).astype(bf16)
        r.grad_packed[rows, cols[1]] = (mm(grad_scores, q2, TN) * c.scaling).astype(bf16)
        r.grad_packed[rows, cols[2]] = mm(soft.astype(bf16), d2, TN).astype(bf16)

    spatial_tiles(c, body)


def fill_heads(c, r):
    lane = lax.broadcasted_iota(jnp.int32, (c.width, LANES), 0) // HEAD_DIM
    col = lax.broadcasted_iota(jnp.int32, (c.width, LANES), 1)
    r.heads_in[...] = jnp.where(lane == col, 1.0, 0.0).astype(bf16)
    col = lax.broadcasted_iota(jnp.int32, (LANES, c.width), 0)
    lane = lax.broadcasted_iota(jnp.int32, (LANES, c.width), 1) // HEAD_DIM
    r.heads_out[...] = jnp.where(lane == col, 1.0, 0.0).astype(bf16)


def head_sums(r, product):
    high = product.astype(bf16)
    low = (product - high.astype(f32)).astype(bf16)
    return mm(high, r.heads_in[...]) + mm(low, r.heads_in[...])


def frame_pairs(c):
    return [(f, g) for f in range(c.frames) for g in range(c.frames)]


def temporal_parts(c, r, ref, rows, part):
    return [
        ref[pl.ds(f * c.patches + rows, TILE), part * c.width : (part + 1) * c.width].astype(f32)
        for f in range(c.frames)
    ]


def temporal_soft(c, r, queries, keys):
    product = jnp.concatenate([queries[f] * keys[g] for f, g in frame_pairs(c)], axis=0)
    scores = head_sums(r, product) * c.scaling
    soft = []
    for f in range(c.frames):
        row = [scores[(f * c.frames + g) * TILE : (f * c.frames + g + 1) * TILE] for g in range(c.frames)]
        top = row[0]
        for entry in row[1:]:
            top = jnp.maximum(top, entry)
        exponent = [jnp.exp(entry - top) for entry in row]
        total = exponent[0]
        for entry in exponent[1:]:
            total = total + entry
        soft += [entry * (1.0 / total) for entry in exponent]
    return soft


def spread(r, columns):
    wide = mm(jnp.concatenate([v.astype(bf16) for v in columns], axis=0), r.heads_out[...])
    return [wide[i * TILE : (i + 1) * TILE] for i in range(len(columns))]


def temporal_merge(c, r):
    def body(rows):
        queries, keys, values = (temporal_parts(c, r, r.packed, rows, i) for i in range(3))
        shares = spread(r, temporal_soft(c, r, queries, keys))
        for f in range(c.frames):
            total = shares[f * c.frames] * values[0]
            for g in range(1, c.frames):
                total = total + shares[f * c.frames + g] * values[g]
            at = f * c.patches + rows
            r.merged[pl.ds(at, TILE), :] = total.astype(bf16)

    tiles(c.patches, body)


def temporal_back(c, r):
    n = c.frames

    def body(rows):
        queries, keys, values = (temporal_parts(c, r, r.packed, rows, i) for i in range(3))
        grads = temporal_parts(c, r, r.grad_merged, rows, 0)
        soft = temporal_soft(c, r, queries, keys)
        product = jnp.concatenate([grads[f] * values[g] for f, g in frame_pairs(c)], axis=0)
        wide = head_sums(r, product)
        grad_shares = [wide[i * TILE : (i + 1) * TILE] for i in range(n * n)]
        grad_scores = []
        for f in range(n):
            inner = soft[f * n] * grad_shares[f * n]
            for g in range(1, n):
                inner = inner + soft[f * n + g] * grad_shares[f * n + g]
            grad_scores += [
                soft[f * n + g] * (grad_shares[f * n + g] - inner) for g in range(n)
            ]
        shares = spread(r, soft)
        scores = spread(r, grad_scores)

        def put(frame, part, value):
            at = frame * c.patches + rows
            r.grad_packed[pl.ds(at, TILE), part * c.width : (part + 1) * c.width] = value.astype(bf16)

        for f in range(n):
            put(f, 0, sum(scores[f * n + g] * keys[g] for g in range(n)) * c.scaling)
            put(f, 1, sum(scores[g * n + f] * queries[g] for g in range(n)) * c.scaling)
            put(f, 2, sum(shares[g * n + f] * grads[g] for g in range(n)))

    tiles(c.patches, body)


def forward_b(c, r):
    r.branch[...] = mm(r.merged[...], square(c, r, 3))

    def body(rows):
        given = is_given(r, rows)
        middle = r.x[rows, :].astype(f32) + pick(c, r, 2, given) * r.branch[rows, :]
        r.middle[rows, :] = middle
        normed, _ = ln(middle)
        r.mixed_b[rows, :] = (normed * (1.0 + pick(c, r, 4, given)) + pick(c, r, 3, given)).astype(
            bf16
        )

    by_rows(c.rows, body)


GELU_A = math.sqrt(2.0 / math.pi)
GELU_B = 0.044715


def forward_mlp(c, r, weight_wait):
    @pl.loop(0, c.ratio)
    def _(j):
        cols = columns(c, j)
        r.hidden[:, cols] = mm(r.mixed_b[...], square(c, r, 4 + j))

        def body(rows):
            h = r.hidden[rows, cols]
            bent = jnp.tanh(GELU_A * (h + GELU_B * (h * h * h)))
            r.active[rows, cols] = (0.5 * h * (1.0 + bent)).astype(bf16)

        by_rows(c.rows, body)

    weight_wait(2)
    r.out_branch[...] = mm(r.active[...], down_whole(c, r))


def forward_end(c, r):
    def body(rows):
        given = is_given(r, rows)
        result = r.middle[rows, :] + pick(c, r, 5, given) * r.out_branch[rows, :]
        r.acts[rows, :] = result
        if N.send in r:
            r.send[rows, :] = result.astype(bf16)

    by_rows(c.rows, body)


def add_sums(c, r, index, given, value):
    cols = slice(index * c.width, (index + 1) * c.width)
    mine = jnp.where(given, value, 0.0)
    rest = jnp.where(given, 0.0, value)
    shape = (value.shape[0] // 8, 8, c.width)
    r.sums[0, :, cols] += jnp.sum(mine.reshape(shape), axis=0)
    r.sums[1, :, cols] += jnp.sum(rest.reshape(shape), axis=0)


def backward_mlp(c, r, gelu_again, put):
    def start(rows):
        given = is_given(r, rows)
        grad = r.grad[rows, :].astype(f32)
        r.grad_out_b[rows, :] = (pick(c, r, 5, given) * grad).astype(bf16)
        add_sums(c, r, 5, given, grad * r.out_branch[rows, :])

    by_rows(c.rows, start)
    put(N.grad_out_b)

    @pl.loop(0, c.ratio)
    def _(j):
        cols = columns(c, j)
        r.temp[...] = mm(r.grad_out_b[...], down_block(c, r, j), NT)

        def body(rows):
            h = r.hidden[rows, cols]
            square_h = h * h
            bent = jnp.tanh(GELU_A * (h + GELU_B * (square_h * h)))
            slope = 0.5 * (1.0 + bent) + 0.5 * h * (1.0 - bent * bent) * (
                GELU_A * (1.0 + 3.0 * GELU_B * square_h)
            )
            r.grad_hidden[rows, cols] = (r.temp[rows, :] * slope).astype(bf16)
            if gelu_again:
                r.active[rows, cols] = (0.5 * h * (1.0 + bent)).astype(bf16)

        by_rows(c.rows, body)

    total = 0.0
    for j in range(c.ratio):
        block = r.grad_hidden[:, j * c.width : (j + 1) * c.width]
        total = total + mm(block, square(c, r, 4 + j), NT)
    r.temp[...] = total


def backward_mid(c, r, mix_again):
    def body(rows):
        given = is_given(r, rows)
        normed, inv = ln(r.middle[rows, :])
        scale = 1.0 + pick(c, r, 4, given)
        if mix_again:
            r.mixed_b[rows, :] = (normed * scale + pick(c, r, 3, given)).astype(bf16)
        grad_mixed = r.temp[rows, :]
        middle = r.grad[rows, :].astype(f32) + ln_back(normed, inv, grad_mixed * scale)
        r.grad_middle[rows, :] = middle
        r.grad_branch[rows, :] = (pick(c, r, 2, given) * middle).astype(bf16)
        add_sums(c, r, 3, given, grad_mixed)
        add_sums(c, r, 4, given, grad_mixed * normed)
        add_sums(c, r, 2, given, middle * r.branch[rows, :])

    by_rows(c.rows, body)
    r.grad_merged[...] = mm(
        r.grad_branch[...], square(c, r, 3), NT
    ).astype(bf16)


def backward_end(c, r, mix_again):
    total = 0.0
    for j in range(3):
        block = r.grad_packed[:, j * c.width : (j + 1) * c.width]
        total = total + mm(block, square(c, r, j), NT)
    r.temp[...] = total

    def body(rows):
        given = is_given(r, rows)
        normed, inv = ln(r.x[rows, :].astype(f32))
        scale = 1.0 + pick(c, r, 1, given)
        if mix_again:
            r.mixed_a[rows, :] = (normed * scale + pick(c, r, 0, given)).astype(bf16)
        grad_mixed = r.temp[rows, :]
        result = r.grad_middle[rows, :] + ln_back(normed, inv, grad_mixed * scale)
        r.grad_in[rows, :] = result
        if N.send in r:
            r.send[rows, :] = result.astype(bf16)
        add_sums(c, r, 0, given, grad_mixed)
        add_sums(c, r, 1, given, grad_mixed * normed)

    by_rows(c.rows, body)


def sizes(c):
    wide, rows = c.width, c.rows
    return dict(
        x=((rows, wide), bf16),
        mod=((2, 6 * wide), f32),
        given=((rows, LANES), f32),
        mixed_a=((rows, wide), bf16),
        packed=((rows, 3 * wide), bf16),
        merged=((rows, wide), bf16),
        branch=((rows, wide), f32),
        middle=((rows, wide), f32),
        mixed_b=((rows, wide), bf16),
        hidden=((rows, c.hidden), f32),
        active=((rows, c.hidden), bf16),
        out_branch=((rows, wide), f32),
        acts=((rows, wide), f32),
        send=((rows, wide), bf16),
        grad=((rows, wide), bf16),
        grad_out_b=((rows, wide), bf16),
        grad_hidden=((rows, c.hidden), bf16),
        temp=((rows, wide), f32),
        grad_middle=((rows, wide), f32),
        grad_branch=((rows, wide), bf16),
        grad_merged=((rows, wide), bf16),
        grad_packed=((rows, 3 * wide), bf16),
        grad_in=((rows, wide), f32),
        sums=((2, 8, 6 * wide), f32),
        grad_mod=((2, 6 * wide), f32),
        heads_in=((wide, LANES), bf16),
        heads_out=((LANES, wide), bf16),
    )


KEPT = (N.packed, N.merged, N.branch, N.middle, N.hidden, N.out_branch)
TERMS = (
    N.mixed_a,
    N.grad_packed,
    N.merged,
    N.grad_branch,
    N.mixed_b,
    N.grad_hidden,
    N.active,
    N.grad_out_b,
)


class Traffic:
    def __init__(self, sems):
        self.sems, self.used, self.pending = sems, 0, {}

    def start(self, name, src, dst):
        copy = pltpu.make_async_copy(src, dst, self.sems.at[self.used])
        self.used += 1
        copy.start()
        self.pending[name] = copy

    def wait(self, name):
        if name in self.pending:
            self.pending.pop(name).wait()

    def drain(self):
        for name in list(self.pending):
            self.wait(name)


def run_forward(c, r, t, temporal, put, weight_wait):
    t.wait(N.mod)
    t.wait(N.x)
    forward_a(c, r)
    put(N.mixed_a)
    weight_wait(0)
    forward_qkv(c, r)
    put(N.packed)
    if temporal:
        fill_heads(c, r)
        temporal_merge(c, r)
    else:
        spatial_merge(c, r)
    put(N.merged)
    forward_b(c, r)
    put(N.branch)
    put(N.middle)
    put(N.mixed_b)
    weight_wait(1)
    forward_mlp(c, r, weight_wait)
    put(N.hidden)
    put(N.active)
    put(N.out_branch)
    forward_end(c, r)
    put(N.acts)
    put(N.send)


def spatial_forward_kernel(c, micro, names, refs):
    h = Refs(names_hbm(names, refs))
    r = h.vmem
    first = N.near in h
    r[N.w] = h.near if first else h.w
    copies = weight_copies(c, h.w, h.near, r.wsem) if first else []
    for copy in copies:
        copy.start()

    @pl.when(h.ctl[0] == 0)
    def _():
        t = Traffic(r.sems)
        t.start(N.x, h.x.at[micro], r.x)
        t.start(N.mod, h.mod.at[micro], r.mod)
        fill_given(c, h.ctl, r)

        def put(name):
            if name in KEPT or name == N.send:
                t.start(name, r[name], h[name])
            elif name == N.acts:
                t.start(name, r.acts, h.acts.at[micro])

        def weight_wait(part):
            if first:
                copies[part].wait()

        run_forward(c, r, t, False, put, weight_wait)
        t.drain()

    if first:

        @pl.when(h.ctl[0] != 0)
        def _():
            for copy in copies:
                copy.wait()


def temporal_kernel(c, micro, names, refs):
    h = Refs(names_hbm(names, refs))
    r = h.vmem

    @pl.when(h.ctl[0] == 1)
    def _():
        t = Traffic(r.sems)
        r.update(x=h.x, w=h.w)
        t.start(N.mod, h.mod.at[micro], r.mod)
        t.start(N.grad, h.cot.at[micro], r.grad)
        fill_given(c, h.ctl, r)
        forward = Refs({k: v for k, v in r.items() if k != N.send})
        put = partial(put_backward, c, micro, h, r, t)
        run_forward(
            c,
            forward,
            t,
            True,
            lambda name: name == N.send or put(name),
            lambda part: None,
        )
        t.wait(N.grad)
        r.sums[...] = jnp.zeros_like(r.sums)
        backward_first(c, r, t, True, put)
        backward_second(c, r, t, True, put)
        t.drain()


def put_backward(c, micro, h, r, t, name):
    if name == N.send:
        if N.send in h:
            t.start(N.send, r.send, h.send)
    elif name in (N.acts, N.grad_in):
        t.start(name, r[name], h[name].at[micro])
    elif name in (N.late_sums, N.early_sums):
        early = 2 * c.width
        cols = pl.ds(0, early) if name == N.early_sums else pl.ds(early, 2 * early)
        t.start(name, r.grad_mod.at[:, cols], h.grad_mod.at[micro, :, cols])
    elif name in TERMS:
        t.start(name, r[name], h[name].at[pl.ds(micro * c.rows, c.rows), :])


def backward_first(c, r, t, temporal, put):
    backward_mlp(c, r, not temporal, put)
    put(N.grad_hidden)
    if not temporal:
        put(N.active)
    t.wait(N.middle)
    t.wait(N.branch)
    backward_mid(c, r, not temporal)
    put(N.grad_branch)
    if not temporal:
        put(N.mixed_b)
    put_sums(c, r, 2, 6)
    put(N.late_sums)


def backward_second(c, r, t, temporal, put):
    if temporal:
        temporal_back(c, r)
    else:
        spatial_back(c, r)
    put(N.grad_packed)
    t.wait(N.x)
    backward_end(c, r, not temporal)
    if not temporal:
        put(N.mixed_a)
    put(N.send)
    put(N.grad_in)
    put_sums(c, r, 0, 2)
    put(N.early_sums)


def put_sums(c, r, first, last):
    cols = slice(first * c.width, last * c.width)
    r.grad_mod[:, cols] = jnp.sum(r.sums[:, :, cols], axis=1)


def spatial_backward_kernel(c, micro, names, refs):
    h = Refs(names_hbm(names, refs))
    r = h.vmem

    @pl.when(h.ctl[0] == 0)
    def _():
        t = Traffic(r.sems)
        r.update(grad=h.grad, w=h.w)
        t.start(N.mod, h.mod.at[micro], r.mod)
        t.start(N.out_branch, h.out_branch, r.out_branch)
        t.start(N.hidden, h.hidden, r.hidden)
        t.start(N.middle, h.middle, r.middle)
        t.start(N.branch, h.branch, r.branch)
        t.start(N.packed, h.packed, r.packed)
        t.start(N.kept, h.kept, r.merged)
        t.start(N.x, h.x.at[micro], r.x)
        fill_given(c, h.ctl, r)
        r.sums[...] = jnp.zeros_like(r.sums)
        for name in (N.mod, N.out_branch, N.hidden):
            t.wait(name)
        put = partial(put_backward, c, micro, h, r, t)
        backward_first(c, r, t, False, put)
        t.wait(N.packed)
        t.wait(N.kept)
        put(N.merged)
        backward_second(c, r, t, False, put)
        t.drain()


def spatial_first_kernel(c, micro, names, refs):
    h = Refs(names_hbm(names, refs))
    r = h.vmem

    @pl.when(h.ctl[0] == 0)
    def _():
        t = Traffic(r.sems)
        r.update(grad=h.grad, w=h.w)
        t.start(N.mod, h.mod.at[micro], r.mod)
        t.start(N.out_branch, h.out_branch, r.out_branch)
        t.start(N.hidden, h.hidden, r.hidden)
        t.start(N.middle, h.middle, r.middle)
        t.start(N.branch, h.branch, r.branch)
        t.start(N.kept, h.kept, r.merged)
        fill_given(c, h.ctl, r)
        r.sums[...] = jnp.zeros_like(r.sums)
        for name in (N.mod, N.out_branch, N.hidden):
            t.wait(name)
        put = partial(put_backward, c, micro, h, r, t)
        t.wait(N.kept)
        put(N.merged)
        backward_first(c, r, t, False, put)
        t.start(N.grad_middle, r.grad_middle, h.grad_middle)
        t.start(N.grad_merged, r.grad_merged, h.grad_merged)
        t.drain()


def spatial_second_kernel(c, micro, names, refs):
    h = Refs(names_hbm(names, refs))
    r = h.vmem

    @pl.when(h.ctl[0] == 0)
    def _():
        t = Traffic(r.sems)
        r.update(w=h.w)
        for name in (N.packed, N.grad_merged):
            t.start(name, h[name], r[name])
        t.start(N.x, h.x.at[micro], r.x)
        t.start(N.mod, h.mod.at[micro], r.mod)
        t.start(N.grad_middle, h.grad_middle, r.grad_middle)
        fill_given(c, h.ctl, r)
        r.sums[...] = jnp.zeros_like(r.sums)
        for name in (N.packed, N.grad_merged, N.grad_middle, N.mod):
            t.wait(name)
        put = partial(put_backward, c, micro, h, r, t)
        backward_second(c, r, t, False, put)
        t.drain()


def names_hbm(names, refs):
    outer, inner = names
    found = dict(zip(outer, refs[: len(outer)], strict=True))
    found[N.vmem] = Refs(zip(inner, refs[len(outer) :], strict=True))
    return found


def vmem_bytes(scratch):
    sizes = [
        math.prod(v.shape) * jnp.dtype(v.dtype).itemsize
        for v in scratch
        if v.memory_space == pltpu.VMEM
    ]
    return sum(sizes) + SPARE_BYTES


def call(c, kernel, micro, operands, news, alias, scratch, flops):
    ins = list(operands)
    outs = list(alias) + list(news)
    shapes = [pltpu.HBM(operands[n].shape, operands[n].dtype) for n in alias]
    shapes += [
        (pltpu.VMEM if n == N.near else jax.ShapeDtypeStruct if n == N.send else pltpu.HBM)(*news[n])
        for n in news
    ]
    table = sizes(c)
    inner = {n: pltpu.VMEM(*table[n]) for n in scratch}
    if N.near in news:
        inner[N.wsem] = pltpu.SemaphoreType.DMA((3,))
    inner[N.sems] = pltpu.SemaphoreType.DMA((32,))
    in_names = [n if n not in alias else "_" + n for n in ins]
    names = (in_names + outs, list(inner))
    places = {N.ctl: pltpu.SMEM, N.grad: pltpu.VMEM}
    if N.near not in news:
        places[N.w] = pltpu.VMEM
    if kernel is temporal_kernel:
        places[N.x] = pltpu.VMEM
    got = pl.pallas_call(
        lambda *refs: kernel(c, micro, names, refs),
        out_shape=shapes,
        in_specs=[
            pl.BlockSpec(memory_space=places.get(n, pl.ANY)) for n in ins
        ],
        out_specs=[
            pl.BlockSpec(memory_space=pltpu.VMEM if n == N.near else pl.ANY) for n in outs
        ],
        scratch_shapes=list(inner.values()),
        input_output_aliases={ins.index(n): i for i, n in enumerate(alias)},
        compiler_params=pltpu.CompilerParams(vmem_limit_bytes=vmem_bytes(inner.values())),
        cost_estimate=pl.CostEstimate(flops=flops, bytes_accessed=20_000_000, transcendentals=0),
    )(*operands.values())
    return dict(zip(outs, got, strict=True))


FIRST = (N.active, N.grad_out_b, N.mixed_b, N.grad_hidden, N.merged, N.grad_branch)
SECOND = (N.mixed_b, N.grad_hidden, N.mixed_a, N.grad_packed)
LEAD = 2


def group_rows(c):
    return ((c.ratio + 1) * c.own, (c.ratio - LEAD + 3) * c.own, LEAD * c.own)


def gradients_kernel(c, ring, order, place, *refs):
    made = (0, 2) if order == FIRST else (1,)
    count, outs = len(order), len(made) * (4 if ring else 1)
    held = Refs(zip(order, refs[count + outs : 2 * count + outs], strict=True))
    turned, slots, in_sems, out_sems = refs[2 * count + outs :]
    copies = {
        n: pltpu.make_async_copy(refs[i], held[n], in_sems.at[i]) for i, n in enumerate(order)
    }
    for copy in copies.values():
        copy.start()
    own, step, line = c.own, c.blocks // c.ratio, c.blocks // 4
    each = outs // len(made)
    out = {g: refs[count + i * each : count + (i + 1) * each] for i, g in enumerate(made)}

    def puts(slot, group, j, tall=False):
        ref = slots.at[slot]
        if tall:
            ref = ref.reshape(step, c.ratio * own, c.width)
        if not ring:
            rows = pl.ds(j * step, step) if tall else pl.ds(0, c.blocks)
            part = pl.ds(0, c.ratio * own) if tall else pl.ds(j * own, own)
            yield pltpu.make_async_copy(ref, out[group][0].at[rows, part, :], out_sems.at[slot, 0])
            return
        if tall:
            ref = ref.reshape(2, 2, c.ratio * own, c.width)
        else:
            ref = ref.reshape(line, 2, 2, own, c.width)
        for i, (x, core) in enumerate(((0, 0), (1, 0), (0, 1), (1, 1))):
            x, core = (place[0] + x) % 2, (place[1] + core) % 2
            if tall:
                src, dst = ref.at[x, core], out[group][i].at[j, pl.ds(0, c.ratio * own), :]
            else:
                src, dst = ref.at[:, x, core], out[group][i].at[:, pl.ds(j * own, own), :]
            yield pltpu.make_async_copy(src, dst, out_sems.at[slot, i])

    def product(left, right, dims, *target):
        slots[target[0]] = mm(left, right, dims).astype(bf16).reshape(slots.shape[1:])
        for copy in puts(*target):
            copy.start()

    rest = c.ratio - LEAD
    if order == FIRST:
        copies[N.active].wait()
        copies[N.grad_out_b].wait()

        @pl.loop(0, c.ratio)
        def _(j):
            product(held.active[:, columns(c, j)], held.grad_out_b[...], TN, j, 0, j, True)

        copies[N.mixed_b].wait()
        turned[...] = held.mixed_b[...].T
        copies[N.grad_hidden].wait()

        @pl.loop(0, LEAD)
        def _(j):
            product(turned[...], held.grad_hidden[:, columns(c, j)], NN, c.ratio + j, 2, j)

        copies[N.merged].wait()
        copies[N.grad_branch].wait()
        last = c.ratio + LEAD
        product(held.merged[...], held.grad_branch[...], TN, last, 0, c.ratio)
        targets = [(j, 0, j, True) for j in range(c.ratio)] + [(last, 0, c.ratio)]
        targets += [(c.ratio + j, 2, j) for j in range(LEAD)]
    else:
        copies[N.mixed_b].wait()
        turned[...] = held.mixed_b[...].T
        copies[N.grad_hidden].wait()

        @pl.loop(0, rest)
        def _(j):
            product(turned[...], held.grad_hidden[:, columns(c, LEAD + j)], NN, j, 1, j)

        copies[N.mixed_a].wait()
        turned[...] = held.mixed_a[...].T
        copies[N.grad_packed].wait()

        @pl.loop(0, 3)
        def _(j):
            product(turned[...], held.grad_packed[:, columns(c, j)], NN, rest + j, 1, rest + j)

        targets = [(j, 1, j) for j in range(rest + 3)]
    for target in targets:
        for copy in puts(*target):
            copy.wait()


def weight_gradients(c, ring, order, place, terms):
    made = (0, 2) if order == FIRST else (1,)
    jobs = c.ratio + LEAD + 1 if order == FIRST else c.ratio - LEAD + 3
    shapes = [terms[n].shape for n in order]
    line, each = (c.blocks // 4, 4) if ring else (c.blocks, 1)
    out = []
    for group in made:
        out += [jax.ShapeDtypeStruct((line, group_rows(c)[group], c.width), bf16)] * each
    scratch = [pltpu.VMEM(s, bf16) for s in shapes] + [
        pltpu.VMEM((c.width, shapes[0][0]), bf16),
        pltpu.VMEM((jobs, c.blocks, c.own, c.width), bf16),
        pltpu.SemaphoreType.DMA((len(order),)),
        pltpu.SemaphoreType.DMA((jobs, 4)),
    ]
    got = pl.pallas_call(
        partial(gradients_kernel, c, ring, order),
        out_shape=out,
        in_specs=[pl.BlockSpec(memory_space=pltpu.SMEM)]
        + [pl.BlockSpec(memory_space=pl.ANY)] * len(order),
        out_specs=[pl.BlockSpec(memory_space=pl.ANY)] * len(out),
        scratch_shapes=scratch,
        compiler_params=pltpu.CompilerParams(vmem_limit_bytes=vmem_bytes(scratch)),
        cost_estimate=pl.CostEstimate(
            flops=2 * shapes[0][0] * c.width * c.width * jobs,
            bytes_accessed=12_000_000,
            transcendentals=0,
        ),
    )(place, *[pltpu.with_memory_space_constraint(terms[n], pltpu.HBM) for n in order])
    return [got[i * each : (i + 1) * each] for i in range(len(made))]


def add(*parts):
    total = parts[0].astype(f32)
    for part in parts[1:]:
        total = total + part.astype(f32)
    return total


LINE = (3, 2, 1)


def line_terms(terms, z):
    return [lax.dynamic_index_in_dim(terms, z ^ k, 0, keepdims=False) for k in (0,) + LINE]


def line_swap(terms):
    return terms[:1] + [swap(term, 4 * k) for term, k in zip(terms[1:], LINE)]


def ring_sums(first, second, z, sums):
    meet = lax.optimization_barrier
    (near0, far0, *core0), (near2, far2, *core2) = first
    far0 = add(far0, swap(core0[1], 1)).astype(bf16)
    pair = [add(near2, swap(core2[0], 1)).astype(bf16), add(far2, swap(core2[1], 1)).astype(bf16)]
    terms2 = line_terms(jnp.stack(pair, axis=1), z)

    far0, terms2 = meet((far0, terms2))
    group1, small = second((far0, terms2))
    far0, terms2 = swap(far0, 2), line_swap(terms2)
    near0 = add(near0, swap(core0[0], 1)).astype(bf16)

    far0, terms2, near0, (near1, far1, *core1), small = meet((far0, terms2, near0, group1, small))
    far1 = add(far1, swap(core1[1], 1)).astype(bf16)
    near0, far1 = meet((add(near0, far0).astype(bf16), far1))
    terms0 = line_swap(line_terms(near0, z))
    far1 = swap(far1, 2)
    near1 = add(near1, swap(core1[0], 1)).astype(bf16)
    sum2 = add(*terms2)
    other2 = sum2[1].astype(bf16)
    small = gather_step(gather_step(sums(small)[None], 8), 4)

    terms0, far1, near1, other2, small = meet((terms0, far1, near1, other2, small))
    terms1 = line_swap(line_terms(add(near1, far1).astype(bf16), z))
    sum2 = sum2[0] + swap(other2, 2).astype(f32)
    small = gather_step(gather_step(small, 2), 1)
    return add(*terms0), add(*terms1), sum2, small


def swap(block, distance):
    count = lax.axis_size(DP)
    return lax.ppermute(block, DP, [(i, i ^ distance) for i in range(count)])


def gather_small(block):
    count = lax.axis_size(DP)
    if count & (count - 1):
        return lax.all_gather(block, DP, axis=0, tiled=False)
    held, distance = block[None], count // 2
    while distance:
        held = gather_step(held, distance)
        distance //= 2
    return held


def gather_step(held, distance):
    other = swap(held, distance)
    lower = (lax.axis_index(DP) & distance) == 0
    pair = [jnp.where(lower, held, other), jnp.where(lower, other, held)]
    return jnp.stack(pair, axis=1).reshape((-1,) + held.shape[1:])


def scatter_small(blocks):
    count = lax.axis_size(DP)
    if count & (count - 1):
        return lax.psum_scatter(blocks, DP, scatter_dimension=0, tiled=False)
    mine = lax.axis_index(DP)
    distance = 1
    while distance < count:
        low, high = blocks[0::2], blocks[1::2]
        upper = (mine & distance) != 0
        other = swap(jnp.where(upper, low, high), distance)
        blocks = jnp.where(upper, high, low) + other
        distance *= 2
    return blocks[0]


def embed_columns(steps, index, width):
    half = width // 2
    place = (index % half).astype(f32)
    frequency = jnp.exp(-math.log(10000.0) * place / half)
    angles = steps.astype(f32)[:, None] * frequency[None, :]
    wave = jnp.where((index < half)[None, :], jnp.cos(angles), jnp.sin(angles))
    return jax.nn.silu(wave).astype(bf16)


def by_blocks(w, own, width):
    parts = w.shape[1] // width
    return w.reshape(own, parts, width).transpose(1, 0, 2).reshape(parts * own, width)


def in_vmem(block):
    return pltpu.with_memory_space_constraint(block, pltpu.VMEM)


def from_blocks(blocks, own, width):
    parts = blocks.shape[0] // own
    return blocks.reshape(parts, own, width).transpose(1, 0, 2).reshape(own, parts * width)


def local(tokens, cotangent, boxes, timesteps, w_ada, w_qkv, w_proj, w_up, w_down):
    section = lax.axis_index(SECTION)
    group = lax.axis_size(DP)
    micro_count, _, frames, patches, width = tokens.shape
    hidden = w_up.shape[2]
    rows = frames * patches
    own = width // group
    ratio = hidden // width
    direct = own % 16 == 0 and group % ratio == 0
    ring = direct and group == 16 and ratio == 4
    c = Cfg(frames, patches, width, hidden, group if direct else ratio)

    shard = jnp.concatenate(
        [
            by_blocks(w_qkv[0].astype(bf16), own, width),
            w_proj[0].astype(bf16),
            by_blocks(w_up[0].astype(bf16), own, width),
            w_down[0].astype(bf16),
        ],
        axis=0,
    )
    weights = lax.all_gather(shard, DP, axis=0, tiled=False)
    squares = 4 + ratio
    if not direct:
        weights = jnp.concatenate(
            [
                weights[:, i * own : (i + 1) * own].reshape(c.blocks, c.own, width)
                for i in range(squares)
            ]
            + [weights[:, squares * own :].reshape(c.blocks, ratio * c.own, width)],
            axis=1,
        )

    start = lax.axis_index(DP) * own
    index = start + jnp.arange(own, dtype=jnp.int32)
    steps = gather_small(timesteps.reshape(micro_count))
    steps = jnp.concatenate([jnp.zeros((group, 1), steps.dtype), steps], axis=1)
    embed = embed_columns(steps.reshape(-1), index, width)
    modulation = jnp.dot(embed, w_ada[0].astype(bf16), preferred_element_type=f32)
    modulation = scatter_small(modulation.reshape(group, 1 + micro_count, 6 * width))
    modulation = jnp.stack(
        [jnp.stack([modulation[0], modulation[1 + m]]) for m in range(micro_count)]
    )
    ctl = [
        jnp.concatenate([section.astype(jnp.int32)[None], boxes[m].reshape(-1)])
        for m in range(micro_count)
    ]

    tokens = tokens.reshape(micro_count, rows, width)
    cotangent = cotangent.reshape(micro_count, rows, width)
    whole = ((micro_count, rows, width), f32)
    one = ((rows, width), bf16)
    flops = 2 * rows * width * width * (4 + 2 * ratio)
    table = sizes(c)

    forward_names = [
        N.x, N.mod, N.given, N.mixed_a, N.packed, N.merged, N.branch, N.middle, N.mixed_b,
        N.hidden, N.active, N.out_branch, N.acts, N.send,
    ]
    back_names = [
        N.grad, N.grad_out_b, N.grad_hidden, N.temp, N.grad_middle, N.grad_branch, N.grad_merged,
        N.grad_packed, N.grad_in, N.sums, N.grad_mod,
    ]
    kept, received = [], []
    acts = None
    for m in range(micro_count):
        operands = dict(ctl=ctl[m], x=tokens, mod=modulation, w=weights)
        if m == 0:
            operands[N.w] = pltpu.with_memory_space_constraint(weights, pltpu.HBM)
        news = dict(send=one, **{n: table[n] for n in KEPT})
        if acts is None:
            news.update(acts=whole, near=(weights.shape, bf16))
        else:
            operands[N.acts] = acts
        alias = [N.acts] if acts is not None else []
        got = call(c, spatial_forward_kernel, m, operands, news, alias, forward_names, flops)
        acts = got[N.acts]
        if m == 0:
            weights = in_vmem(got[N.near])
        kept.append(got)
        received.append(in_vmem(lax.ppermute(got[N.send], SECTION, [(0, 1)])))

    shared = None
    grads = []
    for m in range(micro_count):
        operands = dict(
            ctl=ctl[m], x=received[m], mod=modulation, w=weights, cot=cotangent, acts=acts
        )
        news = dict(send=one)
        alias = [N.acts]
        if shared is None:
            news[N.grad_in] = whole
            news[N.grad_mod] = ((micro_count, 2, 6 * width), f32)
            for n in TERMS:
                news[n] = ((micro_count * rows, table[n][0][1]), bf16)
        else:
            operands.update(shared)
            alias += list(shared)
        names = forward_names + back_names + [N.heads_in, N.heads_out]
        got = call(c, temporal_kernel, m, operands, news, alias, names, 3 * flops)
        acts = got[N.acts]
        shared = {n: got[n] for n in (N.grad_in, N.grad_mod) + TERMS}
        grads.append(in_vmem(lax.ppermute(got[N.send], SECTION, [(1, 0)])))

    dp_index = lax.axis_index(DP)
    place = jnp.stack([dp_index // 2 % 2, dp_index % 2]).astype(jnp.int32)
    names = [n for n in forward_names if n not in (N.acts, N.send)] + back_names
    firsts = (N.grad_mod, N.grad_out_b, N.grad_hidden, N.active, N.mixed_b, N.grad_branch, N.merged)
    seconds = (N.grad_in, N.grad_mod, N.grad_packed, N.mixed_a)

    def operands_of(m, own_names, **more):
        got = dict(ctl=ctl[m], mod=modulation, w=weights, **more)
        for n in own_names:
            got[N.kept if n == N.merged else n] = kept[m][n]
        return got

    last = micro_count - 1
    for m in range(last):
        operands = operands_of(m, KEPT, grad=grads[m], x=tokens)
        operands.update(shared)
        shared = call(
            c, spatial_backward_kernel, m, operands, {}, list(shared), names, 2 * flops
        )
    ours = (N.out_branch, N.hidden, N.middle, N.branch, N.merged)
    operands = operands_of(last, ours, grad=grads[last])
    operands.update({n: shared[n] for n in firsts})
    news = dict(grad_middle=table[N.grad_middle], grad_merged=one)
    first_names = [
        N.mod, N.given, N.out_branch, N.hidden, N.middle, N.branch, N.merged, N.mixed_b, N.active,
        N.grad_out_b, N.grad_hidden, N.temp, N.grad_middle, N.grad_branch, N.grad_merged, N.sums,
        N.grad_mod,
    ]
    got = call(c, spatial_first_kernel, last, operands, news, firsts, first_names, 4 * flops // 3)
    shared.update({n: got[n] for n in firsts})
    between = {n: got[n] for n in news}
    first = weight_gradients(c, ring, FIRST, place, shared)

    def second(after):
        (grad_middle, grad_merged), _ = lax.optimization_barrier((tuple(between.values()), after))
        operands = operands_of(
            last, (N.packed,), x=tokens, grad_middle=grad_middle, grad_merged=grad_merged
        )
        operands.update({n: shared[n] for n in seconds})
        second_names = [
            N.x, N.mod, N.given, N.packed, N.mixed_a, N.temp, N.grad_middle, N.grad_merged,
            N.grad_packed, N.grad_in, N.sums, N.grad_mod,
        ]
        got = call(
            c, spatial_second_kernel, last, operands, {}, seconds, second_names, 2 * flops // 3
        )
        shared.update({n: got[n] for n in seconds})
        return weight_gradients(c, ring, SECOND, place, shared)[0], shared[N.grad_mod]

    def sums_of(grad_mod):
        given = jnp.sum(grad_mod[:, 0], axis=0, keepdims=True)
        return jnp.concatenate([given, grad_mod[:, 1]]).astype(bf16)

    if ring:
        *totals, sums = ring_sums(first, second, dp_index // 4, sums_of)
    else:
        group1, sums = second(())
        sums = gather_small(sums_of(sums))
        groups = first[0], group1, first[1]
        joined = [parts[0] for parts in groups]
        if not direct:
            tall = ratio * c.own
            joined = [
                jnp.concatenate(
                    [
                        part[:, i * c.own : (i + 1) * c.own].reshape(group, own, width)
                        for i in range(part.shape[1] // c.own)
                    ],
                    axis=1,
                )
                for part in (joined[0][:, tall:], joined[1], joined[2])
            ]
            tall = groups[0][0][:, :tall].reshape(group, ratio * own, width)
            joined[0] = jnp.concatenate([tall, joined[0]], axis=1)
        total = lax.psum_scatter(
            jnp.concatenate(joined, axis=1), DP, scatter_dimension=0, tiled=False
        ).astype(f32)
        cuts = (ratio + 1) * own, (2 * ratio + 4 - LEAD) * own
        totals = jnp.split(total, cuts)
    tall, rest = ratio * own, (ratio - LEAD) * own
    down, proj = totals[0][:tall], totals[0][tall:]
    up, qkv = jnp.concatenate([totals[2], totals[1][:rest]]), totals[1][rest:]
    grad_qkv = from_blocks(qkv, own, width)
    grad_proj = proj
    grad_up = from_blocks(up, own, width)
    grad_down = down

    sums = sums.reshape(group * (1 + micro_count), 6 * width)
    grad_ada = lax.dot_general(embed, sums, TN, preferred_element_type=f32)

    out_shape = (1, micro_count, 1, frames, patches, width)
    return (
        acts.reshape(out_shape),
        shared[N.grad_in].reshape(out_shape),
        grad_ada[None],
        grad_qkv[None],
        grad_proj[None],
        grad_up[None],
        grad_down[None],
    )


def solution(mesh):
    placed = (
        P(None, DP, None, None, None),
        P(None, DP, None, None, None),
        P(None, DP, None, None),
        P(None, DP),
        P(SECTION, DP, None),
        P(SECTION, DP, None),
        P(SECTION, DP, None),
        P(SECTION, DP, None),
        P(SECTION, DP, None),
    )
    return jax.shard_map(
        local,
        mesh=mesh,
        in_specs=placed,
        out_specs=(
            P(SECTION, None, DP, None, None, None),
            P(SECTION, None, DP, None, None, None),
            P(SECTION, DP, None),
            P(SECTION, DP, None),
            P(SECTION, DP, None),
            P(SECTION, DP, None),
            P(SECTION, DP, None),
        ),
        check_vma=False,
    )
```

```python
from functools import partial
import math

import jax
import jax.numpy as jnp
from jax import lax
from jax.experimental import pallas as pl
from jax.experimental.pallas import tpu as pltpu
from jax.sharding import PartitionSpec as P

HEAD_DIM = 64
GW = 16
LANES = 128
TILE = 64
STEP = 256
EPS = 1e-06
SPARE_BYTES = 10 * 1024 * 1024
EXTRA_BYTES = 2 * 1024 * 1024
f32 = jnp.float32
bf16 = jnp.bfloat16
NN = (((1,), (0,)), ((), ()))
NT = (((1,), (1,)), ((), ()))
TN = (((0,), (0,)), ((), ()))


def mm(a, b, dims=NN):
    return lax.dot_general(a, b, dims, preferred_element_type=f32)


def ln(v):
    centred = v - jnp.mean(v, axis=-1, keepdims=True)
    inv = lax.rsqrt(jnp.mean(centred * centred, axis=-1, keepdims=True) + EPS)
    return centred * inv, inv


def ln_back(normed, inv, grad):
    return inv * (
        grad
        - jnp.mean(grad, axis=-1, keepdims=True)
        - normed * jnp.mean(grad * normed, axis=-1, keepdims=True)
    )


def by_rows(count, body):
    @pl.loop(0, count // STEP)
    def _(i):
        body(pl.ds(pl.multiple_of(i * STEP, STEP), STEP))


def tiles(count, body):
    @pl.loop(0, count // TILE, unroll=True)
    def _(i):
        body(pl.multiple_of(i * TILE, TILE))


def columns(c, j):
    return pl.ds(pl.multiple_of(j * c.width, c.width), c.width)


class Refs(dict):
    __getattr__ = dict.__getitem__


class Names:
    def __getattr__(self, name):
        return name


N = Names()
DP, SECTION = "dp", "section"


class Cfg:
    def __init__(self, frames, patches, width, hidden, blocks):
        self.frames, self.patches, self.width, self.hidden = frames, patches, width, hidden
        self.rows = frames * patches
        self.ratio = hidden // width
        self.blocks = blocks
        self.own = width // blocks
        self.scaling = HEAD_DIM ** (-0.5)


def weight_copies(c, src, dst, sems):
    cuts = (0, 4 * c.own, (4 + c.ratio) * c.own, (4 + 2 * c.ratio) * c.own)
    parts = [pl.ds(a, b - a) for a, b in zip(cuts, cuts[1:])]
    return [
        pltpu.make_async_copy(src.at[:, part, :], dst.at[:, part, :], sems.at[i])
        for i, part in enumerate(parts)
    ]


def square(c, r, j):
    rows = pl.ds(pl.multiple_of(j * c.own, c.own), c.own)
    return r.w[:, rows, :].reshape(c.width, c.width)


def down_block(c, r, j):
    step = c.blocks // c.ratio
    block = r.w[pl.ds(j * step, step), (4 + c.ratio) * c.own :, :]
    return block.reshape(c.width, c.width)


def down_whole(c, r):
    return r.w[:, (4 + c.ratio) * c.own :, :].reshape(c.hidden, c.width)


def fill_given(c, ctl, r):
    patch = lax.broadcasted_iota(jnp.int32, (c.patches, LANES), 0)
    row, col = patch // GW, patch % GW
    for f in range(c.frames):
        top, bottom, left, right = (ctl[1 + 4 * f + i] for i in range(4))
        inside = (row >= top) & (row < bottom) & (col >= left) & (col < right)
        r.given[f * c.patches : (f + 1) * c.patches, :] = jnp.where(inside, 1.0, 0.0)


def pick(c, r, index, given):
    where = slice(index * c.width, (index + 1) * c.width)
    return jnp.where(given, r.mod[0:1, where], r.mod[1:2, where])


def is_given(r, rows):
    return r.given[rows, 0:1] > 0.5


def forward_a(c, r):
    def body(rows):
        given = is_given(r, rows)
        normed, _ = ln(r.x[rows, :].astype(f32))
        r.mixed_a[rows, :] = (normed * (1.0 + pick(c, r, 1, given)) + pick(c, r, 0, given)).astype(
            bf16
        )

    by_rows(c.rows, body)


def forward_qkv(c, r):
    @pl.loop(0, 3, unroll=True)
    def _(j):
        r.packed[:, columns(c, j)] = mm(r.mixed_a[...], square(c, r, j)).astype(bf16)


def halves(pair):
    first = lax.broadcasted_iota(jnp.int32, pair.shape, 1) < HEAD_DIM
    zero = jnp.zeros_like(pair)
    return jnp.concatenate([jnp.where(first, pair, zero), jnp.where(first, zero, pair)], axis=0)


def softmax_rows(scores):
    top = jnp.max(scores, axis=-1, keepdims=True)
    exponent = jnp.exp(scores - top)
    return exponent * (1.0 / jnp.sum(exponent, axis=-1, keepdims=True))


def spatial_tiles(c, body):
    @pl.loop(0, c.width // LANES, unroll=2)
    def _(pair):
        cols = [pl.ds(pl.multiple_of(i * c.width + pair * LANES, LANES), LANES) for i in range(3)]
        for f in range(c.frames):
            body(slice(f * c.patches, (f + 1) * c.patches), cols)


def spatial_merge(c, r):
    def body(rows, cols):
        q, k, v = (r.packed[rows, cols[i]] for i in range(3))
        shares = softmax_rows(mm(halves(q), k, NT) * c.scaling).astype(bf16)
        side = jnp.concatenate([shares[: c.patches], shares[c.patches :]], axis=1)
        r.merged[rows, cols[0]] = mm(side, halves(v)).astype(bf16)

    spatial_tiles(c, body)


def spatial_back(c, r):
    def body(rows, cols):
        q, k, v = (r.packed[rows, cols[i]] for i in range(3))
        q2, k2 = halves(q), halves(k)
        d2 = halves(r.grad_merged[rows, cols[0]])
        soft = softmax_rows(mm(q2, k, NT) * c.scaling)
        grad_shares = mm(d2, v, NT)
        inner = jnp.sum(soft * grad_shares, axis=-1, keepdims=True)
        grad_scores = (soft * (grad_shares - inner)).astype(bf16)
        side = jnp.concatenate([grad_scores[: c.patches], grad_scores[c.patches :]], axis=1)
        r.grad_packed[rows, cols[0]] = (mm(side, k2) * c.scaling).astype(bf16)
        r.grad_packed[rows, cols[1]] = (mm(grad_scores, q2, TN) * c.scaling).astype(bf16)
        r.grad_packed[rows, cols[2]] = mm(soft.astype(bf16), d2, TN).astype(bf16)

    spatial_tiles(c, body)


def fill_heads(c, r):
    lane = lax.broadcasted_iota(jnp.int32, (c.width, LANES), 0) // HEAD_DIM
    col = lax.broadcasted_iota(jnp.int32, (c.width, LANES), 1)
    r.heads_in[...] = jnp.where(lane == col, 1.0, 0.0).astype(bf16)
    col = lax.broadcasted_iota(jnp.int32, (LANES, c.width), 0)
    lane = lax.broadcasted_iota(jnp.int32, (LANES, c.width), 1) // HEAD_DIM
    r.heads_out[...] = jnp.where(lane == col, 1.0, 0.0).astype(bf16)


def head_sums(r, product):
    high = product.astype(bf16)
    low = (product - high.astype(f32)).astype(bf16)
    return mm(high, r.heads_in[...]) + mm(low, r.heads_in[...])


def frame_pairs(c):
    return [(f, g) for f in range(c.frames) for g in range(c.frames)]


def temporal_parts(c, r, ref, rows, part):
    return [
        ref[pl.ds(f * c.patches + rows, TILE), part * c.width : (part + 1) * c.width].astype(f32)
        for f in range(c.frames)
    ]


def temporal_soft(c, r, queries, keys):
    product = jnp.concatenate([queries[f] * keys[g] for f, g in frame_pairs(c)], axis=0)
    scores = head_sums(r, product) * c.scaling
    soft = []
    for f in range(c.frames):
        row = [scores[(f * c.frames + g) * TILE : (f * c.frames + g + 1) * TILE] for g in range(c.frames)]
        top = row[0]
        for entry in row[1:]:
            top = jnp.maximum(top, entry)
        exponent = [jnp.exp(entry - top) for entry in row]
        total = exponent[0]
        for entry in exponent[1:]:
            total = total + entry
        soft += [entry * (1.0 / total) for entry in exponent]
    return soft


def spread(r, columns):
    wide = mm(jnp.concatenate([v.astype(bf16) for v in columns], axis=0), r.heads_out[...])
    return [wide[i * TILE : (i + 1) * TILE] for i in range(len(columns))]


def temporal_merge(c, r):
    def body(rows):
        queries, keys, values = (temporal_parts(c, r, r.packed, rows, i) for i in range(3))
        shares = spread(r, temporal_soft(c, r, queries, keys))
        for f in range(c.frames):
            total = shares[f * c.frames] * values[0]
            for g in range(1, c.frames):
                total = total + shares[f * c.frames + g] * values[g]
            at = f * c.patches + rows
            r.merged[pl.ds(at, TILE), :] = total.astype(bf16)

    tiles(c.patches, body)


def temporal_back(c, r):
    n = c.frames

    def body(rows):
        queries, keys, values = (temporal_parts(c, r, r.packed, rows, i) for i in range(3))
        grads = temporal_parts(c, r, r.grad_merged, rows, 0)
        soft = temporal_soft(c, r, queries, keys)
        product = jnp.concatenate([grads[f] * values[g] for f, g in frame_pairs(c)], axis=0)
        wide = head_sums(r, product)
        grad_shares = [wide[i * TILE : (i + 1) * TILE] for i in range(n * n)]
        grad_scores = []
        for f in range(n):
            inner = soft[f * n] * grad_shares[f * n]
            for g in range(1, n):
                inner = inner + soft[f * n + g] * grad_shares[f * n + g]
            grad_scores += [
                soft[f * n + g] * (grad_shares[f * n + g] - inner) for g in range(n)
            ]
        shares = spread(r, soft)
        scores = spread(r, grad_scores)

        def put(frame, part, value):
            at = frame * c.patches + rows
            r.grad_packed[pl.ds(at, TILE), part * c.width : (part + 1) * c.width] = value.astype(bf16)

        for f in range(n):
            put(f, 0, sum(scores[f * n + g] * keys[g] for g in range(n)) * c.scaling)
            put(f, 1, sum(scores[g * n + f] * queries[g] for g in range(n)) * c.scaling)
            put(f, 2, sum(shares[g * n + f] * grads[g] for g in range(n)))

    tiles(c.patches, body)


def forward_b(c, r):
    r.branch[...] = mm(r.merged[...], square(c, r, 3))

    def body(rows):
        given = is_given(r, rows)
        middle = r.x[rows, :].astype(f32) + pick(c, r, 2, given) * r.branch[rows, :]
        r.middle[rows, :] = middle
        normed, _ = ln(middle)
        r.mixed_b[rows, :] = (normed * (1.0 + pick(c, r, 4, given)) + pick(c, r, 3, given)).astype(
            bf16
        )

    by_rows(c.rows, body)


GELU_A = math.sqrt(2.0 / math.pi)
GELU_B = 0.044715


def forward_mlp(c, r, weight_wait):
    @pl.loop(0, c.ratio, unroll=True)
    def _(j):
        cols = columns(c, j)
        r.hidden[:, cols] = mm(r.mixed_b[...], square(c, r, 4 + j))

        def body(rows):
            h = r.hidden[rows, cols]
            bent = jnp.tanh(GELU_A * (h + GELU_B * (h * h * h)))
            r.active[rows, cols] = (0.5 * h * (1.0 + bent)).astype(bf16)

        by_rows(c.rows, body)

    weight_wait(2)
    r.out_branch[...] = mm(r.active[...], down_whole(c, r))


def forward_end(c, r):
    def body(rows):
        given = is_given(r, rows)
        result = r.middle[rows, :] + pick(c, r, 5, given) * r.out_branch[rows, :]
        r.acts[rows, :] = result
        if N.send in r:
            r.send[rows, :] = result.astype(bf16)

    by_rows(c.rows, body)


def add_sums(c, r, index, given, value):
    cols = slice(index * c.width, (index + 1) * c.width)
    mine = jnp.where(given, value, 0.0)
    rest = jnp.where(given, 0.0, value)
    shape = (value.shape[0] // 8, 8, c.width)
    r.sums[0, :, cols] += jnp.sum(mine.reshape(shape), axis=0)
    r.sums[1, :, cols] += jnp.sum(rest.reshape(shape), axis=0)


def backward_mlp(c, r, gelu_again, put):
    def start(rows):
        given = is_given(r, rows)
        grad = r.grad[rows, :].astype(f32)
        r.grad_out_b[rows, :] = (pick(c, r, 5, given) * grad).astype(bf16)
        add_sums(c, r, 5, given, grad * r.out_branch[rows, :])

    by_rows(c.rows, start)
    put(N.grad_out_b)

    @pl.loop(0, c.ratio, unroll=True)
    def _(j):
        cols = columns(c, j)
        r.temp[...] = mm(r.grad_out_b[...], down_block(c, r, j), NT)

        def body(rows):
            h = r.hidden[rows, cols]
            square_h = h * h
            bent = jnp.tanh(GELU_A * (h + GELU_B * (square_h * h)))
            slope = 0.5 * (1.0 + bent) + 0.5 * h * (1.0 - bent * bent) * (
                GELU_A * (1.0 + 3.0 * GELU_B * square_h)
            )
            r.grad_hidden[rows, cols] = (r.temp[rows, :] * slope).astype(bf16)
            if gelu_again:
                r.active[rows, cols] = (0.5 * h * (1.0 + bent)).astype(bf16)

        by_rows(c.rows, body)

    total = 0.0
    for j in range(c.ratio):
        block = r.grad_hidden[:, j * c.width : (j + 1) * c.width]
        total = total + mm(block, square(c, r, 4 + j), NT)
    r.temp[...] = total


def backward_mid(c, r, mix_again):
    def body(rows):
        given = is_given(r, rows)
        normed, inv = ln(r.middle[rows, :])
        scale = 1.0 + pick(c, r, 4, given)
        if mix_again:
            r.mixed_b[rows, :] = (normed * scale + pick(c, r, 3, given)).astype(bf16)
        grad_mixed = r.temp[rows, :]
        middle = r.grad[rows, :].astype(f32) + ln_back(normed, inv, grad_mixed * scale)
        r.grad_middle[rows, :] = middle
        r.grad_branch[rows, :] = (pick(c, r, 2, given) * middle).astype(bf16)
        add_sums(c, r, 3, given, grad_mixed)
        add_sums(c, r, 4, given, grad_mixed * normed)
        add_sums(c, r, 2, given, middle * r.branch[rows, :])

    by_rows(c.rows, body)
    r.grad_merged[...] = mm(
        r.grad_branch[...], square(c, r, 3), NT
    ).astype(bf16)


def backward_end(c, r, mix_again):
    total = 0.0
    for j in range(3):
        block = r.grad_packed[:, j * c.width : (j + 1) * c.width]
        total = total + mm(block, square(c, r, j), NT)
    r.temp[...] = total

    def body(rows):
        given = is_given(r, rows)
        normed, inv = ln(r.x[rows, :].astype(f32))
        scale = 1.0 + pick(c, r, 1, given)
        if mix_again:
            r.mixed_a[rows, :] = (normed * scale + pick(c, r, 0, given)).astype(bf16)
        grad_mixed = r.temp[rows, :]
        result = r.grad_middle[rows, :] + ln_back(normed, inv, grad_mixed * scale)
        r.grad_in[rows, :] = result
        if N.send in r:
            r.send[rows, :] = result.astype(bf16)
        add_sums(c, r, 0, given, grad_mixed)
        add_sums(c, r, 1, given, grad_mixed * normed)

    by_rows(c.rows, body)


def sizes(c):
    wide, rows = c.width, c.rows
    return dict(
        x=((rows, wide), bf16),
        mod=((2, 6 * wide), f32),
        given=((rows, LANES), f32),
        mixed_a=((rows, wide), bf16),
        packed=((rows, 3 * wide), bf16),
        merged=((rows, wide), bf16),
        branch=((rows, wide), f32),
        middle=((rows, wide), f32),
        mixed_b=((rows, wide), bf16),
        hidden=((rows, c.hidden), f32),
        active=((rows, c.hidden), bf16),
        out_branch=((rows, wide), f32),
        acts=((rows, wide), f32),
        send=((rows, wide), bf16),
        grad=((rows, wide), bf16),
        grad_out_b=((rows, wide), bf16),
        grad_hidden=((rows, c.hidden), bf16),
        temp=((rows, wide), f32),
        grad_middle=((rows, wide), f32),
        grad_branch=((rows, wide), bf16),
        grad_merged=((rows, wide), bf16),
        grad_packed=((rows, 3 * wide), bf16),
        grad_in=((rows, wide), f32),
        sums=((2, 8, 6 * wide), f32),
        grad_mod=((2, 6 * wide), f32),
        heads_in=((wide, LANES), bf16),
        heads_out=((LANES, wide), bf16),
    )


KEPT = (N.packed, N.merged, N.branch, N.middle, N.hidden, N.out_branch)
TERMS = (
    N.mixed_a,
    N.grad_packed,
    N.merged,
    N.grad_branch,
    N.mixed_b,
    N.grad_hidden,
    N.active,
    N.grad_out_b,
)


class Traffic:
    def __init__(self, sems):
        self.sems, self.used, self.pending = sems, 0, {}

    def start(self, name, src, dst):
        copy = pltpu.make_async_copy(src, dst, self.sems.at[self.used])
        self.used += 1
        copy.start()
        self.pending[name] = copy

    def wait(self, name):
        if name in self.pending:
            self.pending.pop(name).wait()

    def drain(self):
        for name in list(self.pending):
            self.wait(name)


def run_forward(c, r, t, temporal, put, weight_wait):
    t.wait(N.mod)
    t.wait(N.x)
    forward_a(c, r)
    put(N.mixed_a)
    weight_wait(0)
    forward_qkv(c, r)
    put(N.packed)
    if temporal:
        fill_heads(c, r)
        temporal_merge(c, r)
    else:
        spatial_merge(c, r)
    put(N.merged)
    forward_b(c, r)
    put(N.branch)
    put(N.middle)
    put(N.mixed_b)
    weight_wait(1)
    forward_mlp(c, r, weight_wait)
    put(N.hidden)
    put(N.active)
    put(N.out_branch)
    forward_end(c, r)
    put(N.acts)
    put(N.send)


def spatial_forward_kernel(c, micro, names, refs):
    h = Refs(names_hbm(names, refs))
    r = h.vmem
    first = N.near in h
    r[N.w] = h.near if first else h.w
    copies = weight_copies(c, h.w, h.near, r.wsem) if first else []
    for copy in copies:
        copy.start()

    @pl.when(h.ctl[0] == 0)
    def _():
        t = Traffic(r.sems)
        t.start(N.x, h.x.at[micro], r.x)
        t.start(N.mod, h.mod.at[micro], r.mod)
        fill_given(c, h.ctl, r)

        def put(name):
            if name in KEPT or name == N.send:
                t.start(name, r[name], h[name])
            elif name == N.acts:
                t.start(name, r.acts, h.acts.at[micro])

        def weight_wait(part):
            if first:
                copies[part].wait()

        run_forward(c, r, t, False, put, weight_wait)
        t.drain()

    if first:

        @pl.when(h.ctl[0] != 0)
        def _():
            for copy in copies:
                copy.wait()


def temporal_kernel(c, micro, names, refs):
    h = Refs(names_hbm(names, refs))
    r = h.vmem

    @pl.when(h.ctl[0] == 1)
    def _():
        t = Traffic(r.sems)
        r.update(x=h.x, w=h.w)
        t.start(N.mod, h.mod.at[micro], r.mod)
        t.start(N.grad, h.cot.at[micro], r.grad)
        fill_given(c, h.ctl, r)
        forward = Refs({k: v for k, v in r.items() if k != N.send})
        put = partial(put_backward, c, micro, h, r, t)
        run_forward(
            c,
            forward,
            t,
            True,
            lambda name: name == N.send or put(name),
            lambda part: None,
        )
        t.wait(N.grad)
        r.sums[...] = jnp.zeros_like(r.sums)
        backward_first(c, r, t, True, put)
        backward_second(c, r, t, True, put)
        t.drain()


def put_backward(c, micro, h, r, t, name):
    if name == N.send:
        if N.send in h:
            t.start(N.send, r.send, h.send)
    elif name in (N.acts, N.grad_in):
        t.start(name, r[name], h[name].at[micro])
    elif name in (N.late_sums, N.early_sums):
        early = 2 * c.width
        cols = pl.ds(0, early) if name == N.early_sums else pl.ds(early, 2 * early)
        t.start(name, r.grad_mod.at[:, cols], h.grad_mod.at[micro, :, cols])
    elif name in TERMS:
        t.start(name, r[name], h[name].at[pl.ds(micro * c.rows, c.rows), :])


def backward_first(c, r, t, temporal, put):
    backward_mlp(c, r, not temporal, put)
    put(N.grad_hidden)
    if not temporal:
        put(N.active)
    t.wait(N.middle)
    t.wait(N.branch)
    backward_mid(c, r, not temporal)
    put(N.grad_branch)
    if not temporal:
        put(N.mixed_b)
    put_sums(c, r, 2, 6)
    put(N.late_sums)


def backward_second(c, r, t, temporal, put):
    if temporal:
        temporal_back(c, r)
    else:
        spatial_back(c, r)
    put(N.grad_packed)
    t.wait(N.x)
    backward_end(c, r, not temporal)
    if not temporal:
        put(N.mixed_a)
    put(N.send)
    put(N.grad_in)
    put_sums(c, r, 0, 2)
    put(N.early_sums)


def put_sums(c, r, first, last):
    cols = slice(first * c.width, last * c.width)
    r.grad_mod[:, cols] = jnp.sum(r.sums[:, :, cols], axis=1)


def spatial_backward_kernel(c, micro, names, refs):
    h = Refs(names_hbm(names, refs))
    r = h.vmem

    @pl.when(h.ctl[0] == 0)
    def _():
        t = Traffic(r.sems)
        r.update(grad=h.grad, w=h.w)
        t.start(N.mod, h.mod.at[micro], r.mod)
        t.start(N.out_branch, h.out_branch, r.out_branch)
        t.start(N.hidden, h.hidden, r.hidden)
        t.start(N.middle, h.middle, r.middle)
        t.start(N.branch, h.branch, r.branch)
        t.start(N.packed, h.packed, r.packed)
        t.start(N.kept, h.kept, r.merged)
        t.start(N.x, h.x.at[micro], r.x)
        fill_given(c, h.ctl, r)
        r.sums[...] = jnp.zeros_like(r.sums)
        for name in (N.mod, N.out_branch, N.hidden):
            t.wait(name)
        put = partial(put_backward, c, micro, h, r, t)
        backward_first(c, r, t, False, put)
        t.wait(N.packed)
        t.wait(N.kept)
        put(N.merged)
        backward_second(c, r, t, False, put)
        t.drain()


def spatial_first_kernel(c, micro, names, refs):
    h = Refs(names_hbm(names, refs))
    r = h.vmem

    @pl.when(h.ctl[0] == 0)
    def _():
        t = Traffic(r.sems)
        r.update(grad=h.grad, w=h.w)
        t.start(N.mod, h.mod.at[micro], r.mod)
        t.start(N.out_branch, h.out_branch, r.out_branch)
        t.start(N.hidden, h.hidden, r.hidden)
        t.start(N.middle, h.middle, r.middle)
        t.start(N.branch, h.branch, r.branch)
        t.start(N.kept, h.kept, r.merged)
        fill_given(c, h.ctl, r)
        r.sums[...] = jnp.zeros_like(r.sums)
        for name in (N.mod, N.out_branch, N.hidden):
            t.wait(name)
        put = partial(put_backward, c, micro, h, r, t)
        t.wait(N.kept)
        put(N.merged)
        backward_first(c, r, t, False, put)
        t.start(N.grad_middle, r.grad_middle, h.grad_middle)
        t.start(N.grad_merged, r.grad_merged, h.grad_merged)
        t.drain()


def spatial_second_kernel(c, micro, names, refs):
    h = Refs(names_hbm(names, refs))
    r = h.vmem

    @pl.when(h.ctl[0] == 0)
    def _():
        t = Traffic(r.sems)
        r.update(w=h.w)
        for name in (N.packed, N.grad_merged):
            t.start(name, h[name], r[name])
        t.start(N.x, h.x.at[micro], r.x)
        t.start(N.mod, h.mod.at[micro], r.mod)
        t.start(N.grad_middle, h.grad_middle, r.grad_middle)
        fill_given(c, h.ctl, r)
        r.sums[...] = jnp.zeros_like(r.sums)
        for name in (N.packed, N.grad_merged, N.grad_middle, N.mod):
            t.wait(name)
        put = partial(put_backward, c, micro, h, r, t)
        backward_second(c, r, t, False, put)
        t.drain()


def names_hbm(names, refs):
    outer, inner = names
    found = dict(zip(outer, refs[: len(outer)], strict=True))
    found[N.vmem] = Refs(zip(inner, refs[len(outer) :], strict=True))
    return found


def vmem_bytes(scratch):
    sizes = [
        math.prod(v.shape) * jnp.dtype(v.dtype).itemsize
        for v in scratch
        if v.memory_space == pltpu.VMEM
    ]
    return sum(sizes) + SPARE_BYTES


def call(c, kernel, micro, operands, news, alias, scratch, flops):
    ins = list(operands)
    outs = list(alias) + list(news)
    shapes = [pltpu.HBM(operands[n].shape, operands[n].dtype) for n in alias]
    shapes += [
        (pltpu.VMEM if n == N.near else jax.ShapeDtypeStruct if n == N.send else pltpu.HBM)(*news[n])
        for n in news
    ]
    table = sizes(c)
    inner = {n: pltpu.VMEM(*table[n]) for n in scratch}
    if N.near in news:
        inner[N.wsem] = pltpu.SemaphoreType.DMA((3,))
    inner[N.sems] = pltpu.SemaphoreType.DMA((32,))
    in_names = [n if n not in alias else "_" + n for n in ins]
    names = (in_names + outs, list(inner))
    places = {N.ctl: pltpu.SMEM, N.grad: pltpu.VMEM}
    if N.near not in news:
        places[N.w] = pltpu.VMEM
    if kernel is temporal_kernel:
        places[N.x] = pltpu.VMEM
    got = pl.pallas_call(
        lambda *refs: kernel(c, micro, names, refs),
        out_shape=shapes,
        in_specs=[
            pl.BlockSpec(memory_space=places.get(n, pl.ANY)) for n in ins
        ],
        out_specs=[
            pl.BlockSpec(memory_space=pltpu.VMEM if n == N.near else pl.ANY) for n in outs
        ],
        scratch_shapes=list(inner.values()),
        input_output_aliases={ins.index(n): i for i, n in enumerate(alias)},
        compiler_params=pltpu.CompilerParams(
            vmem_limit_bytes=vmem_bytes(inner.values()) + EXTRA_BYTES * (kernel is temporal_kernel)
        ),
        cost_estimate=pl.CostEstimate(flops=flops, bytes_accessed=20_000_000, transcendentals=0),
    )(*operands.values())
    return dict(zip(outs, got, strict=True))


FIRST = (N.merged, N.grad_branch, N.mixed_b, N.grad_hidden, N.active, N.grad_out_b)
SECOND = (N.mixed_b, N.grad_hidden, N.mixed_a, N.grad_packed)
LEAD = 2


def group_rows(c):
    return ((c.ratio + 1) * c.own, (c.ratio - LEAD + 3) * c.own, LEAD * c.own)


def gradients_kernel(c, ring, order, place, *refs):
    made = (0, 2) if order == FIRST else (1,)
    each = (4, 4, 2) if ring else (1, 1, 1)
    count, outs = len(order), sum(each[g] for g in made)
    held = Refs(zip(order, refs[count + outs : 2 * count + outs], strict=True))
    turned, slots, in_sems, out_sems = refs[2 * count + outs :]
    sources = dict(zip(order, refs, strict=False))
    lead = LEAD * c.width
    needed = pl.ds(0, lead) if order == FIRST else pl.ds(lead, c.hidden - lead)
    sources[N.grad_hidden] = sources[N.grad_hidden].at[:, needed]
    copies = {
        n: pltpu.make_async_copy(sources[n], held[n], in_sems.at[i]) for i, n in enumerate(order)
    }
    for copy in copies.values():
        copy.start()
    own, step, line = c.own, c.blocks // c.ratio, c.blocks // 4
    out, at = {}, count
    for g in made:
        out[g] = refs[at : at + each[g]]
        at += each[g]

    def puts(slot, group, j, tall=False):
        ref = slots.at[slot]
        if tall:
            ref = ref.reshape(step, c.ratio * own, c.width)
        if not ring:
            rows = pl.ds(j * step, step) if tall else pl.ds(0, c.blocks)
            part = pl.ds(0, c.ratio * own) if tall else pl.ds(j * own, own)
            yield pltpu.make_async_copy(ref, out[group][0].at[rows, part, :], out_sems.at[slot, 0])
            return
        if tall:
            ref = ref.reshape(2, 2, c.ratio * own, c.width)
            places, rows = j, pl.ds(0, c.ratio * own)
        else:
            ref = ref.reshape(line, 2, 2, own, c.width)
            places, rows = slice(None), pl.ds(j * own, own)
        for i, (x, core) in enumerate(((0, 0), (1, 0), (0, 1), (1, 1))):
            at = ((place[0] + x) % 2, (place[1] + core) % 2)
            src = ref.at[at] if tall else ref.at[:, at[0], at[1]]
            if group == 2:
                dst = out[group][core].at[places, x, rows, :]
            else:
                dst = out[group][i].at[places, rows, :]
            yield pltpu.make_async_copy(src, dst, out_sems.at[slot, i])

    def product(left, right, dims, *target):
        slots[target[0]] = mm(left, right, dims).astype(bf16).reshape(slots.shape[1:])
        for copy in puts(*target):
            copy.start()

    rest = c.ratio - LEAD
    if order == FIRST:
        last = c.ratio + LEAD
        copies[N.merged].wait()
        copies[N.grad_branch].wait()
        product(held.merged[...], held.grad_branch[...], TN, last, 0, c.ratio)
        copies[N.mixed_b].wait()
        turned[...] = held.mixed_b[...].T
        copies[N.grad_hidden].wait()

        @pl.loop(0, LEAD)
        def _(j):
            product(turned[...], held.grad_hidden[:, columns(c, j)], NN, c.ratio + j, 2, j)

        copies[N.active].wait()
        copies[N.grad_out_b].wait()

        @pl.loop(0, c.ratio)
        def _(j):
            product(held.active[:, columns(c, j)], held.grad_out_b[...], TN, j, 0, j, True)

        targets = [(j, 0, j, True) for j in range(c.ratio)] + [(last, 0, c.ratio)]
        targets += [(c.ratio + j, 2, j) for j in range(LEAD)]
    else:
        copies[N.mixed_b].wait()
        turned[...] = held.mixed_b[...].T
        copies[N.grad_hidden].wait()

        @pl.loop(0, rest)
        def _(j):
            product(turned[...], held.grad_hidden[:, columns(c, j)], NN, j, 1, j)

        copies[N.mixed_a].wait()
        turned[...] = held.mixed_a[...].T
        copies[N.grad_packed].wait()

        @pl.loop(0, 3)
        def _(j):
            product(turned[...], held.grad_packed[:, columns(c, j)], NN, rest + j, 1, rest + j)

        targets = [(j, 1, j) for j in range(rest + 3)]
    for target in targets:
        for copy in puts(*target):
            copy.wait()


def weight_gradients(c, ring, order, place, terms):
    made = (0, 2) if order == FIRST else (1,)
    jobs = c.ratio + LEAD + 1 if order == FIRST else c.ratio - LEAD + 3
    shapes = [terms[n].shape for n in order]
    lead = LEAD * c.width
    at = order.index(N.grad_hidden)
    shapes[at] = (shapes[at][0], lead if order == FIRST else c.hidden - lead)
    line, each = (c.blocks // 4, (4, 4, 2)) if ring else (c.blocks, (1, 1, 1))
    out = []
    for group in made:
        shape = (line, group_rows(c)[group], c.width)
        if ring and group == 2:
            shape = (line, 2) + shape[1:]
        plain = jax.ShapeDtypeStruct(shape, bf16)
        if ring and group == 0:
            out += [pltpu.HBM(shape, bf16), plain, pltpu.HBM(shape, bf16), plain]
        else:
            out += [plain] * each[group]
    scratch = [pltpu.VMEM(s, bf16) for s in shapes] + [
        pltpu.VMEM((c.width, shapes[0][0]), bf16),
        pltpu.VMEM((jobs, c.blocks, c.own, c.width), bf16),
        pltpu.SemaphoreType.DMA((len(order),)),
        pltpu.SemaphoreType.DMA((jobs, 4)),
    ]
    got = pl.pallas_call(
        partial(gradients_kernel, c, ring, order),
        out_shape=out,
        in_specs=[pl.BlockSpec(memory_space=pltpu.SMEM)]
        + [pl.BlockSpec(memory_space=pl.ANY)] * len(order),
        out_specs=[pl.BlockSpec(memory_space=pl.ANY)] * len(out),
        scratch_shapes=scratch,
        compiler_params=pltpu.CompilerParams(vmem_limit_bytes=vmem_bytes(scratch)),
        cost_estimate=pl.CostEstimate(
            flops=2 * shapes[0][0] * c.width * c.width * jobs,
            bytes_accessed=12_000_000,
            transcendentals=0,
        ),
    )(place, *[pltpu.with_memory_space_constraint(terms[n], pltpu.HBM) for n in order])
    return [got[: each[0]], got[each[0] :]] if order == FIRST else [got]


def add(*parts):
    total = parts[0].astype(f32)
    for part in parts[1:]:
        total = total + part.astype(f32)
    return total


LINE = (3, 2, 1)


def line_terms(z, *parts):
    def at(part, k):
        return lax.dynamic_index_in_dim(part, z ^ k, 0, keepdims=False)

    return [add(*[at(part, k) for part in parts]).astype(bf16) for k in (0,) + LINE]


def line_swap(terms):
    return terms[:1] + [swap(term, 4 * k) for term, k in zip(terms[1:], LINE)]


def ring_sums(first, second, z, sums):
    meet = lax.optimization_barrier
    (near0, far0, *core0), (both2, core2) = first
    far0 = add(far0, swap(core0[1], 1)).astype(bf16)
    terms2 = line_terms(z, both2, swap(core2, 1))

    far0, terms2 = meet((far0, terms2))
    group1, small = second((far0, terms2))
    far0, terms2 = swap(far0, 2), line_swap(terms2)
    core0 = swap(core0[0], 1)

    far0, terms2, core0, (near1, far1, *core1), small = meet((far0, terms2, core0, group1, small))
    far1 = add(far1, swap(core1[1], 1)).astype(bf16)
    sum2 = add(*terms2)
    other2, sum2 = sum2[1].astype(bf16), sum2[0]
    far0, far1, other2, sum2, small = meet((far0, far1, other2, sum2, small))
    terms0 = line_swap(line_terms(z, near0, core0, far0))
    far1 = swap(far1, 2)
    core1 = swap(core1[0], 1)
    small = gather_step(gather_step(sums(small)[None], 8), 4)

    terms0, far1, core1, small = meet((terms0, far1, core1, small))
    terms1 = line_swap(line_terms(z, near1, core1, far1))
    sum2 = sum2 + swap(other2, 2).astype(f32)
    small = gather_step(gather_step(small, 2), 1)
    return add(*terms0), add(*terms1), sum2, small


def swap(block, distance):
    count = lax.axis_size(DP)
    return lax.ppermute(block, DP, [(i, i ^ distance) for i in range(count)])


def gather_small(block):
    count = lax.axis_size(DP)
    if count & (count - 1):
        return lax.all_gather(block, DP, axis=0, tiled=False)
    held, distance = block[None], count // 2
    while distance:
        held = gather_step(held, distance)
        distance //= 2
    return held


def gather_step(held, distance):
    other = swap(held, distance)
    lower = (lax.axis_index(DP) & distance) == 0
    pair = [jnp.where(lower, held, other), jnp.where(lower, other, held)]
    return jnp.stack(pair, axis=1).reshape((-1,) + held.shape[1:])


def scatter_small(blocks):
    count = lax.axis_size(DP)
    if count & (count - 1):
        return lax.psum_scatter(blocks, DP, scatter_dimension=0, tiled=False)
    mine = lax.axis_index(DP)
    distance = 1
    while distance < count:
        low, high = blocks[0::2], blocks[1::2]
        upper = (mine & distance) != 0
        other = swap(jnp.where(upper, low, high), distance)
        blocks = jnp.where(upper, high, low) + other
        distance *= 2
    return blocks[0]


def embed_columns(steps, index, width):
    half = width // 2
    place = (index % half).astype(f32)
    frequency = jnp.exp(-math.log(10000.0) * place / half)
    angles = steps.astype(f32)[:, None] * frequency[None, :]
    wave = jnp.where((index < half)[None, :], jnp.cos(angles), jnp.sin(angles))
    return jax.nn.silu(wave).astype(bf16)


def by_blocks(w, own, width):
    return jnp.concatenate([w[:, at : at + width] for at in range(0, w.shape[1], width)])


def in_vmem(block):
    return pltpu.with_memory_space_constraint(block, pltpu.VMEM)


def from_blocks(blocks, own, width):
    starts = range(0, blocks.shape[0], own)
    return jnp.concatenate([blocks[at : at + own] for at in starts], axis=1)


def local(tokens, cotangent, boxes, timesteps, w_ada, w_qkv, w_proj, w_up, w_down):
    section = lax.axis_index(SECTION)
    group = lax.axis_size(DP)
    micro_count, _, frames, patches, width = tokens.shape
    hidden = w_up.shape[2]
    rows = frames * patches
    own = width // group
    ratio = hidden // width
    direct = own % 16 == 0 and group % ratio == 0
    ring = direct and group == 16 and ratio == 4
    c = Cfg(frames, patches, width, hidden, group if direct else ratio)

    shard = jnp.concatenate(
        [
            by_blocks(w_qkv[0].astype(bf16), own, width),
            w_proj[0].astype(bf16),
            by_blocks(w_up[0].astype(bf16), own, width),
            w_down[0].astype(bf16),
        ],
        axis=0,
    )
    weights = lax.all_gather(shard, DP, axis=0, tiled=False)
    squares = 4 + ratio
    if not direct:
        weights = jnp.concatenate(
            [
                weights[:, i * own : (i + 1) * own].reshape(c.blocks, c.own, width)
                for i in range(squares)
            ]
            + [weights[:, squares * own :].reshape(c.blocks, ratio * c.own, width)],
            axis=1,
        )

    start = lax.axis_index(DP) * own
    index = start + jnp.arange(own, dtype=jnp.int32)
    steps = gather_small(timesteps.reshape(micro_count))
    steps = jnp.concatenate([jnp.zeros((group, 1), steps.dtype), steps], axis=1)
    embed = embed_columns(steps.reshape(-1), index, width)
    modulation = jnp.dot(embed, w_ada[0].astype(bf16), preferred_element_type=f32)
    modulation = scatter_small(modulation.reshape(group, 1 + micro_count, 6 * width))
    modulation = jnp.stack(
        [jnp.stack([modulation[0], modulation[1 + m]]) for m in range(micro_count)]
    )
    ctl = [
        jnp.concatenate([section.astype(jnp.int32)[None], boxes[m].reshape(-1)])
        for m in range(micro_count)
    ]

    tokens = tokens.reshape(micro_count, rows, width)
    cotangent = cotangent.reshape(micro_count, rows, width)
    whole = ((micro_count, rows, width), f32)
    one = ((rows, width), bf16)
    flops = 2 * rows * width * width * (4 + 2 * ratio)
    table = sizes(c)

    forward_names = [
        N.x, N.mod, N.given, N.mixed_a, N.packed, N.merged, N.branch, N.middle, N.mixed_b,
        N.hidden, N.active, N.out_branch, N.acts, N.send,
    ]
    back_names = [
        N.grad, N.grad_out_b, N.grad_hidden, N.temp, N.grad_middle, N.grad_branch, N.grad_merged,
        N.grad_packed, N.grad_in, N.sums, N.grad_mod,
    ]
    kept, received = [], []
    acts = None
    for m in range(micro_count):
        operands = dict(ctl=ctl[m], x=tokens, mod=modulation, w=weights)
        if m == 0:
            operands[N.w] = pltpu.with_memory_space_constraint(weights, pltpu.HBM)
        news = dict(send=one, **{n: table[n] for n in KEPT})
        if acts is None:
            news.update(acts=whole, near=(weights.shape, bf16))
        else:
            operands[N.acts] = acts
        alias = [N.acts] if acts is not None else []
        got = call(c, spatial_forward_kernel, m, operands, news, alias, forward_names, flops)
        acts = got[N.acts]
        if m == 0:
            weights = in_vmem(got[N.near])
        kept.append(got)
        received.append(in_vmem(lax.ppermute(got[N.send], SECTION, [(0, 1)])))

    shared = None
    grads = []
    for m in range(micro_count):
        operands = dict(
            ctl=ctl[m], x=received[m], mod=modulation, w=weights, cot=cotangent, acts=acts
        )
        news = dict(send=one)
        alias = [N.acts]
        if shared is None:
            news[N.grad_in] = whole
            news[N.grad_mod] = ((micro_count, 2, 6 * width), f32)
            for n in TERMS:
                news[n] = ((micro_count * rows, table[n][0][1]), bf16)
        else:
            operands.update(shared)
            alias += list(shared)
        names = forward_names + back_names + [N.heads_in, N.heads_out]
        got = call(c, temporal_kernel, m, operands, news, alias, names, 3 * flops)
        acts = got[N.acts]
        shared = {n: got[n] for n in (N.grad_in, N.grad_mod) + TERMS}
        grads.append(in_vmem(lax.ppermute(got[N.send], SECTION, [(1, 0)])))

    dp_index = lax.axis_index(DP)
    place = jnp.stack([dp_index // 2 % 2, dp_index % 2]).astype(jnp.int32)
    names = [n for n in forward_names if n not in (N.acts, N.send)] + back_names
    firsts = (N.grad_mod, N.grad_out_b, N.grad_hidden, N.active, N.mixed_b, N.grad_branch, N.merged)
    seconds = (N.grad_in, N.grad_mod, N.grad_packed, N.mixed_a)

    def operands_of(m, own_names, **more):
        got = dict(ctl=ctl[m], mod=modulation, w=weights, **more)
        for n in own_names:
            got[N.kept if n == N.merged else n] = kept[m][n]
        return got

    last = micro_count - 1
    for m in range(last):
        operands = operands_of(m, KEPT, grad=grads[m], x=tokens)
        operands.update(shared)
        shared = call(
            c, spatial_backward_kernel, m, operands, {}, list(shared), names, 2 * flops
        )
    ours = (N.out_branch, N.hidden, N.middle, N.branch, N.merged)
    operands = operands_of(last, ours, grad=grads[last])
    operands.update({n: shared[n] for n in firsts})
    news = dict(grad_middle=table[N.grad_middle], grad_merged=one)
    first_names = [
        N.mod, N.given, N.out_branch, N.hidden, N.middle, N.branch, N.merged, N.mixed_b, N.active,
        N.grad_out_b, N.grad_hidden, N.temp, N.grad_middle, N.grad_branch, N.grad_merged, N.sums,
        N.grad_mod,
    ]
    got = call(c, spatial_first_kernel, last, operands, news, firsts, first_names, 4 * flops // 3)
    shared.update({n: got[n] for n in firsts})
    between = {n: got[n] for n in news}
    first = weight_gradients(c, ring, FIRST, place, shared)

    def second(after):
        (grad_middle, grad_merged), _ = lax.optimization_barrier((tuple(between.values()), after))
        operands = operands_of(
            last, (N.packed,), x=tokens, grad_middle=grad_middle, grad_merged=grad_merged
        )
        operands.update({n: shared[n] for n in seconds})
        second_names = [
            N.x, N.mod, N.given, N.packed, N.mixed_a, N.temp, N.grad_middle, N.grad_merged,
            N.grad_packed, N.grad_in, N.sums, N.grad_mod,
        ]
        got = call(
            c, spatial_second_kernel, last, operands, {}, seconds, second_names, 2 * flops // 3
        )
        shared.update({n: got[n] for n in seconds})
        return weight_gradients(c, ring, SECOND, place, shared)[0], shared[N.grad_mod]

    def sums_of(grad_mod):
        given = jnp.sum(grad_mod[:, 0], axis=0, keepdims=True)
        return jnp.concatenate([given, grad_mod[:, 1]]).astype(bf16)

    if ring:
        *totals, sums = ring_sums(first, second, dp_index // 4, sums_of)
    else:
        group1, sums = second(())
        sums = gather_small(sums_of(sums))
        groups = first[0], group1, first[1]
        joined = [parts[0] for parts in groups]
        if not direct:
            tall = ratio * c.own
            joined = [
                jnp.concatenate(
                    [
                        part[:, i * c.own : (i + 1) * c.own].reshape(group, own, width)
                        for i in range(part.shape[1] // c.own)
                    ],
                    axis=1,
                )
                for part in (joined[0][:, tall:], joined[1], joined[2])
            ]
            tall = groups[0][0][:, :tall].reshape(group, ratio * own, width)
            joined[0] = jnp.concatenate([tall, joined[0]], axis=1)
        total = lax.psum_scatter(
            jnp.concatenate(joined, axis=1), DP, scatter_dimension=0, tiled=False
        ).astype(f32)
        cuts = (ratio + 1) * own, (2 * ratio + 4 - LEAD) * own
        totals = jnp.split(total, cuts)
    tall, rest = ratio * own, (ratio - LEAD) * own
    down, proj = totals[0][:tall], totals[0][tall:]
    up, qkv = jnp.concatenate([totals[2], totals[1][:rest]]), totals[1][rest:]
    grad_qkv = from_blocks(qkv, own, width)
    grad_proj = proj
    grad_up = from_blocks(up, own, width)
    grad_down = down

    sums = sums.reshape(group * (1 + micro_count), 6 * width)
    grad_ada = lax.dot_general(embed, sums, TN, preferred_element_type=f32)

    out_shape = (1, micro_count, 1, frames, patches, width)
    return (
        acts.reshape(out_shape),
        shared[N.grad_in].reshape(out_shape),
        grad_ada[None],
        grad_qkv[None],
        grad_proj[None],
        grad_up[None],
        grad_down[None],
    )


def solution(mesh):
    placed = (
        P(None, DP, None, None, None),
        P(None, DP, None, None, None),
        P(None, DP, None, None),
        P(None, DP),
        P(SECTION, DP, None),
        P(SECTION, DP, None),
        P(SECTION, DP, None),
        P(SECTION, DP, None),
        P(SECTION, DP, None),
    )
    return jax.shard_map(
        local,
        mesh=mesh,
        in_specs=placed,
        out_specs=(
            P(SECTION, None, DP, None, None, None),
            P(SECTION, None, DP, None, None, None),
            P(SECTION, DP, None),
            P(SECTION, DP, None),
            P(SECTION, DP, None),
            P(SECTION, DP, None),
            P(SECTION, DP, None),
        ),
        check_vma=False,
    )
```

```python
from functools import partial
import math

import jax
import jax.numpy as jnp
from jax import lax
from jax.experimental import pallas as pl
from jax.experimental.pallas import tpu as pltpu
from jax.sharding import PartitionSpec as P

HEAD_DIM = 64
GW = 16
LANES = 128
TILE = 64
STEP = 256
EPS = 1e-06
SPARE_BYTES = 10 * 1024 * 1024
EXTRA_BYTES = 2 * 1024 * 1024
f32 = jnp.float32
bf16 = jnp.bfloat16
NN = (((1,), (0,)), ((), ()))
NT = (((1,), (1,)), ((), ()))
TN = (((0,), (0,)), ((), ()))


def mm(a, b, dims=NN):
    return lax.dot_general(a, b, dims, preferred_element_type=f32)


def ln(v):
    centred = v - jnp.mean(v, axis=-1, keepdims=True)
    inv = lax.rsqrt(jnp.mean(centred * centred, axis=-1, keepdims=True) + EPS)
    return centred * inv, inv


def ln_back(normed, inv, grad):
    return inv * (
        grad
        - jnp.mean(grad, axis=-1, keepdims=True)
        - normed * jnp.mean(grad * normed, axis=-1, keepdims=True)
    )


def by_rows(count, body):
    @pl.loop(0, count // STEP)
    def _(i):
        body(pl.ds(pl.multiple_of(i * STEP, STEP), STEP))


def tiles(count, body):
    @pl.loop(0, count // TILE, unroll=True)
    def _(i):
        body(pl.multiple_of(i * TILE, TILE))


def columns(c, j):
    return pl.ds(pl.multiple_of(j * c.width, c.width), c.width)


class Refs(dict):
    __getattr__ = dict.__getitem__


class Names:
    def __getattr__(self, name):
        return name


N = Names()
DP, SECTION = "dp", "section"


class Cfg:
    def __init__(self, frames, patches, width, hidden, blocks):
        self.frames, self.patches, self.width, self.hidden = frames, patches, width, hidden
        self.rows = frames * patches
        self.ratio = hidden // width
        self.blocks = blocks
        self.own = width // blocks
        self.scaling = HEAD_DIM ** (-0.5)


def weight_copies(c, src, dst, sems):
    cuts = (0, 4 * c.own, (4 + c.ratio) * c.own, (4 + 2 * c.ratio) * c.own)
    parts = [pl.ds(a, b - a) for a, b in zip(cuts, cuts[1:])]
    return [
        pltpu.make_async_copy(src.at[:, part, :], dst.at[:, part, :], sems.at[i])
        for i, part in enumerate(parts)
    ]


def square(c, r, j):
    rows = pl.ds(pl.multiple_of(j * c.own, c.own), c.own)
    return r.w[:, rows, :].reshape(c.width, c.width)


def down_block(c, r, j):
    step = c.blocks // c.ratio
    block = r.w[pl.ds(j * step, step), (4 + c.ratio) * c.own :, :]
    return block.reshape(c.width, c.width)


def down_whole(c, r):
    return r.w[:, (4 + c.ratio) * c.own :, :].reshape(c.hidden, c.width)


def fill_given(c, ctl, r):
    patch = lax.broadcasted_iota(jnp.int32, (c.patches, LANES), 0)
    row, col = patch // GW, patch % GW
    for f in range(c.frames):
        top, bottom, left, right = (ctl[1 + 4 * f + i] for i in range(4))
        inside = (row >= top) & (row < bottom) & (col >= left) & (col < right)
        r.given[f * c.patches : (f + 1) * c.patches, :] = jnp.where(inside, 1.0, 0.0)


def pick(c, r, index, given):
    where = slice(index * c.width, (index + 1) * c.width)
    return jnp.where(given, r.mod[0:1, where], r.mod[1:2, where])


def is_given(r, rows):
    return r.given[rows, 0:1] > 0.5


def forward_a(c, r):
    def body(rows):
        given = is_given(r, rows)
        normed, _ = ln(r.x[rows, :].astype(f32))
        r.mixed_a[rows, :] = (normed * (1.0 + pick(c, r, 1, given)) + pick(c, r, 0, given)).astype(
            bf16
        )

    by_rows(c.rows, body)


def forward_qkv(c, r):
    @pl.loop(0, 3, unroll=True)
    def _(j):
        r.packed[:, columns(c, j)] = mm(r.mixed_a[...], square(c, r, j)).astype(bf16)


def halves(pair):
    first = lax.broadcasted_iota(jnp.int32, pair.shape, 1) < HEAD_DIM
    zero = jnp.zeros_like(pair)
    return jnp.concatenate([jnp.where(first, pair, zero), jnp.where(first, zero, pair)], axis=0)


def softmax_rows(scores):
    top = jnp.max(scores, axis=-1, keepdims=True)
    exponent = jnp.exp(scores - top)
    return exponent * (1.0 / jnp.sum(exponent, axis=-1, keepdims=True))


def spatial_tiles(c, body):
    @pl.loop(0, c.width // LANES, unroll=2)
    def _(pair):
        cols = [pl.ds(pl.multiple_of(i * c.width + pair * LANES, LANES), LANES) for i in range(3)]
        for f in range(c.frames):
            body(slice(f * c.patches, (f + 1) * c.patches), cols)


def spatial_merge(c, r):
    def body(rows, cols):
        q, k, v = (r.packed[rows, cols[i]] for i in range(3))
        shares = softmax_rows(mm(halves(q), k, NT) * c.scaling).astype(bf16)
        side = jnp.concatenate([shares[: c.patches], shares[c.patches :]], axis=1)
        r.merged[rows, cols[0]] = mm(side, halves(v)).astype(bf16)

    spatial_tiles(c, body)


def spatial_back(c, r):
    def body(rows, cols):
        q, k, v = (r.packed[rows, cols[i]] for i in range(3))
        q2, k2 = halves(q), halves(k)
        d2 = halves(r.grad_merged[rows, cols[0]])
        soft = softmax_rows(mm(q2, k, NT) * c.scaling)
        grad_shares = mm(d2, v, NT)
        inner = jnp.sum(soft * grad_shares, axis=-1, keepdims=True)
        grad_scores = (soft * (grad_shares - inner)).astype(bf16)
        side = jnp.concatenate([grad_scores[: c.patches], grad_scores[c.patches :]], axis=1)
        r.grad_packed[rows, cols[0]] = (mm(side, k2) * c.scaling).astype(bf16)
        r.grad_packed[rows, cols[1]] = (mm(grad_scores, q2, TN) * c.scaling).astype(bf16)
        r.grad_packed[rows, cols[2]] = mm(soft.astype(bf16), d2, TN).astype(bf16)

    spatial_tiles(c, body)


def fill_heads(c, r):
    lane = lax.broadcasted_iota(jnp.int32, (c.width, LANES), 0) // HEAD_DIM
    col = lax.broadcasted_iota(jnp.int32, (c.width, LANES), 1)
    r.heads_in[...] = jnp.where(lane == col, 1.0, 0.0).astype(bf16)
    col = lax.broadcasted_iota(jnp.int32, (LANES, c.width), 0)
    lane = lax.broadcasted_iota(jnp.int32, (LANES, c.width), 1) // HEAD_DIM
    r.heads_out[...] = jnp.where(lane == col, 1.0, 0.0).astype(bf16)


def head_sums(r, product):
    high = product.astype(bf16)
    low = (product - high.astype(f32)).astype(bf16)
    return mm(high, r.heads_in[...]) + mm(low, r.heads_in[...])


def frame_pairs(c):
    return [(f, g) for f in range(c.frames) for g in range(c.frames)]


def temporal_parts(c, r, ref, rows, part):
    return [
        ref[pl.ds(f * c.patches + rows, TILE), part * c.width : (part + 1) * c.width].astype(f32)
        for f in range(c.frames)
    ]


def temporal_soft(c, r, queries, keys):
    product = jnp.concatenate([queries[f] * keys[g] for f, g in frame_pairs(c)], axis=0)
    scores = head_sums(r, product) * c.scaling
    soft = []
    for f in range(c.frames):
        row = [scores[(f * c.frames + g) * TILE : (f * c.frames + g + 1) * TILE] for g in range(c.frames)]
        top = row[0]
        for entry in row[1:]:
            top = jnp.maximum(top, entry)
        exponent = [jnp.exp(entry - top) for entry in row]
        total = exponent[0]
        for entry in exponent[1:]:
            total = total + entry
        soft += [entry * (1.0 / total) for entry in exponent]
    return soft


def spread(r, columns):
    wide = mm(jnp.concatenate([v.astype(bf16) for v in columns], axis=0), r.heads_out[...])
    return [wide[i * TILE : (i + 1) * TILE] for i in range(len(columns))]


def temporal_merge(c, r):
    def body(rows):
        queries, keys, values = (temporal_parts(c, r, r.packed, rows, i) for i in range(3))
        shares = spread(r, temporal_soft(c, r, queries, keys))
        for f in range(c.frames):
            total = shares[f * c.frames] * values[0]
            for g in range(1, c.frames):
                total = total + shares[f * c.frames + g] * values[g]
            at = f * c.patches + rows
            r.merged[pl.ds(at, TILE), :] = total.astype(bf16)

    tiles(c.patches, body)


def temporal_back(c, r):
    n = c.frames

    def body(rows):
        queries, keys, values = (temporal_parts(c, r, r.packed, rows, i) for i in range(3))
        grads = temporal_parts(c, r, r.grad_merged, rows, 0)
        soft = temporal_soft(c, r, queries, keys)
        product = jnp.concatenate([grads[f] * values[g] for f, g in frame_pairs(c)], axis=0)
        wide = head_sums(r, product)
        grad_shares = [wide[i * TILE : (i + 1) * TILE] for i in range(n * n)]
        grad_scores = []
        for f in range(n):
            inner = soft[f * n] * grad_shares[f * n]
            for g in range(1, n):
                inner = inner + soft[f * n + g] * grad_shares[f * n + g]
            grad_scores += [
                soft[f * n + g] * (grad_shares[f * n + g] - inner) for g in range(n)
            ]
        shares = spread(r, soft)
        scores = spread(r, grad_scores)

        def put(frame, part, value):
            at = frame * c.patches + rows
            r.grad_packed[pl.ds(at, TILE), part * c.width : (part + 1) * c.width] = value.astype(bf16)

        for f in range(n):
            put(f, 0, sum(scores[f * n + g] * keys[g] for g in range(n)) * c.scaling)
            put(f, 1, sum(scores[g * n + f] * queries[g] for g in range(n)) * c.scaling)
            put(f, 2, sum(shares[g * n + f] * grads[g] for g in range(n)))

    tiles(c.patches, body)


def forward_b(c, r):
    r.branch[...] = mm(r.merged[...], square(c, r, 3))

    def body(rows):
        given = is_given(r, rows)
        middle = r.x[rows, :].astype(f32) + pick(c, r, 2, given) * r.branch[rows, :]
        r.middle[rows, :] = middle
        normed, _ = ln(middle)
        r.mixed_b[rows, :] = (normed * (1.0 + pick(c, r, 4, given)) + pick(c, r, 3, given)).astype(
            bf16
        )

    by_rows(c.rows, body)


GELU_A = math.sqrt(2.0 / math.pi)
GELU_B = 0.044715


def forward_mlp(c, r, weight_wait):
    @pl.loop(0, c.ratio, unroll=True)
    def _(j):
        cols = columns(c, j)
        r.hidden[:, cols] = mm(r.mixed_b[...], square(c, r, 4 + j))

        def body(rows):
            h = r.hidden[rows, cols]
            bent = jnp.tanh(GELU_A * (h + GELU_B * (h * h * h)))
            r.active[rows, cols] = (0.5 * h * (1.0 + bent)).astype(bf16)

        by_rows(c.rows, body)

    weight_wait(2)
    r.out_branch[...] = mm(r.active[...], down_whole(c, r))


def forward_end(c, r):
    def body(rows):
        given = is_given(r, rows)
        result = r.middle[rows, :] + pick(c, r, 5, given) * r.out_branch[rows, :]
        r.acts[rows, :] = result
        if N.send in r:
            r.send[rows, :] = result.astype(bf16)

    by_rows(c.rows, body)


def add_sums(c, r, index, given, value):
    cols = slice(index * c.width, (index + 1) * c.width)
    mine = jnp.where(given, value, 0.0)
    rest = jnp.where(given, 0.0, value)
    shape = (value.shape[0] // 8, 8, c.width)
    r.sums[0, :, cols] += jnp.sum(mine.reshape(shape), axis=0)
    r.sums[1, :, cols] += jnp.sum(rest.reshape(shape), axis=0)


def backward_mlp(c, r, gelu_again, put):
    def start(rows):
        given = is_given(r, rows)
        grad = r.grad[rows, :].astype(f32)
        r.grad_out_b[rows, :] = (pick(c, r, 5, given) * grad).astype(bf16)
        add_sums(c, r, 5, given, grad * r.out_branch[rows, :])

    by_rows(c.rows, start)
    put(N.grad_out_b)

    @pl.loop(0, c.ratio, unroll=True)
    def _(j):
        cols = columns(c, j)
        r.temp[...] = mm(r.grad_out_b[...], down_block(c, r, j), NT)

        def body(rows):
            h = r.hidden[rows, cols]
            square_h = h * h
            bent = jnp.tanh(GELU_A * (h + GELU_B * (square_h * h)))
            slope = 0.5 * (1.0 + bent) + 0.5 * h * (1.0 - bent * bent) * (
                GELU_A * (1.0 + 3.0 * GELU_B * square_h)
            )
            r.grad_hidden[rows, cols] = (r.temp[rows, :] * slope).astype(bf16)
            if gelu_again:
                r.active[rows, cols] = (0.5 * h * (1.0 + bent)).astype(bf16)

        by_rows(c.rows, body)

    total = 0.0
    for j in range(c.ratio):
        block = r.grad_hidden[:, j * c.width : (j + 1) * c.width]
        total = total + mm(block, square(c, r, 4 + j), NT)
    r.temp[...] = total


def backward_mid(c, r, mix_again):
    def body(rows):
        given = is_given(r, rows)
        normed, inv = ln(r.middle[rows, :])
        scale = 1.0 + pick(c, r, 4, given)
        if mix_again:
            r.mixed_b[rows, :] = (normed * scale + pick(c, r, 3, given)).astype(bf16)
        grad_mixed = r.temp[rows, :]
        middle = r.grad[rows, :].astype(f32) + ln_back(normed, inv, grad_mixed * scale)
        r.grad_middle[rows, :] = middle
        r.grad_branch[rows, :] = (pick(c, r, 2, given) * middle).astype(bf16)
        add_sums(c, r, 3, given, grad_mixed)
        add_sums(c, r, 4, given, grad_mixed * normed)
        add_sums(c, r, 2, given, middle * r.branch[rows, :])

    by_rows(c.rows, body)
    r.grad_merged[...] = mm(
        r.grad_branch[...], square(c, r, 3), NT
    ).astype(bf16)


def backward_end(c, r, mix_again):
    total = 0.0
    for j in range(3):
        block = r.grad_packed[:, j * c.width : (j + 1) * c.width]
        total = total + mm(block, square(c, r, j), NT)
    r.temp[...] = total

    def body(rows):
        given = is_given(r, rows)
        normed, inv = ln(r.x[rows, :].astype(f32))
        scale = 1.0 + pick(c, r, 1, given)
        if mix_again:
            r.mixed_a[rows, :] = (normed * scale + pick(c, r, 0, given)).astype(bf16)
        grad_mixed = r.temp[rows, :]
        result = r.grad_middle[rows, :] + ln_back(normed, inv, grad_mixed * scale)
        r.grad_in[rows, :] = result
        if N.send in r:
            r.send[rows, :] = result.astype(bf16)
        add_sums(c, r, 0, given, grad_mixed)
        add_sums(c, r, 1, given, grad_mixed * normed)

    by_rows(c.rows, body)


def sizes(c):
    wide, rows = c.width, c.rows
    return dict(
        x=((rows, wide), bf16),
        mod=((2, 6 * wide), f32),
        given=((rows, LANES), f32),
        mixed_a=((rows, wide), bf16),
        packed=((rows, 3 * wide), bf16),
        merged=((rows, wide), bf16),
        branch=((rows, wide), f32),
        middle=((rows, wide), f32),
        mixed_b=((rows, wide), bf16),
        hidden=((rows, c.hidden), f32),
        active=((rows, c.hidden), bf16),
        out_branch=((rows, wide), f32),
        acts=((rows, wide), f32),
        send=((rows, wide), bf16),
        grad=((rows, wide), bf16),
        grad_out_b=((rows, wide), bf16),
        grad_hidden=((rows, c.hidden), bf16),
        temp=((rows, wide), f32),
        grad_middle=((rows, wide), f32),
        grad_branch=((rows, wide), bf16),
        grad_merged=((rows, wide), bf16),
        grad_packed=((rows, 3 * wide), bf16),
        grad_in=((rows, wide), f32),
        sums=((2, 8, 6 * wide), f32),
        grad_mod=((2, 6 * wide), f32),
        heads_in=((wide, LANES), bf16),
        heads_out=((LANES, wide), bf16),
    )


KEPT = (N.packed, N.merged, N.branch, N.middle, N.hidden, N.out_branch)
TERMS = (
    N.mixed_a,
    N.grad_packed,
    N.merged,
    N.grad_branch,
    N.mixed_b,
    N.grad_hidden,
    N.active,
    N.grad_out_b,
)


class Traffic:
    def __init__(self, sems):
        self.sems, self.used, self.pending = sems, 0, {}

    def start(self, name, src, dst):
        copy = pltpu.make_async_copy(src, dst, self.sems.at[self.used])
        self.used += 1
        copy.start()
        self.pending[name] = copy

    def wait(self, name):
        if name in self.pending:
            self.pending.pop(name).wait()

    def drain(self):
        for name in list(self.pending):
            self.wait(name)


def run_forward(c, r, t, temporal, put, weight_wait):
    t.wait(N.mod)
    t.wait(N.x)
    forward_a(c, r)
    put(N.mixed_a)
    weight_wait(0)
    forward_qkv(c, r)
    put(N.packed)
    if temporal:
        fill_heads(c, r)
        temporal_merge(c, r)
    else:
        spatial_merge(c, r)
    put(N.merged)
    forward_b(c, r)
    put(N.branch)
    put(N.middle)
    put(N.mixed_b)
    weight_wait(1)
    forward_mlp(c, r, weight_wait)
    put(N.hidden)
    put(N.active)
    put(N.out_branch)
    forward_end(c, r)
    put(N.acts)
    put(N.send)


def spatial_forward_kernel(c, micro, names, refs):
    h = Refs(names_hbm(names, refs))
    r = h.vmem
    first = N.near in h
    r[N.w] = h.near if first else h.w
    copies = weight_copies(c, h.w, h.near, r.wsem) if first else []
    for copy in copies:
        copy.start()

    @pl.when(h.ctl[0] == 0)
    def _():
        t = Traffic(r.sems)
        t.start(N.x, h.x.at[micro], r.x)
        t.start(N.mod, h.mod.at[micro], r.mod)
        fill_given(c, h.ctl, r)

        def put(name):
            if name in KEPT or name == N.send:
                t.start(name, r[name], h[name])
            elif name == N.acts:
                t.start(name, r.acts, h.acts.at[micro])

        def weight_wait(part):
            if first:
                copies[part].wait()

        run_forward(c, r, t, False, put, weight_wait)
        t.drain()

    if first:

        @pl.when(h.ctl[0] != 0)
        def _():
            for copy in copies:
                copy.wait()


def temporal_kernel(c, micro, names, refs):
    h = Refs(names_hbm(names, refs))
    r = h.vmem

    @pl.when(h.ctl[0] == 1)
    def _():
        t = Traffic(r.sems)
        r.update(x=h.x, w=h.w)
        t.start(N.mod, h.mod.at[micro], r.mod)
        t.start(N.grad, h.cot.at[micro], r.grad)
        fill_given(c, h.ctl, r)
        forward = Refs({k: v for k, v in r.items() if k != N.send})
        put = partial(put_backward, c, micro, h, r, t)
        run_forward(
            c,
            forward,
            t,
            True,
            lambda name: name == N.send or put(name),
            lambda part: None,
        )
        t.wait(N.grad)
        r.sums[...] = jnp.zeros_like(r.sums)
        backward_first(c, r, t, True, put)
        backward_second(c, r, t, True, put)
        t.drain()


def put_backward(c, micro, h, r, t, name):
    if name == N.send:
        if N.send in h:
            t.start(N.send, r.send, h.send)
    elif name in (N.acts, N.grad_in):
        t.start(name, r[name], h[name].at[micro])
    elif name in (N.late_sums, N.early_sums):
        early = 2 * c.width
        cols = pl.ds(0, early) if name == N.early_sums else pl.ds(early, 2 * early)
        t.start(name, r.grad_mod.at[:, cols], h.grad_mod.at[micro, :, cols])
    elif name in TERMS:
        t.start(name, r[name], h[name].at[pl.ds(micro * c.rows, c.rows), :])


def backward_first(c, r, t, temporal, put):
    backward_mlp(c, r, not temporal, put)
    put(N.grad_hidden)
    if not temporal:
        put(N.active)
    t.wait(N.middle)
    t.wait(N.branch)
    backward_mid(c, r, not temporal)
    put(N.grad_branch)
    if not temporal:
        put(N.mixed_b)
    put_sums(c, r, 2, 6)
    put(N.late_sums)


def backward_second(c, r, t, temporal, put):
    if temporal:
        temporal_back(c, r)
    else:
        spatial_back(c, r)
    put(N.grad_packed)
    t.wait(N.x)
    backward_end(c, r, not temporal)
    if not temporal:
        put(N.mixed_a)
    put(N.send)
    put(N.grad_in)
    put_sums(c, r, 0, 2)
    put(N.early_sums)


def put_sums(c, r, first, last):
    cols = slice(first * c.width, last * c.width)
    r.grad_mod[:, cols] = jnp.sum(r.sums[:, :, cols], axis=1)


def spatial_backward_kernel(c, micro, names, refs):
    h = Refs(names_hbm(names, refs))
    r = h.vmem

    @pl.when(h.ctl[0] == 0)
    def _():
        t = Traffic(r.sems)
        r.update(grad=h.grad, w=h.w)
        t.start(N.mod, h.mod.at[micro], r.mod)
        t.start(N.out_branch, h.out_branch, r.out_branch)
        t.start(N.hidden, h.hidden, r.hidden)
        t.start(N.middle, h.middle, r.middle)
        t.start(N.branch, h.branch, r.branch)
        t.start(N.packed, h.packed, r.packed)
        t.start(N.kept, h.kept, r.merged)
        t.start(N.x, h.x.at[micro], r.x)
        fill_given(c, h.ctl, r)
        r.sums[...] = jnp.zeros_like(r.sums)
        for name in (N.mod, N.out_branch, N.hidden):
            t.wait(name)
        put = partial(put_backward, c, micro, h, r, t)
        backward_first(c, r, t, False, put)
        t.wait(N.packed)
        t.wait(N.kept)
        put(N.merged)
        backward_second(c, r, t, False, put)
        t.drain()


def spatial_first_kernel(c, micro, names, refs):
    h = Refs(names_hbm(names, refs))
    r = h.vmem

    @pl.when(h.ctl[0] == 0)
    def _():
        t = Traffic(r.sems)
        r.update(grad=h.grad, w=h.w)
        t.start(N.mod, h.mod.at[micro], r.mod)
        t.start(N.out_branch, h.out_branch, r.out_branch)
        t.start(N.hidden, h.hidden, r.hidden)
        t.start(N.middle, h.middle, r.middle)
        t.start(N.branch, h.branch, r.branch)
        t.start(N.kept, h.kept, r.merged)
        fill_given(c, h.ctl, r)
        r.sums[...] = jnp.zeros_like(r.sums)
        for name in (N.mod, N.out_branch, N.hidden):
            t.wait(name)
        put = partial(put_backward, c, micro, h, r, t)
        t.wait(N.kept)
        put(N.merged)
        backward_first(c, r, t, False, put)
        t.start(N.grad_middle, r.grad_middle, h.grad_middle)
        t.start(N.grad_merged, r.grad_merged, h.grad_merged)
        t.drain()


def spatial_second_kernel(c, micro, names, refs):
    h = Refs(names_hbm(names, refs))
    r = h.vmem

    @pl.when(h.ctl[0] == 0)
    def _():
        t = Traffic(r.sems)
        r.update(w=h.w)
        for name in (N.packed, N.grad_merged):
            t.start(name, h[name], r[name])
        t.start(N.x, h.x.at[micro], r.x)
        t.start(N.mod, h.mod.at[micro], r.mod)
        t.start(N.grad_middle, h.grad_middle, r.grad_middle)
        fill_given(c, h.ctl, r)
        r.sums[...] = jnp.zeros_like(r.sums)
        for name in (N.packed, N.grad_merged, N.grad_middle, N.mod):
            t.wait(name)
        put = partial(put_backward, c, micro, h, r, t)
        backward_second(c, r, t, False, put)
        t.drain()


def names_hbm(names, refs):
    outer, inner = names
    found = dict(zip(outer, refs[: len(outer)], strict=True))
    found[N.vmem] = Refs(zip(inner, refs[len(outer) :], strict=True))
    return found


def vmem_bytes(scratch):
    sizes = [
        math.prod(v.shape) * jnp.dtype(v.dtype).itemsize
        for v in scratch
        if v.memory_space == pltpu.VMEM
    ]
    return sum(sizes) + SPARE_BYTES


def call(c, kernel, micro, operands, news, alias, scratch, flops):
    ins = list(operands)
    outs = list(alias) + list(news)
    shapes = [pltpu.HBM(operands[n].shape, operands[n].dtype) for n in alias]
    shapes += [
        (pltpu.VMEM if n == N.near else jax.ShapeDtypeStruct if n == N.send else pltpu.HBM)(*news[n])
        for n in news
    ]
    table = sizes(c)
    inner = {n: pltpu.VMEM(*table[n]) for n in scratch}
    if N.near in news:
        inner[N.wsem] = pltpu.SemaphoreType.DMA((3,))
    inner[N.sems] = pltpu.SemaphoreType.DMA((32,))
    in_names = [n if n not in alias else "_" + n for n in ins]
    names = (in_names + outs, list(inner))
    places = {N.ctl: pltpu.SMEM, N.grad: pltpu.VMEM}
    if N.near not in news:
        places[N.w] = pltpu.VMEM
    if kernel is temporal_kernel:
        places[N.x] = pltpu.VMEM
    got = pl.pallas_call(
        lambda *refs: kernel(c, micro, names, refs),
        out_shape=shapes,
        in_specs=[
            pl.BlockSpec(memory_space=places.get(n, pl.ANY)) for n in ins
        ],
        out_specs=[
            pl.BlockSpec(memory_space=pltpu.VMEM if n == N.near else pl.ANY) for n in outs
        ],
        scratch_shapes=list(inner.values()),
        input_output_aliases={ins.index(n): i for i, n in enumerate(alias)},
        compiler_params=pltpu.CompilerParams(
            vmem_limit_bytes=vmem_bytes(inner.values()) + EXTRA_BYTES * (kernel is temporal_kernel)
        ),
        cost_estimate=pl.CostEstimate(flops=flops, bytes_accessed=20_000_000, transcendentals=0),
    )(*operands.values())
    return dict(zip(outs, got, strict=True))


FIRST = (N.merged, N.grad_branch, N.mixed_b, N.grad_hidden, N.active, N.grad_out_b)
SECOND = (N.mixed_b, N.grad_hidden, N.mixed_a, N.grad_packed)
LEAD = 2


def group_rows(c):
    return ((c.ratio + 1) * c.own, (c.ratio - LEAD + 3) * c.own, LEAD * c.own)


def gradients_kernel(c, ring, order, place, *refs):
    made = (0, 2) if order == FIRST else (1,)
    each = (4, 4, 2) if ring else (1, 1, 1)
    count, outs = len(order), sum(each[g] for g in made)
    held = Refs(zip(order, refs[count + outs : 2 * count + outs], strict=True))
    turned, slots, in_sems, out_sems = refs[2 * count + outs :]
    sources = dict(zip(order, refs, strict=False))
    lead = LEAD * c.width
    needed = pl.ds(0, lead) if order == FIRST else pl.ds(lead, c.hidden - lead)
    sources[N.grad_hidden] = sources[N.grad_hidden].at[:, needed]
    copies = {
        n: pltpu.make_async_copy(sources[n], held[n], in_sems.at[i]) for i, n in enumerate(order)
    }
    for copy in copies.values():
        copy.start()
    own, step, line = c.own, c.blocks // c.ratio, c.blocks // 4
    out, at = {}, count
    for g in made:
        out[g] = refs[at : at + each[g]]
        at += each[g]

    def puts(slot, group, j, tall=False):
        ref = slots.at[slot]
        if tall:
            ref = ref.reshape(step, c.ratio * own, c.width)
        if not ring:
            rows = pl.ds(j * step, step) if tall else pl.ds(0, c.blocks)
            part = pl.ds(0, c.ratio * own) if tall else pl.ds(j * own, own)
            yield pltpu.make_async_copy(ref, out[group][0].at[rows, part, :], out_sems.at[slot, 0])
            return
        if tall:
            ref = ref.reshape(2, 2, c.ratio * own, c.width)
            places, rows = j, pl.ds(0, c.ratio * own)
        else:
            ref = ref.reshape(line, 2, 2, own, c.width)
            places, rows = slice(None), pl.ds(j * own, own)
        for i, (x, core) in enumerate(((0, 0), (1, 0), (0, 1), (1, 1))):
            at = ((place[0] + x) % 2, (place[1] + core) % 2)
            src = ref.at[at] if tall else ref.at[:, at[0], at[1]]
            if group == 2:
                dst = out[group][core].at[places, x, rows, :]
            else:
                dst = out[group][i].at[places, rows, :]
            yield pltpu.make_async_copy(src, dst, out_sems.at[slot, i])

    def product(left, right, dims, *target):
        slots[target[0]] = mm(left, right, dims).astype(bf16).reshape(slots.shape[1:])
        for copy in puts(*target):
            copy.start()

    rest = c.ratio - LEAD
    if order == FIRST:
        last = c.ratio + LEAD
        copies[N.merged].wait()
        copies[N.grad_branch].wait()
        product(held.merged[...], held.grad_branch[...], TN, last, 0, c.ratio)
        copies[N.mixed_b].wait()
        turned[...] = held.mixed_b[...].T
        copies[N.grad_hidden].wait()

        @pl.loop(0, LEAD)
        def _(j):
            product(turned[...], held.grad_hidden[:, columns(c, j)], NN, c.ratio + j, 2, j)

        copies[N.active].wait()
        copies[N.grad_out_b].wait()

        @pl.loop(0, c.ratio)
        def _(j):
            product(held.active[:, columns(c, j)], held.grad_out_b[...], TN, j, 0, j, True)

        targets = [(j, 0, j, True) for j in range(c.ratio)] + [(last, 0, c.ratio)]
        targets += [(c.ratio + j, 2, j) for j in range(LEAD)]
    else:
        copies[N.mixed_b].wait()
        turned[...] = held.mixed_b[...].T
        copies[N.grad_hidden].wait()

        @pl.loop(0, rest)
        def _(j):
            product(turned[...], held.grad_hidden[:, columns(c, j)], NN, j, 1, j)

        copies[N.mixed_a].wait()
        turned[...] = held.mixed_a[...].T
        copies[N.grad_packed].wait()

        @pl.loop(0, 3)
        def _(j):
            product(turned[...], held.grad_packed[:, columns(c, j)], NN, rest + j, 1, rest + j)

        targets = [(j, 1, j) for j in range(rest + 3)]
    for target in targets:
        for copy in puts(*target):
            copy.wait()


def weight_gradients(c, ring, order, place, terms):
    made = (0, 2) if order == FIRST else (1,)
    jobs = c.ratio + LEAD + 1 if order == FIRST else c.ratio - LEAD + 3
    shapes = [terms[n].shape for n in order]
    lead = LEAD * c.width
    at = order.index(N.grad_hidden)
    shapes[at] = (shapes[at][0], lead if order == FIRST else c.hidden - lead)
    line, each = (c.blocks // 4, (4, 4, 2)) if ring else (c.blocks, (1, 1, 1))
    out = []
    for group in made:
        shape = (line, group_rows(c)[group], c.width)
        if ring and group == 2:
            shape = (line, 2) + shape[1:]
        plain = jax.ShapeDtypeStruct(shape, bf16)
        if ring and group == 0:
            out += [pltpu.HBM(shape, bf16), plain, pltpu.HBM(shape, bf16), plain]
        else:
            out += [plain] * each[group]
    scratch = [pltpu.VMEM(s, bf16) for s in shapes] + [
        pltpu.VMEM((c.width, shapes[0][0]), bf16),
        pltpu.VMEM((jobs, c.blocks, c.own, c.width), bf16),
        pltpu.SemaphoreType.DMA((len(order),)),
        pltpu.SemaphoreType.DMA((jobs, 4)),
    ]
    got = pl.pallas_call(
        partial(gradients_kernel, c, ring, order),
        out_shape=out,
        in_specs=[pl.BlockSpec(memory_space=pltpu.SMEM)]
        + [pl.BlockSpec(memory_space=pl.ANY)] * len(order),
        out_specs=[pl.BlockSpec(memory_space=pl.ANY)] * len(out),
        scratch_shapes=scratch,
        compiler_params=pltpu.CompilerParams(vmem_limit_bytes=vmem_bytes(scratch)),
        cost_estimate=pl.CostEstimate(
            flops=2 * shapes[0][0] * c.width * c.width * jobs,
            bytes_accessed=12_000_000,
            transcendentals=0,
        ),
    )(place, *[pltpu.with_memory_space_constraint(terms[n], pltpu.HBM) for n in order])
    return [got[: each[0]], got[each[0] :]] if order == FIRST else [got]


def add(*parts):
    total = parts[0].astype(f32)
    for part in parts[1:]:
        total = total + part.astype(f32)
    return total


LINE = (3, 2, 1)


def line_terms(z, *parts):
    def at(part, k):
        return lax.dynamic_index_in_dim(part, z ^ k, 0, keepdims=False)

    return [add(*[at(part, k) for part in parts]).astype(bf16) for k in (0,) + LINE]


def line_swap(terms):
    return terms[:1] + [swap(term, 4 * k) for term, k in zip(terms[1:], LINE)]


def ring_sums(first, second, z, sums):
    meet = lax.optimization_barrier
    (near0, far0, *core0), (both2, core2) = first
    far0 = add(far0, swap(core0[1], 1)).astype(bf16)
    terms2 = line_terms(z, both2, swap(core2, 1))

    far0, terms2, near_core0 = meet((far0, terms2, core0[0]))
    group1, small = second((far0, terms2))
    far0, terms2 = swap(far0, 2), line_swap(terms2)
    core0 = swap(near_core0, 1)

    far0, terms2, core0, (near1, far1, *core1), small = meet((far0, terms2, core0, group1, small))
    far1 = add(far1, swap(core1[1], 1)).astype(bf16)
    sum2 = add(*terms2)
    other2, sum2 = sum2[1].astype(bf16), sum2[0]
    far0, far1, other2, sum2, small = meet((far0, far1, other2, sum2, small))
    terms0 = line_swap(line_terms(z, near0, core0, far0))
    far1 = swap(far1, 2)
    core1 = swap(core1[0], 1)
    small = gather_step(gather_step(sums(small)[None], 8), 4)

    terms0, far1, core1, small = meet((terms0, far1, core1, small))
    terms1 = line_swap(line_terms(z, near1, core1, far1))
    sum2 = sum2 + swap(other2, 2).astype(f32)
    small = gather_step(gather_step(small, 2), 1)
    return add(*terms0), add(*terms1), sum2, small


def swap(block, distance):
    count = lax.axis_size(DP)
    return lax.ppermute(block, DP, [(i, i ^ distance) for i in range(count)])


def gather_small(block):
    count = lax.axis_size(DP)
    if count & (count - 1):
        return lax.all_gather(block, DP, axis=0, tiled=False)
    held, distance = block[None], count // 2
    while distance:
        held = gather_step(held, distance)
        distance //= 2
    return held


def gather_step(held, distance):
    other = swap(held, distance)
    lower = (lax.axis_index(DP) & distance) == 0
    pair = [jnp.where(lower, held, other), jnp.where(lower, other, held)]
    return jnp.stack(pair, axis=1).reshape((-1,) + held.shape[1:])


def scatter_small(blocks):
    count = lax.axis_size(DP)
    if count & (count - 1):
        return lax.psum_scatter(blocks, DP, scatter_dimension=0, tiled=False)
    mine = lax.axis_index(DP)
    distance = 1
    while distance < count:
        low, high = blocks[0::2], blocks[1::2]
        upper = (mine & distance) != 0
        other = swap(jnp.where(upper, low, high), distance)
        blocks = jnp.where(upper, high, low) + other
        distance *= 2
    return blocks[0]


def embed_columns(steps, index, width):
    half = width // 2
    place = (index % half).astype(f32)
    frequency = jnp.exp(-math.log(10000.0) * place / half)
    angles = steps.astype(f32)[:, None] * frequency[None, :]
    wave = jnp.where((index < half)[None, :], jnp.cos(angles), jnp.sin(angles))
    return jax.nn.silu(wave).astype(bf16)


def by_blocks(w, own, width):
    return jnp.concatenate([w[:, at : at + width] for at in range(0, w.shape[1], width)])


def in_vmem(block):
    return pltpu.with_memory_space_constraint(block, pltpu.VMEM)


def from_blocks(blocks, own, width):
    starts = range(0, blocks.shape[0], own)
    return jnp.concatenate([blocks[at : at + own] for at in starts], axis=1)


def local(tokens, cotangent, boxes, timesteps, w_ada, w_qkv, w_proj, w_up, w_down):
    section = lax.axis_index(SECTION)
    group = lax.axis_size(DP)
    micro_count, _, frames, patches, width = tokens.shape
    hidden = w_up.shape[2]
    rows = frames * patches
    own = width // group
    ratio = hidden // width
    direct = own % 16 == 0 and group % ratio == 0
    ring = direct and group == 16 and ratio == 4
    c = Cfg(frames, patches, width, hidden, group if direct else ratio)

    shard = jnp.concatenate(
        [
            by_blocks(w_qkv[0].astype(bf16), own, width),
            w_proj[0].astype(bf16),
            by_blocks(w_up[0].astype(bf16), own, width),
            w_down[0].astype(bf16),
        ],
        axis=0,
    )
    weights = lax.all_gather(shard, DP, axis=0, tiled=False)
    squares = 4 + ratio
    if not direct:
        weights = jnp.concatenate(
            [
                weights[:, i * own : (i + 1) * own].reshape(c.blocks, c.own, width)
                for i in range(squares)
            ]
            + [weights[:, squares * own :].reshape(c.blocks, ratio * c.own, width)],
            axis=1,
        )

    start = lax.axis_index(DP) * own
    index = start + jnp.arange(own, dtype=jnp.int32)
    steps = gather_small(timesteps.reshape(micro_count))
    steps = jnp.concatenate([jnp.zeros((group, 1), steps.dtype), steps], axis=1)
    embed = embed_columns(steps.reshape(-1), index, width)
    modulation = jnp.dot(embed, w_ada[0].astype(bf16), preferred_element_type=f32)
    modulation = scatter_small(modulation.reshape(group, 1 + micro_count, 6 * width))
    modulation = jnp.stack(
        [jnp.stack([modulation[0], modulation[1 + m]]) for m in range(micro_count)]
    )
    ctl = [
        jnp.concatenate([section.astype(jnp.int32)[None], boxes[m].reshape(-1)])
        for m in range(micro_count)
    ]

    tokens = tokens.reshape(micro_count, rows, width)
    cotangent = cotangent.reshape(micro_count, rows, width)
    whole = ((micro_count, rows, width), f32)
    one = ((rows, width), bf16)
    flops = 2 * rows * width * width * (4 + 2 * ratio)
    table = sizes(c)

    forward_names = [
        N.x, N.mod, N.given, N.mixed_a, N.packed, N.merged, N.branch, N.middle, N.mixed_b,
        N.hidden, N.active, N.out_branch, N.acts, N.send,
    ]
    back_names = [
        N.grad, N.grad_out_b, N.grad_hidden, N.temp, N.grad_middle, N.grad_branch, N.grad_merged,
        N.grad_packed, N.grad_in, N.sums, N.grad_mod,
    ]
    kept, received = [], []
    acts = None
    for m in range(micro_count):
        operands = dict(ctl=ctl[m], x=tokens, mod=modulation, w=weights)
        if m == 0:
            operands[N.w] = pltpu.with_memory_space_constraint(weights, pltpu.HBM)
        news = dict(send=one, **{n: table[n] for n in KEPT})
        if acts is None:
            news.update(acts=whole, near=(weights.shape, bf16))
        else:
            operands[N.acts] = acts
        alias = [N.acts] if acts is not None else []
        got = call(c, spatial_forward_kernel, m, operands, news, alias, forward_names, flops)
        acts = got[N.acts]
        if m == 0:
            weights = in_vmem(got[N.near])
        kept.append(got)
        received.append(in_vmem(lax.ppermute(got[N.send], SECTION, [(0, 1)])))

    shared = None
    grads = []
    for m in range(micro_count):
        operands = dict(
            ctl=ctl[m], x=received[m], mod=modulation, w=weights, cot=cotangent, acts=acts
        )
        news = dict(send=one)
        alias = [N.acts]
        if shared is None:
            news[N.grad_in] = whole
            news[N.grad_mod] = ((micro_count, 2, 6 * width), f32)
            for n in TERMS:
                news[n] = ((micro_count * rows, table[n][0][1]), bf16)
        else:
            operands.update(shared)
            alias += list(shared)
        names = forward_names + back_names + [N.heads_in, N.heads_out]
        got = call(c, temporal_kernel, m, operands, news, alias, names, 3 * flops)
        acts = got[N.acts]
        shared = {n: got[n] for n in (N.grad_in, N.grad_mod) + TERMS}
        grads.append(in_vmem(lax.ppermute(got[N.send], SECTION, [(1, 0)])))

    dp_index = lax.axis_index(DP)
    place = jnp.stack([dp_index // 2 % 2, dp_index % 2]).astype(jnp.int32)
    names = [n for n in forward_names if n not in (N.acts, N.send)] + back_names
    firsts = (N.grad_mod, N.grad_out_b, N.grad_hidden, N.active, N.mixed_b, N.grad_branch, N.merged)
    seconds = (N.grad_in, N.grad_mod, N.grad_packed, N.mixed_a)

    def operands_of(m, own_names, **more):
        got = dict(ctl=ctl[m], mod=modulation, w=weights, **more)
        for n in own_names:
            got[N.kept if n == N.merged else n] = kept[m][n]
        return got

    last = micro_count - 1
    for m in range(last):
        operands = operands_of(m, KEPT, grad=grads[m], x=tokens)
        operands.update(shared)
        shared = call(
            c, spatial_backward_kernel, m, operands, {}, list(shared), names, 2 * flops
        )
    ours = (N.out_branch, N.hidden, N.middle, N.branch, N.merged)
    operands = operands_of(last, ours, grad=grads[last])
    operands.update({n: shared[n] for n in firsts})
    news = dict(grad_middle=table[N.grad_middle], grad_merged=one)
    first_names = [
        N.mod, N.given, N.out_branch, N.hidden, N.middle, N.branch, N.merged, N.mixed_b, N.active,
        N.grad_out_b, N.grad_hidden, N.temp, N.grad_middle, N.grad_branch, N.grad_merged, N.sums,
        N.grad_mod,
    ]
    got = call(c, spatial_first_kernel, last, operands, news, firsts, first_names, 4 * flops // 3)
    shared.update({n: got[n] for n in firsts})
    between = {n: got[n] for n in news}
    first = weight_gradients(c, ring, FIRST, place, shared)

    def second(after):
        (grad_middle, grad_merged), _ = lax.optimization_barrier((tuple(between.values()), after))
        operands = operands_of(
            last, (N.packed,), x=tokens, grad_middle=grad_middle, grad_merged=grad_merged
        )
        operands.update({n: shared[n] for n in seconds})
        second_names = [
            N.x, N.mod, N.given, N.packed, N.mixed_a, N.temp, N.grad_middle, N.grad_merged,
            N.grad_packed, N.grad_in, N.sums, N.grad_mod,
        ]
        got = call(
            c, spatial_second_kernel, last, operands, {}, seconds, second_names, 2 * flops // 3
        )
        shared.update({n: got[n] for n in seconds})
        return weight_gradients(c, ring, SECOND, place, shared)[0], shared[N.grad_mod]

    def sums_of(grad_mod):
        given = jnp.sum(grad_mod[:, 0], axis=0, keepdims=True)
        return jnp.concatenate([given, grad_mod[:, 1]]).astype(bf16)

    if ring:
        *totals, sums = ring_sums(first, second, dp_index // 4, sums_of)
    else:
        group1, sums = second(())
        sums = gather_small(sums_of(sums))
        groups = first[0], group1, first[1]
        joined = [parts[0] for parts in groups]
        if not direct:
            tall = ratio * c.own
            joined = [
                jnp.concatenate(
                    [
                        part[:, i * c.own : (i + 1) * c.own].reshape(group, own, width)
                        for i in range(part.shape[1] // c.own)
                    ],
                    axis=1,
                )
                for part in (joined[0][:, tall:], joined[1], joined[2])
            ]
            tall = groups[0][0][:, :tall].reshape(group, ratio * own, width)
            joined[0] = jnp.concatenate([tall, joined[0]], axis=1)
        total = lax.psum_scatter(
            jnp.concatenate(joined, axis=1), DP, scatter_dimension=0, tiled=False
        ).astype(f32)
        cuts = (ratio + 1) * own, (2 * ratio + 4 - LEAD) * own
        totals = jnp.split(total, cuts)
    tall, rest = ratio * own, (ratio - LEAD) * own
    down, proj = totals[0][:tall], totals[0][tall:]
    up, qkv = jnp.concatenate([totals[2], totals[1][:rest]]), totals[1][rest:]
    grad_qkv = from_blocks(qkv, own, width)
    grad_proj = proj
    grad_up = from_blocks(up, own, width)
    grad_down = down

    sums = sums.reshape(group * (1 + micro_count), 6 * width)
    grad_ada = lax.dot_general(embed, sums, TN, preferred_element_type=f32)

    out_shape = (1, micro_count, 1, frames, patches, width)
    return (
        acts.reshape(out_shape),
        shared[N.grad_in].reshape(out_shape),
        grad_ada[None],
        grad_qkv[None],
        grad_proj[None],
        grad_up[None],
        grad_down[None],
    )


def solution(mesh):
    placed = (
        P(None, DP, None, None, None),
        P(None, DP, None, None, None),
        P(None, DP, None, None),
        P(None, DP),
        P(SECTION, DP, None),
        P(SECTION, DP, None),
        P(SECTION, DP, None),
        P(SECTION, DP, None),
        P(SECTION, DP, None),
    )
    return jax.shard_map(
        local,
        mesh=mesh,
        in_specs=placed,
        out_specs=(
            P(SECTION, None, DP, None, None, None),
            P(SECTION, None, DP, None, None, None),
            P(SECTION, DP, None),
            P(SECTION, DP, None),
            P(SECTION, DP, None),
            P(SECTION, DP, None),
            P(SECTION, DP, None),
        ),
        check_vma=False,
    )
```

```python
from functools import partial
import math

import jax
import jax.numpy as jnp
from jax import lax
from jax.experimental import pallas as pl
from jax.experimental.pallas import tpu as pltpu
from jax.sharding import PartitionSpec as P

HEAD_DIM = 64
GW = 16
LANES = 128
TILE = 64
STEP = 256
EPS = 1e-06
SPARE_BYTES = 10 * 1024 * 1024
EXTRA_BYTES = 2 * 1024 * 1024
f32 = jnp.float32
bf16 = jnp.bfloat16
NN = (((1,), (0,)), ((), ()))
NT = (((1,), (1,)), ((), ()))
TN = (((0,), (0,)), ((), ()))


def mm(a, b, dims=NN):
    return lax.dot_general(a, b, dims, preferred_element_type=f32)


def ln(v):
    centred = v - jnp.mean(v, axis=-1, keepdims=True)
    inv = lax.rsqrt(jnp.mean(centred * centred, axis=-1, keepdims=True) + EPS)
    return centred * inv, inv


def ln_back(normed, inv, grad):
    return inv * (
        grad
        - jnp.mean(grad, axis=-1, keepdims=True)
        - normed * jnp.mean(grad * normed, axis=-1, keepdims=True)
    )


def by_rows(count, body):
    @pl.loop(0, count // STEP)
    def _(i):
        body(pl.ds(pl.multiple_of(i * STEP, STEP), STEP))


def tiles(count, body):
    @pl.loop(0, count // TILE, unroll=True)
    def _(i):
        body(pl.multiple_of(i * TILE, TILE))


def columns(c, j):
    return pl.ds(pl.multiple_of(j * c.width, c.width), c.width)


class Refs(dict):
    __getattr__ = dict.__getitem__


class Names:
    def __getattr__(self, name):
        return name


N = Names()
DP, SECTION = "dp", "section"


class Cfg:
    def __init__(self, frames, patches, width, hidden, blocks):
        self.frames, self.patches, self.width, self.hidden = frames, patches, width, hidden
        self.rows = frames * patches
        self.ratio = hidden // width
        self.blocks = blocks
        self.own = width // blocks
        self.scaling = HEAD_DIM ** (-0.5)


def weight_copies(c, src, dst, sems):
    cuts = (0, 4 * c.own, (4 + c.ratio) * c.own, (4 + 2 * c.ratio) * c.own)
    parts = [pl.ds(a, b - a) for a, b in zip(cuts, cuts[1:])]
    return [
        pltpu.make_async_copy(src.at[:, part, :], dst.at[:, part, :], sems.at[i])
        for i, part in enumerate(parts)
    ]


def square(c, r, j):
    rows = pl.ds(pl.multiple_of(j * c.own, c.own), c.own)
    return r.w[:, rows, :].reshape(c.width, c.width)


def down_block(c, r, j):
    step = c.blocks // c.ratio
    block = r.w[pl.ds(j * step, step), (4 + c.ratio) * c.own :, :]
    return block.reshape(c.width, c.width)


def down_whole(c, r):
    return r.w[:, (4 + c.ratio) * c.own :, :].reshape(c.hidden, c.width)


def fill_given(c, ctl, r):
    patch = lax.broadcasted_iota(jnp.int32, (c.patches, LANES), 0)
    row, col = patch // GW, patch % GW
    for f in range(c.frames):
        top, bottom, left, right = (ctl[1 + 4 * f + i] for i in range(4))
        inside = (row >= top) & (row < bottom) & (col >= left) & (col < right)
        r.given[f * c.patches : (f + 1) * c.patches, :] = jnp.where(inside, 1.0, 0.0)


def pick(c, r, index, given):
    where = slice(index * c.width, (index + 1) * c.width)
    return jnp.where(given, r.mod[0:1, where], r.mod[1:2, where])


def is_given(r, rows):
    return r.given[rows, 0:1] > 0.5


def forward_a(c, r):
    def body(rows):
        given = is_given(r, rows)
        normed, _ = ln(r.x[rows, :].astype(f32))
        r.mixed_a[rows, :] = (normed * (1.0 + pick(c, r, 1, given)) + pick(c, r, 0, given)).astype(
            bf16
        )

    by_rows(c.rows, body)


def forward_qkv(c, r):
    @pl.loop(0, 3, unroll=True)
    def _(j):
        r.packed[:, columns(c, j)] = mm(r.mixed_a[...], square(c, r, j)).astype(bf16)


def halves(pair):
    first = lax.broadcasted_iota(jnp.int32, pair.shape, 1) < HEAD_DIM
    zero = jnp.zeros_like(pair)
    return jnp.concatenate([jnp.where(first, pair, zero), jnp.where(first, zero, pair)], axis=0)


def softmax_rows(scores):
    top = jnp.max(scores, axis=-1, keepdims=True)
    exponent = jnp.exp(scores - top)
    return exponent * (1.0 / jnp.sum(exponent, axis=-1, keepdims=True))


def spatial_tiles(c, body):
    @pl.loop(0, c.width // LANES, unroll=2)
    def _(pair):
        cols = [pl.ds(pl.multiple_of(i * c.width + pair * LANES, LANES), LANES) for i in range(3)]
        for f in range(c.frames):
            body(slice(f * c.patches, (f + 1) * c.patches), cols)


def spatial_merge(c, r):
    def body(rows, cols):
        q, k, v = (r.packed[rows, cols[i]] for i in range(3))
        shares = softmax_rows(mm(halves(q), k, NT) * c.scaling).astype(bf16)
        side = jnp.concatenate([shares[: c.patches], shares[c.patches :]], axis=1)
        r.merged[rows, cols[0]] = mm(side, halves(v)).astype(bf16)

    spatial_tiles(c, body)


def spatial_back(c, r):
    def body(rows, cols):
        q, k, v = (r.packed[rows, cols[i]] for i in range(3))
        q2, k2 = halves(q), halves(k)
        d2 = halves(r.grad_merged[rows, cols[0]])
        soft = softmax_rows(mm(q2, k, NT) * c.scaling)
        grad_shares = mm(d2, v, NT)
        inner = jnp.sum(soft * grad_shares, axis=-1, keepdims=True)
        grad_scores = (soft * (grad_shares - inner)).astype(bf16)
        side = jnp.concatenate([grad_scores[: c.patches], grad_scores[c.patches :]], axis=1)
        r.grad_packed[rows, cols[0]] = (mm(side, k2) * c.scaling).astype(bf16)
        r.grad_packed[rows, cols[1]] = (mm(grad_scores, q2, TN) * c.scaling).astype(bf16)
        r.grad_packed[rows, cols[2]] = mm(soft.astype(bf16), d2, TN).astype(bf16)

    spatial_tiles(c, body)


def fill_heads(c, r):
    lane = lax.broadcasted_iota(jnp.int32, (c.width, LANES), 0) // HEAD_DIM
    col = lax.broadcasted_iota(jnp.int32, (c.width, LANES), 1)
    r.heads_in[...] = jnp.where(lane == col, 1.0, 0.0).astype(bf16)
    col = lax.broadcasted_iota(jnp.int32, (LANES, c.width), 0)
    lane = lax.broadcasted_iota(jnp.int32, (LANES, c.width), 1) // HEAD_DIM
    r.heads_out[...] = jnp.where(lane == col, 1.0, 0.0).astype(bf16)


def head_sums(r, product):
    high = product.astype(bf16)
    low = (product - high.astype(f32)).astype(bf16)
    return mm(high, r.heads_in[...]) + mm(low, r.heads_in[...])


def frame_pairs(c):
    return [(f, g) for f in range(c.frames) for g in range(c.frames)]


def temporal_parts(c, r, ref, rows, part):
    return [
        ref[pl.ds(f * c.patches + rows, TILE), part * c.width : (part + 1) * c.width].astype(f32)
        for f in range(c.frames)
    ]


def temporal_soft(c, r, queries, keys):
    product = jnp.concatenate([queries[f] * keys[g] for f, g in frame_pairs(c)], axis=0)
    scores = head_sums(r, product) * c.scaling
    soft = []
    for f in range(c.frames):
        row = [scores[(f * c.frames + g) * TILE : (f * c.frames + g + 1) * TILE] for g in range(c.frames)]
        top = row[0]
        for entry in row[1:]:
            top = jnp.maximum(top, entry)
        exponent = [jnp.exp(entry - top) for entry in row]
        total = exponent[0]
        for entry in exponent[1:]:
            total = total + entry
        soft += [entry * (1.0 / total) for entry in exponent]
    return soft


def spread(r, columns):
    wide = mm(jnp.concatenate([v.astype(bf16) for v in columns], axis=0), r.heads_out[...])
    return [wide[i * TILE : (i + 1) * TILE] for i in range(len(columns))]


def temporal_merge(c, r):
    def body(rows):
        queries, keys, values = (temporal_parts(c, r, r.packed, rows, i) for i in range(3))
        shares = spread(r, temporal_soft(c, r, queries, keys))
        for f in range(c.frames):
            total = shares[f * c.frames] * values[0]
            for g in range(1, c.frames):
                total = total + shares[f * c.frames + g] * values[g]
            at = f * c.patches + rows
            r.merged[pl.ds(at, TILE), :] = total.astype(bf16)

    tiles(c.patches, body)


def temporal_back(c, r):
    n = c.frames

    def body(rows):
        queries, keys, values = (temporal_parts(c, r, r.packed, rows, i) for i in range(3))
        grads = temporal_parts(c, r, r.grad_merged, rows, 0)
        soft = temporal_soft(c, r, queries, keys)
        product = jnp.concatenate([grads[f] * values[g] for f, g in frame_pairs(c)], axis=0)
        wide = head_sums(r, product)
        grad_shares = [wide[i * TILE : (i + 1) * TILE] for i in range(n * n)]
        grad_scores = []
        for f in range(n):
            inner = soft[f * n] * grad_shares[f * n]
            for g in range(1, n):
                inner = inner + soft[f * n + g] * grad_shares[f * n + g]
            grad_scores += [
                soft[f * n + g] * (grad_shares[f * n + g] - inner) for g in range(n)
            ]
        shares = spread(r, soft)
        scores = spread(r, grad_scores)

        def put(frame, part, value):
            at = frame * c.patches + rows
            r.grad_packed[pl.ds(at, TILE), part * c.width : (part + 1) * c.width] = value.astype(bf16)

        for f in range(n):
            put(f, 0, sum(scores[f * n + g] * keys[g] for g in range(n)) * c.scaling)
            put(f, 1, sum(scores[g * n + f] * queries[g] for g in range(n)) * c.scaling)
            put(f, 2, sum(shares[g * n + f] * grads[g] for g in range(n)))

    tiles(c.patches, body)


def forward_b(c, r):
    r.branch[...] = mm(r.merged[...], square(c, r, 3))

    def body(rows):
        given = is_given(r, rows)
        middle = r.x[rows, :].astype(f32) + pick(c, r, 2, given) * r.branch[rows, :]
        r.middle[rows, :] = middle
        normed, _ = ln(middle)
        r.mixed_b[rows, :] = (normed * (1.0 + pick(c, r, 4, given)) + pick(c, r, 3, given)).astype(
            bf16
        )

    by_rows(c.rows, body)


GELU_A = math.sqrt(2.0 / math.pi)
GELU_B = 0.044715


def forward_mlp(c, r, weight_wait):
    @pl.loop(0, c.ratio, unroll=True)
    def _(j):
        cols = columns(c, j)
        r.hidden[:, cols] = mm(r.mixed_b[...], square(c, r, 4 + j))

        def body(rows):
            h = r.hidden[rows, cols]
            bent = jnp.tanh(GELU_A * (h + GELU_B * (h * h * h)))
            r.active[rows, cols] = (0.5 * h * (1.0 + bent)).astype(bf16)

        by_rows(c.rows, body)

    weight_wait(2)
    r.out_branch[...] = mm(r.active[...], down_whole(c, r))


def forward_end(c, r):
    def body(rows):
        given = is_given(r, rows)
        result = r.middle[rows, :] + pick(c, r, 5, given) * r.out_branch[rows, :]
        r.acts[rows, :] = result
        if N.send in r:
            r.send[rows, :] = result.astype(bf16)

    by_rows(c.rows, body)


def add_sums(c, r, index, given, value):
    cols = slice(index * c.width, (index + 1) * c.width)
    mine = jnp.where(given, value, 0.0)
    rest = jnp.where(given, 0.0, value)
    shape = (value.shape[0] // 8, 8, c.width)
    r.sums[0, :, cols] += jnp.sum(mine.reshape(shape), axis=0)
    r.sums[1, :, cols] += jnp.sum(rest.reshape(shape), axis=0)


def backward_mlp(c, r, gelu_again, put):
    def start(rows):
        given = is_given(r, rows)
        grad = r.grad[rows, :].astype(f32)
        r.grad_out_b[rows, :] = (pick(c, r, 5, given) * grad).astype(bf16)
        add_sums(c, r, 5, given, grad * r.out_branch[rows, :])

    by_rows(c.rows, start)
    put(N.grad_out_b)

    @pl.loop(0, c.ratio, unroll=True)
    def _(j):
        cols = columns(c, j)
        r.temp[...] = mm(r.grad_out_b[...], down_block(c, r, j), NT)

        def body(rows):
            h = r.hidden[rows, cols]
            square_h = h * h
            bent = jnp.tanh(GELU_A * (h + GELU_B * (square_h * h)))
            slope = 0.5 * (1.0 + bent) + 0.5 * h * (1.0 - bent * bent) * (
                GELU_A * (1.0 + 3.0 * GELU_B * square_h)
            )
            r.grad_hidden[rows, cols] = (r.temp[rows, :] * slope).astype(bf16)
            if gelu_again:
                r.active[rows, cols] = (0.5 * h * (1.0 + bent)).astype(bf16)

        by_rows(c.rows, body)

    total = 0.0
    for j in range(c.ratio):
        block = r.grad_hidden[:, j * c.width : (j + 1) * c.width]
        total = total + mm(block, square(c, r, 4 + j), NT)
    r.temp[...] = total


def backward_mid(c, r, mix_again):
    def body(rows):
        given = is_given(r, rows)
        normed, inv = ln(r.middle[rows, :])
        scale = 1.0 + pick(c, r, 4, given)
        if mix_again:
            r.mixed_b[rows, :] = (normed * scale + pick(c, r, 3, given)).astype(bf16)
        grad_mixed = r.temp[rows, :]
        middle = r.grad[rows, :].astype(f32) + ln_back(normed, inv, grad_mixed * scale)
        r.grad_middle[rows, :] = middle
        r.grad_branch[rows, :] = (pick(c, r, 2, given) * middle).astype(bf16)
        add_sums(c, r, 3, given, grad_mixed)
        add_sums(c, r, 4, given, grad_mixed * normed)
        add_sums(c, r, 2, given, middle * r.branch[rows, :])

    by_rows(c.rows, body)
    r.grad_merged[...] = mm(
        r.grad_branch[...], square(c, r, 3), NT
    ).astype(bf16)


def backward_end(c, r, mix_again):
    total = 0.0
    for j in range(3):
        block = r.grad_packed[:, j * c.width : (j + 1) * c.width]
        total = total + mm(block, square(c, r, j), NT)
    r.temp[...] = total

    def body(rows):
        given = is_given(r, rows)
        normed, inv = ln(r.x[rows, :].astype(f32))
        scale = 1.0 + pick(c, r, 1, given)
        if mix_again:
            r.mixed_a[rows, :] = (normed * scale + pick(c, r, 0, given)).astype(bf16)
        grad_mixed = r.temp[rows, :]
        result = r.grad_middle[rows, :] + ln_back(normed, inv, grad_mixed * scale)
        r.grad_in[rows, :] = result
        if N.send in r:
            r.send[rows, :] = result.astype(bf16)
        add_sums(c, r, 0, given, grad_mixed)
        add_sums(c, r, 1, given, grad_mixed * normed)

    by_rows(c.rows, body)


def sizes(c):
    wide, rows = c.width, c.rows
    return dict(
        x=((rows, wide), bf16),
        mod=((2, 6 * wide), f32),
        given=((rows, LANES), f32),
        mixed_a=((rows, wide), bf16),
        packed=((rows, 3 * wide), bf16),
        merged=((rows, wide), bf16),
        branch=((rows, wide), f32),
        middle=((rows, wide), f32),
        mixed_b=((rows, wide), bf16),
        hidden=((rows, c.hidden), f32),
        active=((rows, c.hidden), bf16),
        out_branch=((rows, wide), f32),
        acts=((rows, wide), f32),
        send=((rows, wide), bf16),
        grad=((rows, wide), bf16),
        grad_out_b=((rows, wide), bf16),
        grad_hidden=((rows, c.hidden), bf16),
        temp=((rows, wide), f32),
        grad_middle=((rows, wide), f32),
        grad_branch=((rows, wide), bf16),
        grad_merged=((rows, wide), bf16),
        grad_packed=((rows, 3 * wide), bf16),
        grad_in=((rows, wide), f32),
        sums=((2, 8, 6 * wide), f32),
        grad_mod=((2, 6 * wide), f32),
        heads_in=((wide, LANES), bf16),
        heads_out=((LANES, wide), bf16),
    )


KEPT = (N.packed, N.merged, N.branch, N.middle, N.hidden, N.out_branch)
TERMS = (
    N.mixed_a,
    N.grad_packed,
    N.merged,
    N.grad_branch,
    N.mixed_b,
    N.grad_hidden,
    N.active,
    N.grad_out_b,
)


class Traffic:
    def __init__(self, sems):
        self.sems, self.used, self.pending = sems, 0, {}

    def start(self, name, src, dst):
        copy = pltpu.make_async_copy(src, dst, self.sems.at[self.used])
        self.used += 1
        copy.start()
        self.pending[name] = copy

    def wait(self, name):
        if name in self.pending:
            self.pending.pop(name).wait()

    def drain(self):
        for name in list(self.pending):
            self.wait(name)


def run_forward(c, r, t, temporal, put, weight_wait):
    t.wait(N.mod)
    t.wait(N.x)
    forward_a(c, r)
    put(N.mixed_a)
    weight_wait(0)
    forward_qkv(c, r)
    put(N.packed)
    if temporal:
        fill_heads(c, r)
        temporal_merge(c, r)
    else:
        spatial_merge(c, r)
    put(N.merged)
    forward_b(c, r)
    put(N.branch)
    put(N.middle)
    put(N.mixed_b)
    weight_wait(1)
    forward_mlp(c, r, weight_wait)
    put(N.hidden)
    put(N.active)
    put(N.out_branch)
    forward_end(c, r)
    put(N.acts)
    put(N.send)


def spatial_forward_kernel(c, micro, names, refs):
    h = Refs(names_hbm(names, refs))
    r = h.vmem
    first = N.near in h
    r[N.w] = h.near if first else h.w
    copies = weight_copies(c, h.w, h.near, r.wsem) if first else []
    for copy in copies:
        copy.start()

    @pl.when(h.ctl[0] == 0)
    def _():
        t = Traffic(r.sems)
        t.start(N.x, h.x.at[micro], r.x)
        t.start(N.mod, h.mod.at[micro], r.mod)
        fill_given(c, h.ctl, r)

        def put(name):
            if name in KEPT or name == N.send:
                t.start(name, r[name], h[name])
            elif name == N.acts:
                t.start(name, r.acts, h.acts.at[micro])

        def weight_wait(part):
            if first:
                copies[part].wait()

        run_forward(c, r, t, False, put, weight_wait)
        t.drain()

    if first:

        @pl.when(h.ctl[0] != 0)
        def _():
            for copy in copies:
                copy.wait()


def temporal_kernel(c, micro, names, refs):
    h = Refs(names_hbm(names, refs))
    r = h.vmem

    @pl.when(h.ctl[0] == 1)
    def _():
        t = Traffic(r.sems)
        r.update(x=h.x, w=h.w)
        t.start(N.mod, h.mod.at[micro], r.mod)
        t.start(N.grad, h.cot.at[micro], r.grad)
        fill_given(c, h.ctl, r)
        forward = Refs({k: v for k, v in r.items() if k != N.send})
        put = partial(put_backward, c, micro, h, r, t)
        run_forward(
            c,
            forward,
            t,
            True,
            lambda name: name == N.send or put(name),
            lambda part: None,
        )
        t.wait(N.grad)
        r.sums[...] = jnp.zeros_like(r.sums)
        backward_first(c, r, t, True, put)
        backward_second(c, r, t, True, put)
        t.drain()


def put_backward(c, micro, h, r, t, name):
    if name == N.send:
        if N.send in h:
            t.start(N.send, r.send, h.send)
    elif name in (N.acts, N.grad_in):
        t.start(name, r[name], h[name].at[micro])
    elif name in (N.late_sums, N.early_sums):
        early = 2 * c.width
        cols = pl.ds(0, early) if name == N.early_sums else pl.ds(early, 2 * early)
        t.start(name, r.grad_mod.at[:, cols], h.grad_mod.at[micro, :, cols])
    elif name in TERMS:
        t.start(name, r[name], h[name].at[pl.ds(micro * c.rows, c.rows), :])


def backward_first(c, r, t, temporal, put):
    backward_mlp(c, r, not temporal, put)
    put(N.grad_hidden)
    if not temporal:
        put(N.active)
    t.wait(N.middle)
    t.wait(N.branch)
    backward_mid(c, r, not temporal)
    put(N.grad_branch)
    if not temporal:
        put(N.mixed_b)
    put_sums(c, r, 2, 6)
    put(N.late_sums)


def backward_second(c, r, t, temporal, put):
    if temporal:
        temporal_back(c, r)
    else:
        spatial_back(c, r)
    put(N.grad_packed)
    t.wait(N.x)
    backward_end(c, r, not temporal)
    if not temporal:
        put(N.mixed_a)
    put(N.send)
    put(N.grad_in)
    put_sums(c, r, 0, 2)
    put(N.early_sums)


def put_sums(c, r, first, last):
    cols = slice(first * c.width, last * c.width)
    r.grad_mod[:, cols] = jnp.sum(r.sums[:, :, cols], axis=1)


def spatial_backward_kernel(c, micro, names, refs):
    h = Refs(names_hbm(names, refs))
    r = h.vmem

    @pl.when(h.ctl[0] == 0)
    def _():
        t = Traffic(r.sems)
        r.update(grad=h.grad, w=h.w)
        t.start(N.mod, h.mod.at[micro], r.mod)
        t.start(N.out_branch, h.out_branch, r.out_branch)
        t.start(N.hidden, h.hidden, r.hidden)
        t.start(N.middle, h.middle, r.middle)
        t.start(N.branch, h.branch, r.branch)
        t.start(N.packed, h.packed, r.packed)
        t.start(N.kept, h.kept, r.merged)
        t.start(N.x, h.x.at[micro], r.x)
        fill_given(c, h.ctl, r)
        r.sums[...] = jnp.zeros_like(r.sums)
        for name in (N.mod, N.out_branch, N.hidden):
            t.wait(name)
        put = partial(put_backward, c, micro, h, r, t)
        backward_first(c, r, t, False, put)
        t.wait(N.packed)
        t.wait(N.kept)
        put(N.merged)
        backward_second(c, r, t, False, put)
        t.drain()


def spatial_first_kernel(c, micro, names, refs):
    h = Refs(names_hbm(names, refs))
    r = h.vmem

    @pl.when(h.ctl[0] == 0)
    def _():
        t = Traffic(r.sems)
        r.update(grad=h.grad, w=h.w)
        t.start(N.mod, h.mod.at[micro], r.mod)
        t.start(N.out_branch, h.out_branch, r.out_branch)
        t.start(N.hidden, h.hidden, r.hidden)
        t.start(N.middle, h.middle, r.middle)
        t.start(N.branch, h.branch, r.branch)
        t.start(N.kept, h.kept, r.merged)
        fill_given(c, h.ctl, r)
        r.sums[...] = jnp.zeros_like(r.sums)
        for name in (N.mod, N.out_branch, N.hidden):
            t.wait(name)
        put = partial(put_backward, c, micro, h, r, t)
        t.wait(N.kept)
        put(N.merged)
        backward_first(c, r, t, False, put)
        t.start(N.grad_middle, r.grad_middle, h.grad_middle)
        t.start(N.grad_merged, r.grad_merged, h.grad_merged)
        t.drain()


def spatial_second_kernel(c, micro, names, refs):
    h = Refs(names_hbm(names, refs))
    r = h.vmem

    @pl.when(h.ctl[0] == 0)
    def _():
        t = Traffic(r.sems)
        r.update(w=h.w)
        for name in (N.packed, N.grad_merged):
            t.start(name, h[name], r[name])
        t.start(N.x, h.x.at[micro], r.x)
        t.start(N.mod, h.mod.at[micro], r.mod)
        t.start(N.grad_middle, h.grad_middle, r.grad_middle)
        fill_given(c, h.ctl, r)
        r.sums[...] = jnp.zeros_like(r.sums)
        for name in (N.packed, N.grad_merged, N.grad_middle, N.mod):
            t.wait(name)
        put = partial(put_backward, c, micro, h, r, t)
        backward_second(c, r, t, False, put)
        t.drain()


def names_hbm(names, refs):
    outer, inner = names
    found = dict(zip(outer, refs[: len(outer)], strict=True))
    found[N.vmem] = Refs(zip(inner, refs[len(outer) :], strict=True))
    return found


def vmem_bytes(scratch):
    sizes = [
        math.prod(v.shape) * jnp.dtype(v.dtype).itemsize
        for v in scratch
        if v.memory_space == pltpu.VMEM
    ]
    return sum(sizes) + SPARE_BYTES


def call(c, kernel, micro, operands, news, alias, scratch, flops):
    ins = list(operands)
    outs = list(alias) + list(news)
    shapes = [pltpu.HBM(operands[n].shape, operands[n].dtype) for n in alias]
    shapes += [
        (pltpu.VMEM if n == N.near else jax.ShapeDtypeStruct if n == N.send else pltpu.HBM)(*news[n])
        for n in news
    ]
    table = sizes(c)
    inner = {n: pltpu.VMEM(*table[n]) for n in scratch}
    if N.near in news:
        inner[N.wsem] = pltpu.SemaphoreType.DMA((3,))
    inner[N.sems] = pltpu.SemaphoreType.DMA((32,))
    in_names = [n if n not in alias else "_" + n for n in ins]
    names = (in_names + outs, list(inner))
    places = {N.ctl: pltpu.SMEM, N.grad: pltpu.VMEM}
    if N.near not in news:
        places[N.w] = pltpu.VMEM
    if kernel is temporal_kernel:
        places[N.x] = pltpu.VMEM
    got = pl.pallas_call(
        lambda *refs: kernel(c, micro, names, refs),
        out_shape=shapes,
        in_specs=[
            pl.BlockSpec(memory_space=places.get(n, pl.ANY)) for n in ins
        ],
        out_specs=[
            pl.BlockSpec(memory_space=pltpu.VMEM if n == N.near else pl.ANY) for n in outs
        ],
        scratch_shapes=list(inner.values()),
        input_output_aliases={ins.index(n): i for i, n in enumerate(alias)},
        compiler_params=pltpu.CompilerParams(
            vmem_limit_bytes=vmem_bytes(inner.values()) + EXTRA_BYTES * (kernel is temporal_kernel)
        ),
        cost_estimate=pl.CostEstimate(flops=flops, bytes_accessed=20_000_000, transcendentals=0),
    )(*operands.values())
    return dict(zip(outs, got, strict=True))


FIRST = (N.merged, N.grad_branch, N.mixed_b, N.grad_hidden, N.active, N.grad_out_b)
SECOND = (N.mixed_b, N.grad_hidden, N.mixed_a, N.grad_packed)
LEAD = 2


def group_rows(c):
    return ((c.ratio + 1) * c.own, (c.ratio - LEAD + 3) * c.own, LEAD * c.own)


def gradients_kernel(c, ring, order, place, *refs):
    made = (0, 2) if order == FIRST else (1,)
    each = (4, 4, 2) if ring else (1, 1, 1)
    count, outs = len(order), sum(each[g] for g in made)
    held = Refs(zip(order, refs[count + outs : 2 * count + outs], strict=True))
    turned, slots, in_sems, out_sems = refs[2 * count + outs :]
    sources = dict(zip(order, refs, strict=False))
    lead = LEAD * c.width
    needed = pl.ds(0, lead) if order == FIRST else pl.ds(lead, c.hidden - lead)
    sources[N.grad_hidden] = sources[N.grad_hidden].at[:, needed]
    copies = {
        n: pltpu.make_async_copy(sources[n], held[n], in_sems.at[i]) for i, n in enumerate(order)
    }
    for copy in copies.values():
        copy.start()
    own, step, line = c.own, c.blocks // c.ratio, c.blocks // 4
    out, at = {}, count
    for g in made:
        out[g] = refs[at : at + each[g]]
        at += each[g]

    def puts(slot, group, j, tall=False):
        ref = slots.at[slot]
        if tall:
            ref = ref.reshape(step, c.ratio * own, c.width)
        if not ring:
            rows = pl.ds(j * step, step) if tall else pl.ds(0, c.blocks)
            part = pl.ds(0, c.ratio * own) if tall else pl.ds(j * own, own)
            yield pltpu.make_async_copy(ref, out[group][0].at[rows, part, :], out_sems.at[slot, 0])
            return
        if tall:
            ref = ref.reshape(2, 2, c.ratio * own, c.width)
            places, rows = j, pl.ds(0, c.ratio * own)
        else:
            ref = ref.reshape(line, 2, 2, own, c.width)
            places, rows = slice(None), pl.ds(j * own, own)
        for i, (x, core) in enumerate(((0, 0), (1, 0), (0, 1), (1, 1))):
            at = ((place[0] + x) % 2, (place[1] + core) % 2)
            src = ref.at[at] if tall else ref.at[:, at[0], at[1]]
            if group == 2:
                dst = out[group][core].at[places, x, rows, :]
            else:
                dst = out[group][i].at[places, rows, :]
            yield pltpu.make_async_copy(src, dst, out_sems.at[slot, i])

    def product(left, right, dims, *target):
        slots[target[0]] = mm(left, right, dims).astype(bf16).reshape(slots.shape[1:])
        for copy in puts(*target):
            copy.start()

    rest = c.ratio - LEAD
    if order == FIRST:
        last = c.ratio + LEAD
        copies[N.merged].wait()
        copies[N.grad_branch].wait()
        product(held.merged[...], held.grad_branch[...], TN, last, 0, c.ratio)
        copies[N.mixed_b].wait()
        turned[...] = held.mixed_b[...].T
        copies[N.grad_hidden].wait()

        @pl.loop(0, LEAD)
        def _(j):
            product(turned[...], held.grad_hidden[:, columns(c, j)], NN, c.ratio + j, 2, j)

        copies[N.active].wait()
        copies[N.grad_out_b].wait()

        @pl.loop(0, c.ratio)
        def _(j):
            product(held.active[:, columns(c, j)], held.grad_out_b[...], TN, j, 0, j, True)

        targets = [(j, 0, j, True) for j in range(c.ratio)] + [(last, 0, c.ratio)]
        targets += [(c.ratio + j, 2, j) for j in range(LEAD)]
    else:
        copies[N.mixed_b].wait()
        turned[...] = held.mixed_b[...].T
        copies[N.grad_hidden].wait()

        @pl.loop(0, rest)
        def _(j):
            product(turned[...], held.grad_hidden[:, columns(c, j)], NN, j, 1, j)

        copies[N.mixed_a].wait()
        turned[...] = held.mixed_a[...].T
        copies[N.grad_packed].wait()

        @pl.loop(0, 3)
        def _(j):
            product(turned[...], held.grad_packed[:, columns(c, j)], NN, rest + j, 1, rest + j)

        targets = [(j, 1, j) for j in range(rest + 3)]
    for target in targets:
        for copy in puts(*target):
            copy.wait()


def weight_gradients(c, ring, order, place, terms):
    made = (0, 2) if order == FIRST else (1,)
    jobs = c.ratio + LEAD + 1 if order == FIRST else c.ratio - LEAD + 3
    shapes = [terms[n].shape for n in order]
    lead = LEAD * c.width
    at = order.index(N.grad_hidden)
    shapes[at] = (shapes[at][0], lead if order == FIRST else c.hidden - lead)
    line, each = (c.blocks // 4, (4, 4, 2)) if ring else (c.blocks, (1, 1, 1))
    out = []
    for group in made:
        shape = (line, group_rows(c)[group], c.width)
        if ring and group == 2:
            shape = (line, 2) + shape[1:]
        plain = jax.ShapeDtypeStruct(shape, bf16)
        if ring and group == 0:
            out += [pltpu.HBM(shape, bf16), plain, pltpu.HBM(shape, bf16), plain]
        else:
            out += [plain] * each[group]
    scratch = [pltpu.VMEM(s, bf16) for s in shapes] + [
        pltpu.VMEM((c.width, shapes[0][0]), bf16),
        pltpu.VMEM((jobs, c.blocks, c.own, c.width), bf16),
        pltpu.SemaphoreType.DMA((len(order),)),
        pltpu.SemaphoreType.DMA((jobs, 4)),
    ]
    got = pl.pallas_call(
        partial(gradients_kernel, c, ring, order),
        out_shape=out,
        in_specs=[pl.BlockSpec(memory_space=pltpu.SMEM)]
        + [pl.BlockSpec(memory_space=pl.ANY)] * len(order),
        out_specs=[pl.BlockSpec(memory_space=pl.ANY)] * len(out),
        scratch_shapes=scratch,
        compiler_params=pltpu.CompilerParams(vmem_limit_bytes=vmem_bytes(scratch)),
        cost_estimate=pl.CostEstimate(
            flops=2 * shapes[0][0] * c.width * c.width * jobs,
            bytes_accessed=12_000_000,
            transcendentals=0,
        ),
    )(place, *[pltpu.with_memory_space_constraint(terms[n], pltpu.HBM) for n in order])
    return [got[: each[0]], got[each[0] :]] if order == FIRST else [got]


def add(*parts):
    total = parts[0].astype(f32)
    for part in parts[1:]:
        total = total + part.astype(f32)
    return total


LINE = (3, 2, 1)


def line_terms(z, *parts):
    def at(part, k):
        return lax.dynamic_index_in_dim(part, z ^ k, 0, keepdims=False)

    return [add(*[at(part, k) for part in parts]).astype(bf16) for k in (0,) + LINE]


def line_swap(terms):
    return terms[:1] + [swap(term, 4 * k) for term, k in zip(terms[1:], LINE)]


def ring_sums(first, second, z, sums):
    meet = lax.optimization_barrier
    (near0, far0, *core0), (both2, core2) = first
    far0 = add(far0, swap(core0[1], 1)).astype(bf16)
    terms2 = line_terms(z, both2, swap(core2, 1))

    far0, terms2, near_core0 = meet((far0, terms2, core0[0]))
    group1, small = second((far0, terms2))
    far0, terms2 = swap(far0, 2), line_swap(terms2)
    core0 = swap(near_core0, 1)

    far0, terms2, core0, (near1, far1, *core1), small = meet((far0, terms2, core0, group1, small))
    far_core1 = swap(core1[1], 1)
    sum2 = add(*terms2)
    other2, sum2 = sum2[1].astype(bf16), sum2[0]
    far0, far_core1, other2, sum2, small = meet((far0, far_core1, other2, sum2, small))
    terms0 = line_swap(line_terms(z, near0, core0, far0))
    far1 = swap(add(far1, far_core1).astype(bf16), 2)
    core1 = swap(core1[0], 1)
    small = gather_step(gather_step(sums(small)[None], 8), 4)

    terms0, far1, core1, small = meet((terms0, far1, core1, small))
    terms1 = line_swap(line_terms(z, near1, core1, far1))
    sum2 = sum2 + swap(other2, 2).astype(f32)
    small = gather_step(gather_step(small, 2), 1)
    return add(*terms0), add(*terms1), sum2, small


def swap(block, distance):
    count = lax.axis_size(DP)
    return lax.ppermute(block, DP, [(i, i ^ distance) for i in range(count)])


def gather_small(block):
    count = lax.axis_size(DP)
    if count & (count - 1):
        return lax.all_gather(block, DP, axis=0, tiled=False)
    held, distance = block[None], count // 2
    while distance:
        held = gather_step(held, distance)
        distance //= 2
    return held


def gather_step(held, distance):
    other = swap(held, distance)
    lower = (lax.axis_index(DP) & distance) == 0
    pair = [jnp.where(lower, held, other), jnp.where(lower, other, held)]
    return jnp.stack(pair, axis=1).reshape((-1,) + held.shape[1:])


def scatter_small(blocks):
    count = lax.axis_size(DP)
    if count & (count - 1):
        return lax.psum_scatter(blocks, DP, scatter_dimension=0, tiled=False)
    mine = lax.axis_index(DP)
    distance = 1
    while distance < count:
        low, high = blocks[0::2], blocks[1::2]
        upper = (mine & distance) != 0
        other = swap(jnp.where(upper, low, high), distance)
        blocks = jnp.where(upper, high, low) + other
        distance *= 2
    return blocks[0]


def embed_columns(steps, index, width):
    half = width // 2
    place = (index % half).astype(f32)
    frequency = jnp.exp(-math.log(10000.0) * place / half)
    angles = steps.astype(f32)[:, None] * frequency[None, :]
    wave = jnp.where((index < half)[None, :], jnp.cos(angles), jnp.sin(angles))
    return jax.nn.silu(wave).astype(bf16)


def by_blocks(w, own, width):
    return jnp.concatenate([w[:, at : at + width] for at in range(0, w.shape[1], width)])


def in_vmem(block):
    return pltpu.with_memory_space_constraint(block, pltpu.VMEM)


def from_blocks(blocks, own, width):
    starts = range(0, blocks.shape[0], own)
    return jnp.concatenate([blocks[at : at + own] for at in starts], axis=1)


def local(tokens, cotangent, boxes, timesteps, w_ada, w_qkv, w_proj, w_up, w_down):
    section = lax.axis_index(SECTION)
    group = lax.axis_size(DP)
    micro_count, _, frames, patches, width = tokens.shape
    hidden = w_up.shape[2]
    rows = frames * patches
    own = width // group
    ratio = hidden // width
    direct = own % 16 == 0 and group % ratio == 0
    ring = direct and group == 16 and ratio == 4
    c = Cfg(frames, patches, width, hidden, group if direct else ratio)

    shard = jnp.concatenate(
        [
            by_blocks(w_qkv[0].astype(bf16), own, width),
            w_proj[0].astype(bf16),
            by_blocks(w_up[0].astype(bf16), own, width),
            w_down[0].astype(bf16),
        ],
        axis=0,
    )
    weights = lax.all_gather(shard, DP, axis=0, tiled=False)
    squares = 4 + ratio
    if not direct:
        weights = jnp.concatenate(
            [
                weights[:, i * own : (i + 1) * own].reshape(c.blocks, c.own, width)
                for i in range(squares)
            ]
            + [weights[:, squares * own :].reshape(c.blocks, ratio * c.own, width)],
            axis=1,
        )

    start = lax.axis_index(DP) * own
    index = start + jnp.arange(own, dtype=jnp.int32)
    steps = gather_small(timesteps.reshape(micro_count))
    steps = jnp.concatenate([jnp.zeros((group, 1), steps.dtype), steps], axis=1)
    embed = embed_columns(steps.reshape(-1), index, width)
    modulation = jnp.dot(embed, w_ada[0].astype(bf16), preferred_element_type=f32)
    modulation = scatter_small(modulation.reshape(group, 1 + micro_count, 6 * width))
    modulation = jnp.stack(
        [jnp.stack([modulation[0], modulation[1 + m]]) for m in range(micro_count)]
    )
    ctl = [
        jnp.concatenate([section.astype(jnp.int32)[None], boxes[m].reshape(-1)])
        for m in range(micro_count)
    ]

    tokens = tokens.reshape(micro_count, rows, width)
    cotangent = cotangent.reshape(micro_count, rows, width)
    whole = ((micro_count, rows, width), f32)
    one = ((rows, width), bf16)
    flops = 2 * rows * width * width * (4 + 2 * ratio)
    table = sizes(c)

    forward_names = [
        N.x, N.mod, N.given, N.mixed_a, N.packed, N.merged, N.branch, N.middle, N.mixed_b,
        N.hidden, N.active, N.out_branch, N.acts, N.send,
    ]
    back_names = [
        N.grad, N.grad_out_b, N.grad_hidden, N.temp, N.grad_middle, N.grad_branch, N.grad_merged,
        N.grad_packed, N.grad_in, N.sums, N.grad_mod,
    ]
    kept, received = [], []
    acts = None
    for m in range(micro_count):
        operands = dict(ctl=ctl[m], x=tokens, mod=modulation, w=weights)
        if m == 0:
            operands[N.w] = pltpu.with_memory_space_constraint(weights, pltpu.HBM)
        news = dict(send=one, **{n: table[n] for n in KEPT})
        if acts is None:
            news.update(acts=whole, near=(weights.shape, bf16))
        else:
            operands[N.acts] = acts
        alias = [N.acts] if acts is not None else []
        got = call(c, spatial_forward_kernel, m, operands, news, alias, forward_names, flops)
        acts = got[N.acts]
        if m == 0:
            weights = in_vmem(got[N.near])
        kept.append(got)
        received.append(in_vmem(lax.ppermute(got[N.send], SECTION, [(0, 1)])))

    shared = None
    grads = []
    for m in range(micro_count):
        operands = dict(
            ctl=ctl[m], x=received[m], mod=modulation, w=weights, cot=cotangent, acts=acts
        )
        news = dict(send=one)
        alias = [N.acts]
        if shared is None:
            news[N.grad_in] = whole
            news[N.grad_mod] = ((micro_count, 2, 6 * width), f32)
            for n in TERMS:
                news[n] = ((micro_count * rows, table[n][0][1]), bf16)
        else:
            operands.update(shared)
            alias += list(shared)
        names = forward_names + back_names + [N.heads_in, N.heads_out]
        got = call(c, temporal_kernel, m, operands, news, alias, names, 3 * flops)
        acts = got[N.acts]
        shared = {n: got[n] for n in (N.grad_in, N.grad_mod) + TERMS}
        grads.append(in_vmem(lax.ppermute(got[N.send], SECTION, [(1, 0)])))

    dp_index = lax.axis_index(DP)
    place = jnp.stack([dp_index // 2 % 2, dp_index % 2]).astype(jnp.int32)
    names = [n for n in forward_names if n not in (N.acts, N.send)] + back_names
    firsts = (N.grad_mod, N.grad_out_b, N.grad_hidden, N.active, N.mixed_b, N.grad_branch, N.merged)
    seconds = (N.grad_in, N.grad_mod, N.grad_packed, N.mixed_a)

    def operands_of(m, own_names, **more):
        got = dict(ctl=ctl[m], mod=modulation, w=weights, **more)
        for n in own_names:
            got[N.kept if n == N.merged else n] = kept[m][n]
        return got

    last = micro_count - 1
    for m in range(last):
        operands = operands_of(m, KEPT, grad=grads[m], x=tokens)
        operands.update(shared)
        shared = call(
            c, spatial_backward_kernel, m, operands, {}, list(shared), names, 2 * flops
        )
    ours = (N.out_branch, N.hidden, N.middle, N.branch, N.merged)
    operands = operands_of(last, ours, grad=grads[last])
    operands.update({n: shared[n] for n in firsts})
    news = dict(grad_middle=table[N.grad_middle], grad_merged=one)
    first_names = [
        N.mod, N.given, N.out_branch, N.hidden, N.middle, N.branch, N.merged, N.mixed_b, N.active,
        N.grad_out_b, N.grad_hidden, N.temp, N.grad_middle, N.grad_branch, N.grad_merged, N.sums,
        N.grad_mod,
    ]
    got = call(c, spatial_first_kernel, last, operands, news, firsts, first_names, 4 * flops // 3)
    shared.update({n: got[n] for n in firsts})
    between = {n: got[n] for n in news}
    first = weight_gradients(c, ring, FIRST, place, shared)

    def second(after):
        (grad_middle, grad_merged), _ = lax.optimization_barrier((tuple(between.values()), after))
        operands = operands_of(
            last, (N.packed,), x=tokens, grad_middle=grad_middle, grad_merged=grad_merged
        )
        operands.update({n: shared[n] for n in seconds})
        second_names = [
            N.x, N.mod, N.given, N.packed, N.mixed_a, N.temp, N.grad_middle, N.grad_merged,
            N.grad_packed, N.grad_in, N.sums, N.grad_mod,
        ]
        got = call(
            c, spatial_second_kernel, last, operands, {}, seconds, second_names, 2 * flops // 3
        )
        shared.update({n: got[n] for n in seconds})
        return weight_gradients(c, ring, SECOND, place, shared)[0], shared[N.grad_mod]

    def sums_of(grad_mod):
        given = jnp.sum(grad_mod[:, 0], axis=0, keepdims=True)
        return jnp.concatenate([given, grad_mod[:, 1]]).astype(bf16)

    if ring:
        *totals, sums = ring_sums(first, second, dp_index // 4, sums_of)
    else:
        group1, sums = second(())
        sums = gather_small(sums_of(sums))
        groups = first[0], group1, first[1]
        joined = [parts[0] for parts in groups]
        if not direct:
            tall = ratio * c.own
            joined = [
                jnp.concatenate(
                    [
                        part[:, i * c.own : (i + 1) * c.own].reshape(group, own, width)
                        for i in range(part.shape[1] // c.own)
                    ],
                    axis=1,
                )
                for part in (joined[0][:, tall:], joined[1], joined[2])
            ]
            tall = groups[0][0][:, :tall].reshape(group, ratio * own, width)
            joined[0] = jnp.concatenate([tall, joined[0]], axis=1)
        total = lax.psum_scatter(
            jnp.concatenate(joined, axis=1), DP, scatter_dimension=0, tiled=False
        ).astype(f32)
        cuts = (ratio + 1) * own, (2 * ratio + 4 - LEAD) * own
        totals = jnp.split(total, cuts)
    tall, rest = ratio * own, (ratio - LEAD) * own
    down, proj = totals[0][:tall], totals[0][tall:]
    up, qkv = jnp.concatenate([totals[2], totals[1][:rest]]), totals[1][rest:]
    grad_qkv = from_blocks(qkv, own, width)
    grad_proj = proj
    grad_up = from_blocks(up, own, width)
    grad_down = down

    sums = sums.reshape(group * (1 + micro_count), 6 * width)
    grad_ada = lax.dot_general(embed, sums, TN, preferred_element_type=f32)

    out_shape = (1, micro_count, 1, frames, patches, width)
    return (
        acts.reshape(out_shape),
        shared[N.grad_in].reshape(out_shape),
        grad_ada[None],
        grad_qkv[None],
        grad_proj[None],
        grad_up[None],
        grad_down[None],
    )


def solution(mesh):
    placed = (
        P(None, DP, None, None, None),
        P(None, DP, None, None, None),
        P(None, DP, None, None),
        P(None, DP),
        P(SECTION, DP, None),
        P(SECTION, DP, None),
        P(SECTION, DP, None),
        P(SECTION, DP, None),
        P(SECTION, DP, None),
    )
    return jax.shard_map(
        local,
        mesh=mesh,
        in_specs=placed,
        out_specs=(
            P(SECTION, None, DP, None, None, None),
            P(SECTION, None, DP, None, None, None),
            P(SECTION, DP, None),
            P(SECTION, DP, None),
            P(SECTION, DP, None),
            P(SECTION, DP, None),
            P(SECTION, DP, None),
        ),
        check_vma=False,
    )
```

```python
from functools import partial
import math

import jax
import jax.numpy as jnp
from jax import lax
from jax.experimental import pallas as pl
from jax.experimental.pallas import tpu as pltpu
from jax.sharding import PartitionSpec as P

HEAD_DIM = 64
GW = 16
LANES = 128
TILE = 64
STEP = 256
EPS = 1e-06
SPARE_BYTES = 10 * 1024 * 1024
EXTRA_BYTES = 2 * 1024 * 1024
f32 = jnp.float32
bf16 = jnp.bfloat16
NN = (((1,), (0,)), ((), ()))
NT = (((1,), (1,)), ((), ()))
TN = (((0,), (0,)), ((), ()))


def mm(a, b, dims=NN):
    return lax.dot_general(a, b, dims, preferred_element_type=f32)


def ln(v):
    centred = v - jnp.mean(v, axis=-1, keepdims=True)
    inv = lax.rsqrt(jnp.mean(centred * centred, axis=-1, keepdims=True) + EPS)
    return centred * inv, inv


def ln_back(normed, inv, grad):
    return inv * (
        grad
        - jnp.mean(grad, axis=-1, keepdims=True)
        - normed * jnp.mean(grad * normed, axis=-1, keepdims=True)
    )


def by_rows(count, body):
    @pl.loop(0, count // STEP)
    def _(i):
        body(pl.ds(pl.multiple_of(i * STEP, STEP), STEP))


def tiles(count, body):
    @pl.loop(0, count // TILE, unroll=True)
    def _(i):
        body(pl.multiple_of(i * TILE, TILE))


def columns(c, j):
    return pl.ds(pl.multiple_of(j * c.width, c.width), c.width)


class Refs(dict):
    __getattr__ = dict.__getitem__


class Names:
    def __getattr__(self, name):
        return name


N = Names()
DP, SECTION = "dp", "section"


class Cfg:
    def __init__(self, frames, patches, width, hidden, blocks):
        self.frames, self.patches, self.width, self.hidden = frames, patches, width, hidden
        self.rows = frames * patches
        self.ratio = hidden // width
        self.blocks = blocks
        self.own = width // blocks
        self.scaling = HEAD_DIM ** (-0.5)


def weight_copies(c, src, dst, sems):
    cuts = (0, 4 * c.own, (4 + c.ratio) * c.own, (4 + 2 * c.ratio) * c.own)
    parts = [pl.ds(a, b - a) for a, b in zip(cuts, cuts[1:])]
    return [
        pltpu.make_async_copy(src.at[:, part, :], dst.at[:, part, :], sems.at[i])
        for i, part in enumerate(parts)
    ]


def square(c, r, j):
    rows = pl.ds(pl.multiple_of(j * c.own, c.own), c.own)
    return r.w[:, rows, :].reshape(c.width, c.width)


def down_block(c, r, j):
    step = c.blocks // c.ratio
    block = r.w[pl.ds(j * step, step), (4 + c.ratio) * c.own :, :]
    return block.reshape(c.width, c.width)


def down_whole(c, r):
    return r.w[:, (4 + c.ratio) * c.own :, :].reshape(c.hidden, c.width)


def fill_given(c, ctl, r):
    patch = lax.broadcasted_iota(jnp.int32, (c.patches, LANES), 0)
    row, col = patch // GW, patch % GW
    for f in range(c.frames):
        top, bottom, left, right = (ctl[1 + 4 * f + i] for i in range(4))
        inside = (row >= top) & (row < bottom) & (col >= left) & (col < right)
        r.given[f * c.patches : (f + 1) * c.patches, :] = jnp.where(inside, 1.0, 0.0)


def pick(c, r, index, given):
    where = slice(index * c.width, (index + 1) * c.width)
    return jnp.where(given, r.mod[0:1, where], r.mod[1:2, where])


def is_given(r, rows):
    return r.given[rows, 0:1] > 0.5


def forward_a(c, r):
    def body(rows):
        given = is_given(r, rows)
        normed, _ = ln(r.x[rows, :].astype(f32))
        r.mixed_a[rows, :] = (normed * (1.0 + pick(c, r, 1, given)) + pick(c, r, 0, given)).astype(
            bf16
        )

    by_rows(c.rows, body)


def forward_qkv(c, r):
    @pl.loop(0, 3, unroll=True)
    def _(j):
        r.packed[:, columns(c, j)] = mm(r.mixed_a[...], square(c, r, j)).astype(bf16)


def halves(pair):
    first = lax.broadcasted_iota(jnp.int32, pair.shape, 1) < HEAD_DIM
    zero = jnp.zeros_like(pair)
    return jnp.concatenate([jnp.where(first, pair, zero), jnp.where(first, zero, pair)], axis=0)


def softmax_rows(scores):
    top = jnp.max(scores, axis=-1, keepdims=True)
    exponent = jnp.exp(scores - top)
    return exponent * (1.0 / jnp.sum(exponent, axis=-1, keepdims=True))


def spatial_tiles(c, body):
    @pl.loop(0, c.width // LANES, unroll=2)
    def _(pair):
        cols = [pl.ds(pl.multiple_of(i * c.width + pair * LANES, LANES), LANES) for i in range(3)]
        for f in range(c.frames):
            body(slice(f * c.patches, (f + 1) * c.patches), cols)


def spatial_merge(c, r):
    def body(rows, cols):
        q, k, v = (r.packed[rows, cols[i]] for i in range(3))
        shares = softmax_rows(mm(halves(q), k, NT) * c.scaling).astype(bf16)
        side = jnp.concatenate([shares[: c.patches], shares[c.patches :]], axis=1)
        r.merged[rows, cols[0]] = mm(side, halves(v)).astype(bf16)

    spatial_tiles(c, body)


def spatial_back(c, r):
    def body(rows, cols):
        q, k, v = (r.packed[rows, cols[i]] for i in range(3))
        q2, k2 = halves(q), halves(k)
        d2 = halves(r.grad_merged[rows, cols[0]])
        soft = softmax_rows(mm(q2, k, NT) * c.scaling)
        grad_shares = mm(d2, v, NT)
        inner = jnp.sum(soft * grad_shares, axis=-1, keepdims=True)
        grad_scores = (soft * (grad_shares - inner)).astype(bf16)
        side = jnp.concatenate([grad_scores[: c.patches], grad_scores[c.patches :]], axis=1)
        r.grad_packed[rows, cols[0]] = (mm(side, k2) * c.scaling).astype(bf16)
        r.grad_packed[rows, cols[1]] = (mm(grad_scores, q2, TN) * c.scaling).astype(bf16)
        r.grad_packed[rows, cols[2]] = mm(soft.astype(bf16), d2, TN).astype(bf16)

    spatial_tiles(c, body)


def fill_heads(c, r):
    lane = lax.broadcasted_iota(jnp.int32, (c.width, LANES), 0) // HEAD_DIM
    col = lax.broadcasted_iota(jnp.int32, (c.width, LANES), 1)
    r.heads_in[...] = jnp.where(lane == col, 1.0, 0.0).astype(bf16)
    col = lax.broadcasted_iota(jnp.int32, (LANES, c.width), 0)
    lane = lax.broadcasted_iota(jnp.int32, (LANES, c.width), 1) // HEAD_DIM
    r.heads_out[...] = jnp.where(lane == col, 1.0, 0.0).astype(bf16)


def head_sums(r, product):
    high = product.astype(bf16)
    low = (product - high.astype(f32)).astype(bf16)
    return mm(high, r.heads_in[...]) + mm(low, r.heads_in[...])


def frame_pairs(c):
    return [(f, g) for f in range(c.frames) for g in range(c.frames)]


def temporal_parts(c, r, ref, rows, part):
    return [
        ref[pl.ds(f * c.patches + rows, TILE), part * c.width : (part + 1) * c.width].astype(f32)
        for f in range(c.frames)
    ]


def temporal_soft(c, r, queries, keys):
    product = jnp.concatenate([queries[f] * keys[g] for f, g in frame_pairs(c)], axis=0)
    scores = head_sums(r, product) * c.scaling
    soft = []
    for f in range(c.frames):
        row = [scores[(f * c.frames + g) * TILE : (f * c.frames + g + 1) * TILE] for g in range(c.frames)]
        top = row[0]
        for entry in row[1:]:
            top = jnp.maximum(top, entry)
        exponent = [jnp.exp(entry - top) for entry in row]
        total = exponent[0]
        for entry in exponent[1:]:
            total = total + entry
        soft += [entry * (1.0 / total) for entry in exponent]
    return soft


def spread(r, columns):
    wide = mm(jnp.concatenate([v.astype(bf16) for v in columns], axis=0), r.heads_out[...])
    return [wide[i * TILE : (i + 1) * TILE] for i in range(len(columns))]


def temporal_merge(c, r):
    def body(rows):
        queries, keys, values = (temporal_parts(c, r, r.packed, rows, i) for i in range(3))
        shares = spread(r, temporal_soft(c, r, queries, keys))
        for f in range(c.frames):
            total = shares[f * c.frames] * values[0]
            for g in range(1, c.frames):
                total = total + shares[f * c.frames + g] * values[g]
            at = f * c.patches + rows
            r.merged[pl.ds(at, TILE), :] = total.astype(bf16)

    tiles(c.patches, body)


def temporal_back(c, r):
    n = c.frames

    def body(rows):
        queries, keys, values = (temporal_parts(c, r, r.packed, rows, i) for i in range(3))
        grads = temporal_parts(c, r, r.grad_merged, rows, 0)
        soft = temporal_soft(c, r, queries, keys)
        product = jnp.concatenate([grads[f] * values[g] for f, g in frame_pairs(c)], axis=0)
        wide = head_sums(r, product)
        grad_shares = [wide[i * TILE : (i + 1) * TILE] for i in range(n * n)]
        grad_scores = []
        for f in range(n):
            inner = soft[f * n] * grad_shares[f * n]
            for g in range(1, n):
                inner = inner + soft[f * n + g] * grad_shares[f * n + g]
            grad_scores += [
                soft[f * n + g] * (grad_shares[f * n + g] - inner) for g in range(n)
            ]
        shares = spread(r, soft)
        scores = spread(r, grad_scores)

        def put(frame, part, value):
            at = frame * c.patches + rows
            r.grad_packed[pl.ds(at, TILE), part * c.width : (part + 1) * c.width] = value.astype(bf16)

        for f in range(n):
            put(f, 0, sum(scores[f * n + g] * keys[g] for g in range(n)) * c.scaling)
            put(f, 1, sum(scores[g * n + f] * queries[g] for g in range(n)) * c.scaling)
            put(f, 2, sum(shares[g * n + f] * grads[g] for g in range(n)))

    tiles(c.patches, body)


def forward_b(c, r):
    r.branch[...] = mm(r.merged[...], square(c, r, 3))

    def body(rows):
        given = is_given(r, rows)
        middle = r.x[rows, :].astype(f32) + pick(c, r, 2, given) * r.branch[rows, :]
        r.middle[rows, :] = middle
        normed, _ = ln(middle)
        r.mixed_b[rows, :] = (normed * (1.0 + pick(c, r, 4, given)) + pick(c, r, 3, given)).astype(
            bf16
        )

    by_rows(c.rows, body)


GELU_A = math.sqrt(2.0 / math.pi)
GELU_B = 0.044715


def forward_mlp(c, r, weight_wait):
    @pl.loop(0, c.ratio, unroll=True)
    def _(j):
        cols = columns(c, j)
        r.hidden[:, cols] = mm(r.mixed_b[...], square(c, r, 4 + j))

        def body(rows):
            h = r.hidden[rows, cols]
            bent = jnp.tanh(GELU_A * (h + GELU_B * (h * h * h)))
            r.active[rows, cols] = (0.5 * h * (1.0 + bent)).astype(bf16)

        by_rows(c.rows, body)

    weight_wait(2)
    r.out_branch[...] = mm(r.active[...], down_whole(c, r))


def forward_end(c, r):
    def body(rows):
        given = is_given(r, rows)
        result = r.middle[rows, :] + pick(c, r, 5, given) * r.out_branch[rows, :]
        r.acts[rows, :] = result
        if N.send in r:
            r.send[rows, :] = result.astype(bf16)

    by_rows(c.rows, body)


def add_sums(c, r, index, given, value):
    cols = slice(index * c.width, (index + 1) * c.width)
    mine = jnp.where(given, value, 0.0)
    rest = jnp.where(given, 0.0, value)
    shape = (value.shape[0] // 8, 8, c.width)
    r.sums[0, :, cols] += jnp.sum(mine.reshape(shape), axis=0)
    r.sums[1, :, cols] += jnp.sum(rest.reshape(shape), axis=0)


def backward_mlp(c, r, gelu_again, put):
    def start(rows):
        given = is_given(r, rows)
        grad = r.grad[rows, :].astype(f32)
        r.grad_out_b[rows, :] = (pick(c, r, 5, given) * grad).astype(bf16)
        add_sums(c, r, 5, given, grad * r.out_branch[rows, :])

    by_rows(c.rows, start)
    put(N.grad_out_b)

    @pl.loop(0, c.ratio, unroll=True)
    def _(j):
        cols = columns(c, j)
        r.temp[...] = mm(r.grad_out_b[...], down_block(c, r, j), NT)

        def body(rows):
            h = r.hidden[rows, cols]
            square_h = h * h
            bent = jnp.tanh(GELU_A * (h + GELU_B * (square_h * h)))
            slope = 0.5 * (1.0 + bent) + 0.5 * h * (1.0 - bent * bent) * (
                GELU_A * (1.0 + 3.0 * GELU_B * square_h)
            )
            r.grad_hidden[rows, cols] = (r.temp[rows, :] * slope).astype(bf16)
            if gelu_again:
                r.active[rows, cols] = (0.5 * h * (1.0 + bent)).astype(bf16)

        by_rows(c.rows, body)

    total = 0.0
    for j in range(c.ratio):
        block = r.grad_hidden[:, j * c.width : (j + 1) * c.width]
        total = total + mm(block, square(c, r, 4 + j), NT)
    r.temp[...] = total


def backward_mid(c, r, mix_again):
    def body(rows):
        given = is_given(r, rows)
        normed, inv = ln(r.middle[rows, :])
        scale = 1.0 + pick(c, r, 4, given)
        if mix_again:
            r.mixed_b[rows, :] = (normed * scale + pick(c, r, 3, given)).astype(bf16)
        grad_mixed = r.temp[rows, :]
        middle = r.grad[rows, :].astype(f32) + ln_back(normed, inv, grad_mixed * scale)
        r.grad_middle[rows, :] = middle
        r.grad_branch[rows, :] = (pick(c, r, 2, given) * middle).astype(bf16)
        add_sums(c, r, 3, given, grad_mixed)
        add_sums(c, r, 4, given, grad_mixed * normed)
        add_sums(c, r, 2, given, middle * r.branch[rows, :])

    by_rows(c.rows, body)
    r.grad_merged[...] = mm(
        r.grad_branch[...], square(c, r, 3), NT
    ).astype(bf16)


def backward_end(c, r, mix_again):
    total = 0.0
    for j in range(3):
        block = r.grad_packed[:, j * c.width : (j + 1) * c.width]
        total = total + mm(block, square(c, r, j), NT)
    r.temp[...] = total

    def body(rows):
        given = is_given(r, rows)
        normed, inv = ln(r.x[rows, :].astype(f32))
        scale = 1.0 + pick(c, r, 1, given)
        if mix_again:
            r.mixed_a[rows, :] = (normed * scale + pick(c, r, 0, given)).astype(bf16)
        grad_mixed = r.temp[rows, :]
        result = r.grad_middle[rows, :] + ln_back(normed, inv, grad_mixed * scale)
        r.grad_in[rows, :] = result
        if N.send in r:
            r.send[rows, :] = result.astype(bf16)
        add_sums(c, r, 0, given, grad_mixed)
        add_sums(c, r, 1, given, grad_mixed * normed)

    by_rows(c.rows, body)


def sizes(c):
    wide, rows = c.width, c.rows
    return dict(
        x=((rows, wide), bf16),
        mod=((2, 6 * wide), f32),
        given=((rows, LANES), f32),
        mixed_a=((rows, wide), bf16),
        packed=((rows, 3 * wide), bf16),
        merged=((rows, wide), bf16),
        branch=((rows, wide), f32),
        middle=((rows, wide), f32),
        mixed_b=((rows, wide), bf16),
        hidden=((rows, c.hidden), f32),
        active=((rows, c.hidden), bf16),
        out_branch=((rows, wide), f32),
        acts=((rows, wide), f32),
        send=((rows, wide), bf16),
        grad=((rows, wide), bf16),
        grad_out_b=((rows, wide), bf16),
        grad_hidden=((rows, c.hidden), bf16),
        temp=((rows, wide), f32),
        grad_middle=((rows, wide), f32),
        grad_branch=((rows, wide), bf16),
        grad_merged=((rows, wide), bf16),
        grad_packed=((rows, 3 * wide), bf16),
        grad_in=((rows, wide), f32),
        sums=((2, 8, 6 * wide), f32),
        grad_mod=((2, 6 * wide), f32),
        heads_in=((wide, LANES), bf16),
        heads_out=((LANES, wide), bf16),
    )


KEPT = (N.packed, N.merged, N.branch, N.middle, N.hidden, N.out_branch)
TERMS = (
    N.mixed_a,
    N.grad_packed,
    N.merged,
    N.grad_branch,
    N.mixed_b,
    N.grad_hidden,
    N.active,
    N.grad_out_b,
)


class Traffic:
    def __init__(self, sems):
        self.sems, self.used, self.pending = sems, 0, {}

    def start(self, name, src, dst):
        copy = pltpu.make_async_copy(src, dst, self.sems.at[self.used])
        self.used += 1
        copy.start()
        self.pending[name] = copy

    def wait(self, name):
        if name in self.pending:
            self.pending.pop(name).wait()

    def drain(self):
        for name in list(self.pending):
            self.wait(name)


def run_forward(c, r, t, temporal, put, weight_wait):
    t.wait(N.mod)
    t.wait(N.x)
    forward_a(c, r)
    put(N.mixed_a)
    weight_wait(0)
    forward_qkv(c, r)
    put(N.packed)
    if temporal:
        fill_heads(c, r)
        temporal_merge(c, r)
    else:
        spatial_merge(c, r)
    put(N.merged)
    forward_b(c, r)
    put(N.branch)
    put(N.middle)
    put(N.mixed_b)
    weight_wait(1)
    forward_mlp(c, r, weight_wait)
    put(N.hidden)
    put(N.active)
    put(N.out_branch)
    forward_end(c, r)
    put(N.acts)
    put(N.send)


def spatial_forward_kernel(c, micro, names, refs):
    h = Refs(names_hbm(names, refs))
    r = h.vmem
    first = N.near in h
    r[N.w] = h.near if first else h.w
    copies = weight_copies(c, h.w, h.near, r.wsem) if first else []
    for copy in copies:
        copy.start()

    @pl.when(h.ctl[0] == 0)
    def _():
        t = Traffic(r.sems)
        t.start(N.x, h.x.at[micro], r.x)
        t.start(N.mod, h.mod.at[micro], r.mod)
        fill_given(c, h.ctl, r)

        def put(name):
            if name in KEPT or name == N.send:
                t.start(name, r[name], h[name])
            elif name == N.acts:
                t.start(name, r.acts, h.acts.at[micro])

        def weight_wait(part):
            if first:
                copies[part].wait()

        run_forward(c, r, t, False, put, weight_wait)
        t.drain()

    if first:

        @pl.when(h.ctl[0] != 0)
        def _():
            for copy in copies:
                copy.wait()


def temporal_kernel(c, micro, names, refs):
    h = Refs(names_hbm(names, refs))
    r = h.vmem

    @pl.when(h.ctl[0] == 1)
    def _():
        t = Traffic(r.sems)
        r.update(x=h.x, w=h.w)
        t.start(N.mod, h.mod.at[micro], r.mod)
        t.start(N.grad, h.cot.at[micro], r.grad)
        fill_given(c, h.ctl, r)
        forward = Refs({k: v for k, v in r.items() if k != N.send})
        put = partial(put_backward, c, micro, h, r, t)
        run_forward(
            c,
            forward,
            t,
            True,
            lambda name: name == N.send or put(name),
            lambda part: None,
        )
        t.wait(N.grad)
        r.sums[...] = jnp.zeros_like(r.sums)
        backward_first(c, r, t, True, put)
        backward_second(c, r, t, True, put)
        t.drain()


def put_backward(c, micro, h, r, t, name):
    if name == N.send:
        if N.send in h:
            t.start(N.send, r.send, h.send)
    elif name in (N.acts, N.grad_in):
        t.start(name, r[name], h[name].at[micro])
    elif name in (N.late_sums, N.early_sums):
        early = 2 * c.width
        cols = pl.ds(0, early) if name == N.early_sums else pl.ds(early, 2 * early)
        t.start(name, r.grad_mod.at[:, cols], h.grad_mod.at[micro, :, cols])
    elif name in TERMS:
        t.start(name, r[name], h[name].at[pl.ds(micro * c.rows, c.rows), :])


def backward_first(c, r, t, temporal, put):
    backward_mlp(c, r, not temporal, put)
    put(N.grad_hidden)
    if not temporal:
        put(N.active)
    t.wait(N.middle)
    t.wait(N.branch)
    backward_mid(c, r, not temporal)
    put(N.grad_branch)
    if not temporal:
        put(N.mixed_b)
    put_sums(c, r, 2, 6)
    put(N.late_sums)


def backward_second(c, r, t, temporal, put):
    if temporal:
        temporal_back(c, r)
    else:
        spatial_back(c, r)
    put(N.grad_packed)
    t.wait(N.x)
    backward_end(c, r, not temporal)
    if not temporal:
        put(N.mixed_a)
    put(N.send)
    put(N.grad_in)
    put_sums(c, r, 0, 2)
    put(N.early_sums)


def put_sums(c, r, first, last):
    cols = slice(first * c.width, last * c.width)
    r.grad_mod[:, cols] = jnp.sum(r.sums[:, :, cols], axis=1)


def spatial_backward_kernel(c, micro, names, refs):
    h = Refs(names_hbm(names, refs))
    r = h.vmem

    @pl.when(h.ctl[0] == 0)
    def _():
        t = Traffic(r.sems)
        r.update(grad=h.grad, w=h.w)
        t.start(N.mod, h.mod.at[micro], r.mod)
        t.start(N.out_branch, h.out_branch, r.out_branch)
        t.start(N.hidden, h.hidden, r.hidden)
        t.start(N.middle, h.middle, r.middle)
        t.start(N.branch, h.branch, r.branch)
        t.start(N.packed, h.packed, r.packed)
        t.start(N.kept, h.kept, r.merged)
        t.start(N.x, h.x.at[micro], r.x)
        fill_given(c, h.ctl, r)
        r.sums[...] = jnp.zeros_like(r.sums)
        for name in (N.mod, N.out_branch, N.hidden):
            t.wait(name)
        put = partial(put_backward, c, micro, h, r, t)
        backward_first(c, r, t, False, put)
        t.wait(N.packed)
        t.wait(N.kept)
        put(N.merged)
        backward_second(c, r, t, False, put)
        t.drain()


def spatial_first_kernel(c, micro, names, refs):
    h = Refs(names_hbm(names, refs))
    r = h.vmem

    @pl.when(h.ctl[0] == 0)
    def _():
        t = Traffic(r.sems)
        r.update(grad=h.grad, w=h.w)
        t.start(N.mod, h.mod.at[micro], r.mod)
        t.start(N.out_branch, h.out_branch, r.out_branch)
        t.start(N.hidden, h.hidden, r.hidden)
        t.start(N.middle, h.middle, r.middle)
        t.start(N.branch, h.branch, r.branch)
        t.start(N.kept, h.kept, r.merged)
        fill_given(c, h.ctl, r)
        r.sums[...] = jnp.zeros_like(r.sums)
        for name in (N.mod, N.out_branch, N.hidden):
            t.wait(name)
        put = partial(put_backward, c, micro, h, r, t)
        t.wait(N.kept)
        put(N.merged)
        backward_first(c, r, t, False, put)
        t.start(N.grad_middle, r.grad_middle, h.grad_middle)
        t.start(N.grad_merged, r.grad_merged, h.grad_merged)
        t.drain()


def spatial_second_kernel(c, micro, names, refs):
    h = Refs(names_hbm(names, refs))
    r = h.vmem

    @pl.when(h.ctl[0] == 0)
    def _():
        t = Traffic(r.sems)
        r.update(w=h.w)
        for name in (N.packed, N.grad_merged):
            t.start(name, h[name], r[name])
        t.start(N.x, h.x.at[micro], r.x)
        t.start(N.mod, h.mod.at[micro], r.mod)
        t.start(N.grad_middle, h.grad_middle, r.grad_middle)
        fill_given(c, h.ctl, r)
        r.sums[...] = jnp.zeros_like(r.sums)
        for name in (N.packed, N.grad_merged, N.grad_middle, N.mod):
            t.wait(name)
        put = partial(put_backward, c, micro, h, r, t)
        backward_second(c, r, t, False, put)
        t.drain()


def names_hbm(names, refs):
    outer, inner = names
    found = dict(zip(outer, refs[: len(outer)], strict=True))
    found[N.vmem] = Refs(zip(inner, refs[len(outer) :], strict=True))
    return found


def vmem_bytes(scratch):
    sizes = [
        math.prod(v.shape) * jnp.dtype(v.dtype).itemsize
        for v in scratch
        if v.memory_space == pltpu.VMEM
    ]
    return sum(sizes) + SPARE_BYTES


def call(c, kernel, micro, operands, news, alias, scratch, flops):
    ins = list(operands)
    outs = list(alias) + list(news)
    shapes = [pltpu.HBM(operands[n].shape, operands[n].dtype) for n in alias]
    shapes += [
        (pltpu.VMEM if n == N.near else jax.ShapeDtypeStruct if n == N.send else pltpu.HBM)(*news[n])
        for n in news
    ]
    table = sizes(c)
    inner = {n: pltpu.VMEM(*table[n]) for n in scratch}
    if N.near in news:
        inner[N.wsem] = pltpu.SemaphoreType.DMA((3,))
    inner[N.sems] = pltpu.SemaphoreType.DMA((32,))
    in_names = [n if n not in alias else "_" + n for n in ins]
    names = (in_names + outs, list(inner))
    places = {N.ctl: pltpu.SMEM, N.grad: pltpu.VMEM}
    if N.near not in news:
        places[N.w] = pltpu.VMEM
    if kernel is temporal_kernel:
        places[N.x] = pltpu.VMEM
    got = pl.pallas_call(
        lambda *refs: kernel(c, micro, names, refs),
        out_shape=shapes,
        in_specs=[
            pl.BlockSpec(memory_space=places.get(n, pl.ANY)) for n in ins
        ],
        out_specs=[
            pl.BlockSpec(memory_space=pltpu.VMEM if n == N.near else pl.ANY) for n in outs
        ],
        scratch_shapes=list(inner.values()),
        input_output_aliases={ins.index(n): i for i, n in enumerate(alias)},
        compiler_params=pltpu.CompilerParams(
            vmem_limit_bytes=vmem_bytes(inner.values()) + EXTRA_BYTES * (kernel is temporal_kernel)
        ),
        cost_estimate=pl.CostEstimate(flops=flops, bytes_accessed=20_000_000, transcendentals=0),
    )(*operands.values())
    return dict(zip(outs, got, strict=True))


FIRST = (N.merged, N.grad_branch, N.mixed_b, N.grad_hidden, N.active, N.grad_out_b)
SECOND = (N.mixed_b, N.grad_hidden, N.mixed_a, N.grad_packed)
LEAD = 2


def group_rows(c):
    return ((c.ratio + 1) * c.own, (c.ratio - LEAD + 3) * c.own, LEAD * c.own)


def gradients_kernel(c, ring, order, place, *refs):
    made = (0, 2) if order == FIRST else (1,)
    each = (4, 4, 2) if ring else (1, 1, 1)
    count, outs = len(order), sum(each[g] for g in made)
    held = Refs(zip(order, refs[count + outs : 2 * count + outs], strict=True))
    turned, slots, in_sems, out_sems = refs[2 * count + outs :]
    sources = dict(zip(order, refs, strict=False))
    lead = LEAD * c.width
    needed = pl.ds(0, lead) if order == FIRST else pl.ds(lead, c.hidden - lead)
    sources[N.grad_hidden] = sources[N.grad_hidden].at[:, needed]
    copies = {
        n: pltpu.make_async_copy(sources[n], held[n], in_sems.at[i]) for i, n in enumerate(order)
    }
    for copy in copies.values():
        copy.start()
    own, step, line = c.own, c.blocks // c.ratio, c.blocks // 4
    out, at = {}, count
    for g in made:
        out[g] = refs[at : at + each[g]]
        at += each[g]

    def puts(slot, group, j, tall=False):
        ref = slots.at[slot]
        if tall:
            ref = ref.reshape(step, c.ratio * own, c.width)
        if not ring:
            rows = pl.ds(j * step, step) if tall else pl.ds(0, c.blocks)
            part = pl.ds(0, c.ratio * own) if tall else pl.ds(j * own, own)
            yield pltpu.make_async_copy(ref, out[group][0].at[rows, part, :], out_sems.at[slot, 0])
            return
        if tall:
            ref = ref.reshape(2, 2, c.ratio * own, c.width)
            places, rows = j, pl.ds(0, c.ratio * own)
        else:
            ref = ref.reshape(line, 2, 2, own, c.width)
            places, rows = slice(None), pl.ds(j * own, own)
        for i, (x, core) in enumerate(((0, 0), (1, 0), (0, 1), (1, 1))):
            at = ((place[0] + x) % 2, (place[1] + core) % 2)
            src = ref.at[at] if tall else ref.at[:, at[0], at[1]]
            if group == 2:
                dst = out[group][core].at[places, x, rows, :]
            else:
                dst = out[group][i].at[places, rows, :]
            yield pltpu.make_async_copy(src, dst, out_sems.at[slot, i])

    def product(left, right, dims, *target):
        slots[target[0]] = mm(left, right, dims).astype(bf16).reshape(slots.shape[1:])
        for copy in puts(*target):
            copy.start()

    rest = c.ratio - LEAD
    if order == FIRST:
        last = c.ratio + LEAD
        copies[N.merged].wait()
        copies[N.grad_branch].wait()
        product(held.merged[...], held.grad_branch[...], TN, last, 0, c.ratio)
        copies[N.mixed_b].wait()
        turned[...] = held.mixed_b[...].T
        copies[N.grad_hidden].wait()

        @pl.loop(0, LEAD)
        def _(j):
            product(turned[...], held.grad_hidden[:, columns(c, j)], NN, c.ratio + j, 2, j)

        copies[N.active].wait()
        copies[N.grad_out_b].wait()

        @pl.loop(0, c.ratio)
        def _(j):
            product(held.active[:, columns(c, j)], held.grad_out_b[...], TN, j, 0, j, True)

        targets = [(j, 0, j, True) for j in range(c.ratio)] + [(last, 0, c.ratio)]
        targets += [(c.ratio + j, 2, j) for j in range(LEAD)]
    else:
        copies[N.mixed_b].wait()
        turned[...] = held.mixed_b[...].T
        copies[N.grad_hidden].wait()

        @pl.loop(0, rest)
        def _(j):
            product(turned[...], held.grad_hidden[:, columns(c, j)], NN, j, 1, j)

        copies[N.mixed_a].wait()
        turned[...] = held.mixed_a[...].T
        copies[N.grad_packed].wait()

        @pl.loop(0, 3)
        def _(j):
            product(turned[...], held.grad_packed[:, columns(c, j)], NN, rest + j, 1, rest + j)

        targets = [(j, 1, j) for j in range(rest + 3)]
    for target in targets:
        for copy in puts(*target):
            copy.wait()


def weight_gradients(c, ring, order, place, terms):
    made = (0, 2) if order == FIRST else (1,)
    jobs = c.ratio + LEAD + 1 if order == FIRST else c.ratio - LEAD + 3
    shapes = [terms[n].shape for n in order]
    lead = LEAD * c.width
    at = order.index(N.grad_hidden)
    shapes[at] = (shapes[at][0], lead if order == FIRST else c.hidden - lead)
    line, each = (c.blocks // 4, (4, 4, 2)) if ring else (c.blocks, (1, 1, 1))
    out = []
    for group in made:
        shape = (line, group_rows(c)[group], c.width)
        if ring and group == 2:
            shape = (line, 2) + shape[1:]
        plain = jax.ShapeDtypeStruct(shape, bf16)
        if ring and group == 0:
            out += [pltpu.HBM(shape, bf16), plain, pltpu.HBM(shape, bf16), plain]
        else:
            out += [plain] * each[group]
    scratch = [pltpu.VMEM(s, bf16) for s in shapes] + [
        pltpu.VMEM((c.width, shapes[0][0]), bf16),
        pltpu.VMEM((jobs, c.blocks, c.own, c.width), bf16),
        pltpu.SemaphoreType.DMA((len(order),)),
        pltpu.SemaphoreType.DMA((jobs, 4)),
    ]
    got = pl.pallas_call(
        partial(gradients_kernel, c, ring, order),
        out_shape=out,
        in_specs=[pl.BlockSpec(memory_space=pltpu.SMEM)]
        + [pl.BlockSpec(memory_space=pl.ANY)] * len(order),
        out_specs=[pl.BlockSpec(memory_space=pl.ANY)] * len(out),
        scratch_shapes=scratch,
        compiler_params=pltpu.CompilerParams(vmem_limit_bytes=vmem_bytes(scratch)),
        cost_estimate=pl.CostEstimate(
            flops=2 * shapes[0][0] * c.width * c.width * jobs,
            bytes_accessed=12_000_000,
            transcendentals=0,
        ),
    )(place, *[pltpu.with_memory_space_constraint(terms[n], pltpu.HBM) for n in order])
    return [got[: each[0]], got[each[0] :]] if order == FIRST else [got]


def add(*parts):
    total = parts[0].astype(f32)
    for part in parts[1:]:
        total = total + part.astype(f32)
    return total


LINE = (3, 2, 1)


def line_terms(z, *parts):
    def at(part, k):
        return lax.dynamic_index_in_dim(part, z ^ k, 0, keepdims=False)

    return [add(*[at(part, k) for part in parts]).astype(bf16) for k in (0,) + LINE]


def line_swap(terms):
    return terms[:1] + [swap(term, 4 * k) for term, k in zip(terms[1:], LINE)]


def ring_sums(first, second, z, sums):
    meet = lax.optimization_barrier
    (near0, far0, *core0), (both2, core2) = first
    far0 = add(far0, swap(core0[1], 1)).astype(bf16)
    terms2 = line_terms(z, both2, swap(core2, 1))

    *ready, near_core0 = meet((far0, terms2, core0[0]))
    group1, small = second(ready)
    far0, terms2 = swap(far0, 2), line_swap(terms2)
    core0 = swap(near_core0, 1)

    far0, terms2, core0, (near1, far1, *core1), small = meet((far0, terms2, core0, group1, small))
    far_core1 = swap(core1[1], 1)
    sum2 = add(*terms2)
    other2, sum2 = sum2[1].astype(bf16), sum2[0]
    far0, far_core1, other2, sum2, small = meet((far0, far_core1, other2, sum2, small))
    terms0 = line_swap(line_terms(z, near0, core0, far0))
    far1 = swap(add(far1, far_core1).astype(bf16), 2)
    core1 = swap(core1[0], 1)
    small = gather_step(gather_step(sums(small)[None], 8), 4)

    terms0, far1, core1, small = meet((terms0, far1, core1, small))
    terms1 = line_swap(line_terms(z, near1, core1, far1))
    sum2 = sum2 + swap(other2, 2).astype(f32)
    small = gather_step(gather_step(small, 2), 1)
    return add(*terms0), add(*terms1), sum2, small


def swap(block, distance):
    count = lax.axis_size(DP)
    return lax.ppermute(block, DP, [(i, i ^ distance) for i in range(count)])


def gather_small(block):
    count = lax.axis_size(DP)
    if count & (count - 1):
        return lax.all_gather(block, DP, axis=0, tiled=False)
    held, distance = block[None], count // 2
    while distance:
        held = gather_step(held, distance)
        distance //= 2
    return held


def gather_step(held, distance):
    other = swap(held, distance)
    lower = (lax.axis_index(DP) & distance) == 0
    pair = [jnp.where(lower, held, other), jnp.where(lower, other, held)]
    return jnp.stack(pair, axis=1).reshape((-1,) + held.shape[1:])


def scatter_small(blocks):
    count = lax.axis_size(DP)
    if count & (count - 1):
        return lax.psum_scatter(blocks, DP, scatter_dimension=0, tiled=False)
    mine = lax.axis_index(DP)
    distance = 1
    while distance < count:
        low, high = blocks[0::2], blocks[1::2]
        upper = (mine & distance) != 0
        other = swap(jnp.where(upper, low, high), distance)
        blocks = jnp.where(upper, high, low) + other
        distance *= 2
    return blocks[0]


def embed_columns(steps, index, width):
    half = width // 2
    place = (index % half).astype(f32)
    frequency = jnp.exp(-math.log(10000.0) * place / half)
    angles = steps.astype(f32)[:, None] * frequency[None, :]
    wave = jnp.where((index < half)[None, :], jnp.cos(angles), jnp.sin(angles))
    return jax.nn.silu(wave).astype(bf16)


def by_blocks(w, own, width):
    return jnp.concatenate([w[:, at : at + width] for at in range(0, w.shape[1], width)])


def in_vmem(block):
    return pltpu.with_memory_space_constraint(block, pltpu.VMEM)


def from_blocks(blocks, own, width):
    starts = range(0, blocks.shape[0], own)
    return jnp.concatenate([blocks[at : at + own] for at in starts], axis=1)


def local(tokens, cotangent, boxes, timesteps, w_ada, w_qkv, w_proj, w_up, w_down):
    section = lax.axis_index(SECTION)
    group = lax.axis_size(DP)
    micro_count, _, frames, patches, width = tokens.shape
    hidden = w_up.shape[2]
    rows = frames * patches
    own = width // group
    ratio = hidden // width
    direct = own % 16 == 0 and group % ratio == 0
    ring = direct and group == 16 and ratio == 4
    c = Cfg(frames, patches, width, hidden, group if direct else ratio)

    shard = jnp.concatenate(
        [
            by_blocks(w_qkv[0].astype(bf16), own, width),
            w_proj[0].astype(bf16),
            by_blocks(w_up[0].astype(bf16), own, width),
            w_down[0].astype(bf16),
        ],
        axis=0,
    )
    weights = lax.all_gather(shard, DP, axis=0, tiled=False)
    squares = 4 + ratio
    if not direct:
        weights = jnp.concatenate(
            [
                weights[:, i * own : (i + 1) * own].reshape(c.blocks, c.own, width)
                for i in range(squares)
            ]
            + [weights[:, squares * own :].reshape(c.blocks, ratio * c.own, width)],
            axis=1,
        )

    start = lax.axis_index(DP) * own
    index = start + jnp.arange(own, dtype=jnp.int32)
    steps = gather_small(timesteps.reshape(micro_count))
    steps = jnp.concatenate([jnp.zeros((group, 1), steps.dtype), steps], axis=1)
    embed = embed_columns(steps.reshape(-1), index, width)
    modulation = jnp.dot(embed, w_ada[0].astype(bf16), preferred_element_type=f32)
    modulation = scatter_small(modulation.reshape(group, 1 + micro_count, 6 * width))
    modulation = jnp.stack(
        [jnp.stack([modulation[0], modulation[1 + m]]) for m in range(micro_count)]
    )
    ctl = [
        jnp.concatenate([section.astype(jnp.int32)[None], boxes[m].reshape(-1)])
        for m in range(micro_count)
    ]

    tokens = tokens.reshape(micro_count, rows, width)
    cotangent = cotangent.reshape(micro_count, rows, width)
    whole = ((micro_count, rows, width), f32)
    one = ((rows, width), bf16)
    flops = 2 * rows * width * width * (4 + 2 * ratio)
    table = sizes(c)

    forward_names = [
        N.x, N.mod, N.given, N.mixed_a, N.packed, N.merged, N.branch, N.middle, N.mixed_b,
        N.hidden, N.active, N.out_branch, N.acts, N.send,
    ]
    back_names = [
        N.grad, N.grad_out_b, N.grad_hidden, N.temp, N.grad_middle, N.grad_branch, N.grad_merged,
        N.grad_packed, N.grad_in, N.sums, N.grad_mod,
    ]
    kept, received = [], []
    acts = None
    for m in range(micro_count):
        operands = dict(ctl=ctl[m], x=tokens, mod=modulation, w=weights)
        if m == 0:
            operands[N.w] = pltpu.with_memory_space_constraint(weights, pltpu.HBM)
        news = dict(send=one, **{n: table[n] for n in KEPT})
        if acts is None:
            news.update(acts=whole, near=(weights.shape, bf16))
        else:
            operands[N.acts] = acts
        alias = [N.acts] if acts is not None else []
        got = call(c, spatial_forward_kernel, m, operands, news, alias, forward_names, flops)
        acts = got[N.acts]
        if m == 0:
            weights = in_vmem(got[N.near])
        kept.append(got)
        received.append(in_vmem(lax.ppermute(got[N.send], SECTION, [(0, 1)])))

    shared = None
    grads = []
    for m in range(micro_count):
        operands = dict(
            ctl=ctl[m], x=received[m], mod=modulation, w=weights, cot=cotangent, acts=acts
        )
        news = dict(send=one)
        alias = [N.acts]
        if shared is None:
            news[N.grad_in] = whole
            news[N.grad_mod] = ((micro_count, 2, 6 * width), f32)
            for n in TERMS:
                news[n] = ((micro_count * rows, table[n][0][1]), bf16)
        else:
            operands.update(shared)
            alias += list(shared)
        names = forward_names + back_names + [N.heads_in, N.heads_out]
        got = call(c, temporal_kernel, m, operands, news, alias, names, 3 * flops)
        acts = got[N.acts]
        shared = {n: got[n] for n in (N.grad_in, N.grad_mod) + TERMS}
        grads.append(in_vmem(lax.ppermute(got[N.send], SECTION, [(1, 0)])))

    dp_index = lax.axis_index(DP)
    place = jnp.stack([dp_index // 2 % 2, dp_index % 2]).astype(jnp.int32)
    names = [n for n in forward_names if n not in (N.acts, N.send)] + back_names
    firsts = (N.grad_mod, N.grad_out_b, N.grad_hidden, N.active, N.mixed_b, N.grad_branch, N.merged)
    seconds = (N.grad_in, N.grad_mod, N.grad_packed, N.mixed_a)

    def operands_of(m, own_names, **more):
        got = dict(ctl=ctl[m], mod=modulation, w=weights, **more)
        for n in own_names:
            got[N.kept if n == N.merged else n] = kept[m][n]
        return got

    last = micro_count - 1
    for m in range(last):
        operands = operands_of(m, KEPT, grad=grads[m], x=tokens)
        operands.update(shared)
        shared = call(
            c, spatial_backward_kernel, m, operands, {}, list(shared), names, 2 * flops
        )
    ours = (N.out_branch, N.hidden, N.middle, N.branch, N.merged)
    operands = operands_of(last, ours, grad=grads[last])
    operands.update({n: shared[n] for n in firsts})
    news = dict(grad_middle=table[N.grad_middle], grad_merged=one)
    first_names = [
        N.mod, N.given, N.out_branch, N.hidden, N.middle, N.branch, N.merged, N.mixed_b, N.active,
        N.grad_out_b, N.grad_hidden, N.temp, N.grad_middle, N.grad_branch, N.grad_merged, N.sums,
        N.grad_mod,
    ]
    got = call(c, spatial_first_kernel, last, operands, news, firsts, first_names, 4 * flops // 3)
    shared.update({n: got[n] for n in firsts})
    between = {n: got[n] for n in news}
    first = weight_gradients(c, ring, FIRST, place, shared)

    def second(after):
        (grad_middle, grad_merged), _ = lax.optimization_barrier((tuple(between.values()), after))
        operands = operands_of(
            last, (N.packed,), x=tokens, grad_middle=grad_middle, grad_merged=grad_merged
        )
        operands.update({n: shared[n] for n in seconds})
        second_names = [
            N.x, N.mod, N.given, N.packed, N.mixed_a, N.temp, N.grad_middle, N.grad_merged,
            N.grad_packed, N.grad_in, N.sums, N.grad_mod,
        ]
        got = call(
            c, spatial_second_kernel, last, operands, {}, seconds, second_names, 2 * flops // 3
        )
        shared.update({n: got[n] for n in seconds})
        return weight_gradients(c, ring, SECOND, place, shared)[0], shared[N.grad_mod]

    def sums_of(grad_mod):
        given = jnp.sum(grad_mod[:, 0], axis=0, keepdims=True)
        return jnp.concatenate([given, grad_mod[:, 1]]).astype(bf16)

    if ring:
        *totals, sums = ring_sums(first, second, dp_index // 4, sums_of)
    else:
        group1, sums = second(())
        sums = gather_small(sums_of(sums))
        groups = first[0], group1, first[1]
        joined = [parts[0] for parts in groups]
        if not direct:
            tall = ratio * c.own
            joined = [
                jnp.concatenate(
                    [
                        part[:, i * c.own : (i + 1) * c.own].reshape(group, own, width)
                        for i in range(part.shape[1] // c.own)
                    ],
                    axis=1,
                )
                for part in (joined[0][:, tall:], joined[1], joined[2])
            ]
            tall = groups[0][0][:, :tall].reshape(group, ratio * own, width)
            joined[0] = jnp.concatenate([tall, joined[0]], axis=1)
        total = lax.psum_scatter(
            jnp.concatenate(joined, axis=1), DP, scatter_dimension=0, tiled=False
        ).astype(f32)
        cuts = (ratio + 1) * own, (2 * ratio + 4 - LEAD) * own
        totals = jnp.split(total, cuts)
    tall, rest = ratio * own, (ratio - LEAD) * own
    down, proj = totals[0][:tall], totals[0][tall:]
    up, qkv = jnp.concatenate([totals[2], totals[1][:rest]]), totals[1][rest:]
    grad_qkv = from_blocks(qkv, own, width)
    grad_proj = proj
    grad_up = from_blocks(up, own, width)
    grad_down = down

    sums = sums.reshape(group * (1 + micro_count), 6 * width)
    grad_ada = lax.dot_general(embed, sums, TN, preferred_element_type=f32)

    out_shape = (1, micro_count, 1, frames, patches, width)
    return (
        acts.reshape(out_shape),
        shared[N.grad_in].reshape(out_shape),
        grad_ada[None],
        grad_qkv[None],
        grad_proj[None],
        grad_up[None],
        grad_down[None],
    )


def solution(mesh):
    placed = (
        P(None, DP, None, None, None),
        P(None, DP, None, None, None),
        P(None, DP, None, None),
        P(None, DP),
        P(SECTION, DP, None),
        P(SECTION, DP, None),
        P(SECTION, DP, None),
        P(SECTION, DP, None),
        P(SECTION, DP, None),
    )
    return jax.shard_map(
        local,
        mesh=mesh,
        in_specs=placed,
        out_specs=(
            P(SECTION, None, DP, None, None, None),
            P(SECTION, None, DP, None, None, None),
            P(SECTION, DP, None),
            P(SECTION, DP, None),
            P(SECTION, DP, None),
            P(SECTION, DP, None),
            P(SECTION, DP, None),
        ),
        check_vma=False,
    )
```
